256 devices in a mesh: seq: 64 (over x, y_lo, z), kvh: 4 (over y_hi, core).
Axes of the slice: x: 4, y: 4 (y_hi: 2, y_lo: 2; y = y_hi * 2 + y_lo), z: 8, core: 2. Of those that a mesh axis runs over, the one named last changes fastest.
Arguments:
- hidden_in: bfloat16 [32768, 4096], P('seq'), may hold values from -16 to 16
- w_qkv: bfloat16 [4096, 3072], P(None, 'kvh'), may hold values from -0.09375 to 0.09375
- queries: bfloat16 [32768, 2048], P('seq', 'kvh'), may hold values from -2 to 2
- keys: bfloat16 [32768, 512], P('seq', 'kvh'), may hold values from -2 to 2
- values: bfloat16 [32768, 512], P('seq', 'kvh'), may hold values from -6 to 6
- d_out: bfloat16 [32768, 2048], P('seq', 'kvh'), may hold values from -6 to 6
- block_order: int32 [128], replicated, may hold values from 0 to 127, as said below
Outputs:
- grad_in: bfloat16 [32768, 4096], P(('seq', 'kvh'))
- grad_w: bfloat16 [4096, 3072], P('seq', 'kvh')
The draws below stay inside these ranges and needn't reach their ends.
Inputs may be any that keep to these rules, and one draw needn't show every extreme that they name: `block_order`: device i holds the blocks i and 127 - i, one in each of its two slots, in either order.
All inputs are finite; a program needn't handle non-finite values.
Results may differ from the reference program's by a relative error of at most 0.0058.
Values may be sent and summed in bfloat16 or wider, within the bound.
No kernel may reach another device: no remote copies, remote signals or barrier semaphores. Data moves between devices by JAX's collectives and lax.ppermute only.
A program may use at most 192 MiB of HBM per device.

```python
import jax
import jax.numpy as jnp
from jax import lax

D = 4096
HD = 128
GROUP = 4
HOPS = 4
TOK_DEV = 512
BLOCKS = 128
TOKENS = 32768
KVHEADS = 4
QHEADS = 16
COLS = 3072
N_SEQ = 64


def draw_block_order(key, part):
    key = jax.random.fold_in(key, 1)
    device_count = BLOCKS // 2
    flips = jax.random.randint(key, (device_count,), 0, 2).astype(jnp.int32)
    lower = jnp.arange(device_count, dtype=jnp.int32)
    upper = (BLOCKS - 1 - lower).astype(jnp.int32)
    first = jnp.where(flips == 1, upper, lower)
    second = jnp.where(flips == 1, lower, upper)
    return jnp.stack([first, second], axis=1).reshape(-1).astype(jnp.int32)


def raised(entries, stream_key, source, target, blocks, factor):
    owner, partner = [(jnp.arange(entries.shape[axis_at]) // (entries.shape[axis_at] // blocks)).reshape([-1 if axis == axis_at else 1 for axis in range(entries.ndim)]) for axis_at in (source, target)]
    chosen = jax.random.permutation(stream_key, blocks)[partner]
    strong = (owner == chosen) | (owner == (partner + blocks // 2) % blocks)
    return jnp.where(strong, factor * entries, entries)


def level_of(rng, shape, split, smallest, largest):
    gain = 1.0
    for axis_at, parts in split:
        draws = jax.random.uniform(jax.random.fold_in(jax.random.fold_in(rng, 6), axis_at), (parts,), jnp.float32, smallest / len(split), largest / len(split))
        gain = gain * jnp.repeat(jnp.exp(draws), shape[axis_at] // parts).reshape((-1,) + (1,) * (len(shape) - 1 - axis_at))
    return gain


def centred(key, dims, deviation, bound, pieces=(), held_as=jnp.bfloat16):
    entries = deviation * jax.random.normal(key, dims, jnp.float32)
    if pieces:
        entries = entries * level_of(key, dims, pieces, -0.22, 0.18)
    return jnp.clip(entries, -bound, bound).astype(held_as)


def gaussian_with(rng, extent, scale, limit, pieces, heavy, held_as=jnp.bfloat16):
    entries = scale * jax.random.normal(rng, extent, jnp.float32)
    if pieces:
        entries = entries * level_of(rng, extent, pieces, -0.22, 0.18)
    return jnp.clip(raised(entries, jax.random.fold_in(rng, 3), *heavy), -limit, limit).astype(held_as)


def setup_inputs(seed: int = 0) -> dict:
    streams_of = jax.random.split(jax.random.key(seed), 8)
    hidden_in = gaussian_with(streams_of[0], (TOKENS, D), 1.0, 16.0, ((0, 64),), (0, 1, 64, 4.0))
    w_qkv = centred(streams_of[1], (D, COLS), D ** -0.5, 0.09375, ((1, 4),))
    queries = jnp.clip(jax.random.uniform(streams_of[2], (TOKENS, QHEADS * HD), jnp.float32, -2.0, 2.0) * level_of(streams_of[2], (TOKENS, QHEADS * HD), ((0, 64), (1, 4)), -0.4, 0.0), -2.0, 2.0).astype(jnp.bfloat16)
    keys = jnp.clip(jax.random.uniform(streams_of[3], (TOKENS, KVHEADS * HD), jnp.float32, -2.0, 2.0) * level_of(streams_of[3], (TOKENS, KVHEADS * HD), ((0, 64), (1, 4)), -0.4, 0.0), -2.0, 2.0).astype(jnp.bfloat16)
    values = centred(streams_of[4], (TOKENS, KVHEADS * HD), 1.0, 6.0, ((0, 64), (1, 4)))
    d_out = centred(streams_of[5], (TOKENS, QHEADS * HD), 1.0, 6.0, ((0, 64), (1, 4)))
    block_order = draw_block_order(jax.random.fold_in(streams_of[7], 71), 0)
    return dict(hidden_in=hidden_in, w_qkv=w_qkv, queries=queries, keys=keys, values=values, d_out=d_out, block_order=block_order)


def positions(block_order):
    half_rows = TOK_DEV // 2
    offsets = jnp.arange(half_rows, dtype=jnp.int32)
    return (block_order[:, None] * half_rows + offsets[None, :]).reshape(N_SEQ, TOK_DEV)


def reference(hidden_in, w_qkv, queries, keys, values, d_out, block_order):
    score_scale = HD ** -0.5
    places = positions(block_order)
    query_all = queries.reshape(N_SEQ, TOK_DEV, KVHEADS, GROUP, HD)
    key_all = keys.reshape(N_SEQ, TOK_DEV, KVHEADS, HD)
    value_all = values.reshape(N_SEQ, TOK_DEV, KVHEADS, HD)
    cotangent = d_out.reshape(N_SEQ, TOK_DEV, KVHEADS, GROUP, HD)

    def one_device(device):
        owners = (device - jnp.arange(HOPS + 1, dtype=jnp.int32)) % N_SEQ
        key_window = key_all[owners].reshape((HOPS + 1) * TOK_DEV, KVHEADS, HD).astype(jnp.float32)
        value_window = value_all[owners].reshape((HOPS + 1) * TOK_DEV, KVHEADS, HD).astype(jnp.float32)
        key_places = places[owners].reshape(-1)
        query_rows = query_all[device].astype(jnp.float32)
        grad_rows = cotangent[device].astype(jnp.float32)
        visible = key_places[None, :] <= places[device][:, None]
        scores = jnp.einsum("tkgd,wkd->kgtw", query_rows, key_window) * score_scale
        weights = jnp.where(visible[None, None], jnp.exp(scores), 0.0)
        probability = weights / jnp.sum(weights, axis=-1, keepdims=True)
        grad_prob = jnp.einsum("tkgd,wkd->kgtw", grad_rows, value_window)
        row_delta = jnp.sum(probability * grad_prob, axis=-1, keepdims=True)
        grad_score = lax.optimization_barrier((probability * (grad_prob - row_delta) * score_scale).astype(jnp.bfloat16)).astype(jnp.float32)
        probability_low = lax.optimization_barrier(probability.astype(jnp.bfloat16)).astype(jnp.float32)
        grad_query = jnp.einsum("kgtw,wkd->tkgd", grad_score, key_window)
        grad_key = jnp.einsum("kgtw,tkgd->wkd", grad_score, query_rows)
        grad_value = jnp.einsum("kgtw,tkgd->wkd", probability_low, grad_rows)
        window_terms = jnp.stack([grad_key, grad_value], 0).reshape(2, HOPS + 1, TOK_DEV, KVHEADS, HD)
        return grad_query.astype(jnp.bfloat16), window_terms

    grad_query, window_terms = lax.map(one_device, jnp.arange(N_SEQ, dtype=jnp.int32))
    totals = jnp.zeros((N_SEQ, 2, TOK_DEV, KVHEADS, HD), jnp.float32)
    for hop_index in range(HOPS + 1):
        totals = totals + jnp.roll(window_terms[:, :, hop_index], -hop_index, axis=0)
    kv_grads = totals.astype(jnp.bfloat16)
    grads = jnp.concatenate([grad_query.reshape(N_SEQ, TOK_DEV, KVHEADS, GROUP * HD), kv_grads[:, 0], kv_grads[:, 1]], axis=-1)
    grads = grads.reshape(TOKENS, COLS)
    grad_in = lax.dot_general(grads, w_qkv, (((1,), (1,)), ((), ())), preferred_element_type=jnp.float32).astype(jnp.bfloat16)
    token_sum = lax.dot_general(hidden_in, grads, (((0,), (0,)), ((), ())), preferred_element_type=jnp.float32)
    grad_w = (token_sum * float(TOKENS) ** -0.5).astype(jnp.bfloat16)
    return grad_in, grad_w
```

```python
import functools

import jax
import jax.numpy as jnp
from jax import lax
from jax.experimental import pallas as pl
from jax.experimental.pallas import tpu as pltpu
from jax.sharding import PartitionSpec as P

HOPS = 4
LOG2E = 1.4426950408889634
BF16 = jnp.bfloat16
F32 = jnp.float32
SEQ_DIMS = {64: (4, 2, 8), 16: (2, 2, 4)}


def shift_seq(value, steps, sources=None):
    count = lax.axis_size("seq")
    sources = range(count) if sources is None else sources
    return lax.ppermute(value, "seq", [(s, (s + steps) % count) for s in sources])


def shift_dim(value, dim, steps):
    count = lax.axis_size("seq")
    nx, ny, nz = SEQ_DIMS[count]
    pairs = []
    for s in range(count):
        x, y, z = s // (ny * nz), s // nz % ny, s % nz
        if dim == 0:
            x = (x + steps) % nx
        elif dim == 1:
            y = (y + steps) % ny
        else:
            z = (z + steps) % nz
        pairs.append((s, (x * ny + y) * nz + z))
    return lax.ppermute(value, "seq", pairs)


def swap_kvh(value, bit):
    return lax.ppermute(value, "kvh", [(s, s ^ bit) for s in range(lax.axis_size("kvh"))])


def dot_nt(a, b):
    return lax.dot_general(a, b, (((1,), (1,)), ((), ())), preferred_element_type=F32)


def dot_nn(a, b):
    return lax.dot_general(a, b, (((1,), (0,)), ((), ())), preferred_element_type=F32)


def dot_tn(a, b):
    return lax.dot_general(a, b, (((0,), (0,)), ((), ())), preferred_element_type=F32)


def pair_weights(query, grad, key, value, diagonal, scale):
    weights = jnp.exp2(dot_nt(key, query) * (scale * LOG2E))
    if diagonal:
        rows = lax.broadcasted_iota(jnp.int32, weights.shape, 0)
        cols = lax.broadcasted_iota(jnp.int32, weights.shape, 1)
        weights = jnp.where(rows <= cols, weights, 0.0)
    return weights, dot_nt(value, grad)


def stats_kernel(hops, own, heads, hd, scale, scal, q, do, *refs):
    half = q.shape[0] // 2
    lo = pl.multiple_of(scal[0] * half, half)
    hi = pl.multiple_of((1 - scal[0]) * half, half)
    if own:
        kv, stats = refs
    else:
        pieces, before, stats, picked = refs[: 2 * len(hops)], refs[-3], refs[-2], refs[-1]
    stats[...] = jnp.zeros_like(stats) if own else before[...]

    def quadrant(key, value, place, off, diagonal):
        for j in range(heads):
            cols = slice(j * hd, (j + 1) * hd)
            weights, grad_prob = pair_weights(
                q[pl.ds(off, half), cols], do[pl.ds(off, half), cols], key, value, diagonal, scale
            )
            stats[0, place, j : j + 1, :] += jnp.sum(weights, axis=0, keepdims=True)
            stats[1, place, j : j + 1, :] += jnp.sum(weights * grad_prob, axis=0, keepdims=True)

    if own:
        for key_off, place, off, diagonal in ((lo, 1, hi, False), (hi, 1, hi, True), (lo, 0, lo, True)):
            rows = pl.ds(key_off, half)
            quadrant(kv[rows, :hd], kv[rows, hd:], place, off, diagonal)
    else:
        for n, hop in enumerate(hops):
            low, high = pieces[2 * n], pieces[2 * n + 1]
            wraps = scal[1] < hop
            picked[...] = low[...]

            @pl.when(wraps)
            def _():
                picked[...] = high[...]

            quadrant(low[:, :hd], low[:, hd:], 1, hi, False)
            place = jnp.where(wraps, 1, 0)
            off = pl.multiple_of(jnp.where(wraps, hi, lo), half)
            quadrant(picked[:, :hd], picked[:, hd:], place, off, False)


def stats_call(hops, scal, q, do, pieces, before, heads, hd):
    own = before is None
    half = q.shape[0] // 2
    quads = 3 if own else 2 * len(hops)
    args = [scal, q, do, *pieces] + ([] if own else [before])
    vmem = pl.BlockSpec(memory_space=pltpu.VMEM)
    return pl.pallas_call(
        functools.partial(stats_kernel, hops, own, heads, hd, hd**-0.5),
        out_shape=jax.ShapeDtypeStruct((2, 2, heads, half), F32),
        in_specs=[pl.BlockSpec(memory_space=pltpu.SMEM)] + [vmem] * (len(args) - 1),
        out_specs=vmem,
        scratch_shapes=[] if own else [pltpu.VMEM((half, 2 * hd), BF16)],
        compiler_params=pltpu.CompilerParams(vmem_limit_bytes=32 * 1024 * 1024),
        cost_estimate=pl.CostEstimate(
            flops=quads * heads * half * half * hd * 4,
            bytes_accessed=2 * q.size * 2,
            transcendentals=quads * heads * half * half,
        ),
    )(*args)


def grads_kernel(hops, own, first, heads, hd, scale, scal, q, do, stats, *refs):
    half = q.shape[0] // 2
    lo = pl.multiple_of(scal[0] * half, half)
    hi = pl.multiple_of((1 - scal[0]) * half, half)
    refs = list(refs)
    before = None if first else refs.pop(0)
    if own:
        kv, dq, dkv, dqt = refs
        dqt[...] = before[...]
    else:
        pieces = [refs.pop(0) for _ in range(2 * len(hops))]
        dqt = refs.pop(0)
        outs = [refs.pop(0) for _ in range(2 * len(hops))]
        picked, acc = refs
        dqt[...] = jnp.zeros_like(dqt) if first else before[...]

    def quadrant(key, value, place, off, diagonal):
        grad_key = grad_value = None
        for j in range(heads):
            cols = slice(j * hd, (j + 1) * hd)
            query, grad = q[pl.ds(off, half), cols], do[pl.ds(off, half), cols]
            weights, grad_prob = pair_weights(query, grad, key, value, diagonal, scale)
            inverse = 1.0 / stats[0, place, j : j + 1, :]
            delta = stats[1, place, j : j + 1, :] * inverse
            prob = weights * inverse
            grad_score = (prob * (grad_prob - delta) * scale).astype(BF16)
            term_key = dot_nn(grad_score, query)
            term_value = dot_nn(prob.astype(BF16), grad)
            grad_key = term_key if j == 0 else grad_key + term_key
            grad_value = term_value if j == 0 else grad_value + term_value
            dqt[place, j] += dot_tn(key, grad_score)
        return grad_key, grad_value

    if own:
        gk, gv = quadrant(kv[pl.ds(lo, half), :hd], kv[pl.ds(lo, half), hd:], 1, hi, False)
        gk2, gv2 = quadrant(kv[pl.ds(lo, half), :hd], kv[pl.ds(lo, half), hd:], 0, lo, True)
        dkv[0, :, :hd] = gk + gk2
        dkv[0, :, hd:] = gv + gv2
        gk, gv = quadrant(kv[pl.ds(hi, half), :hd], kv[pl.ds(hi, half), hd:], 1, hi, True)
        dkv[1, :, :hd] = gk
        dkv[1, :, hd:] = gv
        for place, off in ((0, lo), (1, hi)):
            for j in range(heads):
                dq[pl.ds(off, half), j * hd : (j + 1) * hd] = dqt[place, j].T.astype(BF16)
    else:
        for n, hop in enumerate(hops):
            low, high = pieces[2 * n], pieces[2 * n + 1]
            out_low, out_high = outs[2 * n], outs[2 * n + 1]
            wraps = scal[1] < hop
            picked[...] = low[...]

            @pl.when(wraps)
            def _():
                picked[...] = high[...]

            gk, gv = quadrant(low[:, :hd], low[:, hd:], 1, hi, False)
            acc[0, :, :hd] = gk
            acc[0, :, hd:] = gv
            place = jnp.where(wraps, 1, 0)
            off = pl.multiple_of(jnp.where(wraps, hi, lo), half)
            gk, gv = quadrant(picked[:, :hd], picked[:, hd:], place, off, False)
            acc[1, :, :hd] = gk
            acc[1, :, hd:] = gv

            @pl.when(wraps)
            def _():
                out_low[...] = acc[0].astype(BF16)
                out_high[...] = acc[1].astype(BF16)

            @pl.when(jnp.logical_not(wraps))
            def _():
                out_low[...] = (acc[0] + acc[1]).astype(BF16)
                out_high[...] = jnp.zeros_like(out_high)


def grads_call(hops, own, scal, q, do, stats, before, pieces, heads, hd):
    half = q.shape[0] // 2
    quads = 3 if own else 2 * len(hops)
    args = [scal, q, do, stats] + ([] if before is None else [before]) + list(pieces)
    vmem = pl.BlockSpec(memory_space=pltpu.VMEM)
    partial_shape = (2, heads, hd, half)
    if own:
        out_shape = [
            jax.ShapeDtypeStruct(q.shape, BF16),
            jax.ShapeDtypeStruct((2, half, 2 * hd), F32),
        ]
        scratch = [pltpu.VMEM(partial_shape, F32)]
    else:
        out_shape = [jax.ShapeDtypeStruct(partial_shape, F32)]
        out_shape += [jax.ShapeDtypeStruct((half, 2 * hd), BF16)] * (2 * len(hops))
        scratch = [pltpu.VMEM((half, 2 * hd), BF16), pltpu.VMEM((2, half, 2 * hd), F32)]
    return pl.pallas_call(
        functools.partial(grads_kernel, hops, own, before is None, heads, hd, hd**-0.5),
        out_shape=out_shape,
        in_specs=[pl.BlockSpec(memory_space=pltpu.SMEM)] + [vmem] * (len(args) - 1),
        out_specs=[vmem] * len(out_shape),
        scratch_shapes=scratch,
        compiler_params=pltpu.CompilerParams(vmem_limit_bytes=32 * 1024 * 1024),
        cost_estimate=pl.CostEstimate(
            flops=quads * heads * half * half * hd * 10,
            bytes_accessed=2 * q.size * 2 + 8 * half * hd * heads * 4,
            transcendentals=quads * heads * half * half,
        ),
    )(*args)


def chain_sum(term, dim, place, size):
    total = term(place).astype(F32)
    for sign, length in ((1, size // 2), (-1, size - 1 - size // 2)):
        if length == 0:
            continue
        running = term((place + sign * length) % size).astype(BF16)
        for distance in range(length - 1, -1, -1):
            running = shift_dim(running, dim, sign)
            if distance:
                running = (running.astype(F32) + term((place + sign * distance) % size)).astype(BF16)
        total = total + running.astype(F32)
    return total


def direct_sum(pieces, axis, dim, place, size):
    total = lax.dynamic_index_in_dim(pieces, place, axis, keepdims=False)
    for steps in range(1, size):
        piece = lax.dynamic_index_in_dim(pieces, (place + steps) % size, axis, keepdims=False)
        total = total + shift_dim(piece.astype(BF16), dim, steps).astype(F32)
    return total


def shards(hidden_in, w_qkv, queries, keys, values, d_out, block_order):
    count = lax.axis_size("seq")
    nx, ny, nz = SEQ_DIMS[count]
    me = lax.axis_index("seq")
    at_x, at_y, at_z = me // (ny * nz), me // nz % ny, me % nz
    kvh = lax.axis_index("kvh")
    core, y_hi = kvh % 2, kvh // 2
    rows, width = hidden_in.shape
    half = rows // 2
    hd = keys.shape[1]
    heads = queries.shape[1] // hd
    out_rows = width // count

    first = lax.dynamic_index_in_dim(block_order, 2 * me, 0, keepdims=False)
    low_slot = jnp.where(first == me, 0, 1).astype(jnp.int32)
    scal = jnp.stack([low_slot, me.astype(jnp.int32)])
    kv = jnp.concatenate([keys, values], axis=1)
    kv_low = lax.dynamic_slice_in_dim(kv, low_slot * half, half, 0)
    kv_high = lax.dynamic_slice_in_dim(kv, (1 - low_slot) * half, half, 0)
    low = [shift_seq(kv_low, h) for h in range(1, HOPS + 1)]
    high = [shift_seq(kv_high, h, range(count - h, count)) for h in range(1, HOPS + 1)]

    hidden_t = lax.optimization_barrier(hidden_in.T)

    stats = stats_call((), scal, queries, d_out, [kv], None, heads, hd)
    for h in range(1, HOPS + 1):
        stats = stats_call(
            (h,), scal, queries, d_out, [low[h - 1], high[h - 1]], stats, heads, hd
        )

    partial_q = None
    back_low, back_high = [None] * HOPS, [None] * HOPS
    for hops in ((4, 3), (2, 1)):
        pieces = [piece for h in hops for piece in (low[h - 1], high[h - 1])]
        partial_q, *terms = grads_call(
            hops, False, scal, queries, d_out, stats, partial_q, pieces, heads, hd
        )
        for n, h in enumerate(hops):
            back_low[h - 1] = shift_seq(terms[2 * n], -h)
            back_high[h - 1] = shift_seq(terms[2 * n + 1], -h, range(h))
    grad_q, own_kv = grads_call(
        (), True, scal, queries, d_out, stats, partial_q, [kv], heads, hd
    )
    low_total, high_total = own_kv[0], own_kv[1]
    for h in range(HOPS):
        low_total = low_total + back_low[h].astype(F32)
        high_total = high_total + back_high[h].astype(F32)
    low_total, high_total = low_total.astype(BF16), high_total.astype(BF16)
    grad_kv = jnp.where(
        low_slot == 0,
        jnp.concatenate([low_total, high_total], axis=0),
        jnp.concatenate([high_total, low_total], axis=0),
    )

    by_z = hidden_t.reshape(nx * ny, nz, out_rows, rows)
    by_x = hidden_t.reshape(nx, ny * nz * out_rows, rows)

    def z_first(columns):
        cols = columns.shape[1]

        def term(place):
            chunk = lax.dynamic_index_in_dim(by_z, place, 1, keepdims=False)
            return dot_nn(chunk.reshape(nx * ny * out_rows, rows), columns)

        total = chain_sum(term, 2, at_z, nz).reshape(nx, ny, out_rows, cols)
        return direct_sum(total, 0, 0, at_x, nx)

    def x_first(columns):
        cols = columns.shape[1]

        def term(place):
            return dot_nn(lax.dynamic_index_in_dim(by_x, place, 0, keepdims=False), columns)

        total = chain_sum(term, 0, at_x, nx).reshape(ny, nz, out_rows, cols)
        return direct_sum(total, 1, 2, at_z, nz)

    parts = []
    for matrix in (grad_q, grad_kv):
        middle = matrix.shape[1] // 2
        total = jnp.concatenate([z_first(matrix[:, :middle]), x_first(matrix[:, middle:])], axis=-1)
        parts.append(direct_sum(total, 0, 1, at_y, ny))
    grad_w = jnp.concatenate(parts, axis=-1) * float(rows * count) ** (-0.5)

    grads = jnp.concatenate([grad_q, grad_kv], axis=1).reshape(2, 2, rows // 4, -1)
    theirs = lax.dynamic_index_in_dim(grads, 1 - core, 1, keepdims=False).reshape(rows // 2, -1)
    mine = lax.dynamic_index_in_dim(grads, core, 1, keepdims=False).reshape(rows // 2, -1)
    outs = []
    step = width // 2
    for start in range(0, width, step):
        weight = w_qkv[start : start + step]
        received = swap_kvh(dot_nt(theirs, weight).astype(BF16), 1)
        total = (dot_nt(mine, weight) + received.astype(F32)).reshape(2, rows // 4, step)
        send = lax.dynamic_index_in_dim(total, 1 - y_hi, 0, keepdims=False).astype(BF16)
        keep = lax.dynamic_index_in_dim(total, y_hi, 0, keepdims=False)
        outs.append((keep + swap_kvh(send, 2).astype(F32)).astype(BF16))
    return jnp.concatenate(outs, axis=1), grad_w.astype(BF16)


def solution(mesh):
    return jax.shard_map(
        shards,
        mesh=mesh,
        in_specs=(
            P("seq", None),
            P(None, "kvh"),
            P("seq", "kvh"),
            P("seq", "kvh"),
            P("seq", "kvh"),
            P("seq", "kvh"),
            P(),
        ),
        out_specs=(P(("seq", "kvh"), None), P("seq", "kvh")),
        check_vma=False,
    )
```

```python
import functools

import jax
import jax.numpy as jnp
import numpy as np
from jax import lax
from jax.experimental import pallas as pl
from jax.experimental.pallas import tpu as pltpu
from jax.sharding import Mesh
from jax.sharding import PartitionSpec as P

LOG2E = 1.4426950408889634
BF16 = jnp.bfloat16
F32 = jnp.float32
SEQ_DIMS = {64: (4, 2, 8), 16: (2, 2, 4)}
SEQ = ("x", "y_lo", "z")
KVH = ("y_hi", "core")
VMEM_LIMIT = 40 * 1024 * 1024


def shift_seq(value, steps, sources=None):
    count = lax.axis_size(SEQ)
    sources = range(count) if sources is None else [s % count for s in sources]
    return lax.ppermute(value, SEQ, [(s, (s + steps) % count) for s in sources])


def shift(value, axis, steps):
    size = lax.axis_size(axis)
    return lax.ppermute(value, axis, [(s, (s + steps) % size) for s in range(size)])


def dot_nt(a, b):
    return lax.dot_general(a, b, (((1,), (1,)), ((), ())), preferred_element_type=F32)


def dot_nn(a, b):
    return lax.dot_general(a, b, (((1,), (0,)), ((), ())), preferred_element_type=F32)


def dot_tn(a, b):
    return lax.dot_general(a, b, (((0,), (0,)), ((), ())), preferred_element_type=F32)


def low_slot_of(me, order):
    return jnp.where(order[2 * me[0]] == me[0], 0, 1)


def offsets(me, order, half):
    slot = low_slot_of(me, order)
    return pl.multiple_of(slot * half, half), pl.multiple_of((1 - slot) * half, half)


def call(kernel, out_shape, args, scratch=(), cost=1):
    vmem = pl.BlockSpec(memory_space=pltpu.VMEM)
    smem = pl.BlockSpec(memory_space=pltpu.SMEM)
    return pl.pallas_call(
        kernel,
        out_shape=out_shape,
        in_specs=[smem, smem] + [vmem] * (len(args) - 2),
        out_specs=jax.tree.map(lambda _: vmem, out_shape),
        scratch_shapes=list(scratch),
        compiler_params=pltpu.CompilerParams(vmem_limit_bytes=VMEM_LIMIT),
        cost_estimate=pl.CostEstimate(flops=0, bytes_accessed=int(cost * 3.5e6), transcendentals=0),
    )(*args)


def split_kernel(me, order, keys, values, low, high):
    half, hd = low.shape[0], keys.shape[1]
    for out, off in zip((low, high), offsets(me, order, half)):
        out[:, :hd] = keys[pl.ds(off, half), :]
        out[:, hd:] = values[pl.ds(off, half), :]


def pair_weights(query, grad, key, value, diagonal, scale):
    weights = jnp.exp2(dot_nt(key, query) * (scale * LOG2E))
    if diagonal:
        rows = lax.broadcasted_iota(jnp.int32, weights.shape, 0)
        cols = lax.broadcasted_iota(jnp.int32, weights.shape, 1)
        weights = jnp.where(rows <= cols, weights, 0.0)
    return weights, dot_nt(value, grad)


def add_stats(q, do, stats, heads, piece, place, off, diagonal):
    half, hd = piece.shape[0], piece.shape[1] // 2
    key, value = piece[:, :hd], piece[:, hd:]
    for j in range(heads):
        cols = slice(j * hd, (j + 1) * hd)
        query, grad = q[pl.ds(off, half), cols], do[pl.ds(off, half), cols]
        weights, grad_prob = pair_weights(query, grad, key, value, diagonal, hd**-0.5)
        stats[0, place, j : j + 1, :] += jnp.sum(weights, axis=0, keepdims=True)
        stats[1, place, j : j + 1, :] += jnp.sum(weights * grad_prob, axis=0, keepdims=True)


def add_grads(q, do, stats, dqt, heads, piece, place, off, diagonal):
    half, hd = piece.shape[0], piece.shape[1] // 2
    key, value = piece[:, :hd], piece[:, hd:]
    grad_key = grad_value = None
    for j in range(heads):
        cols = slice(j * hd, (j + 1) * hd)
        query, grad = q[pl.ds(off, half), cols], do[pl.ds(off, half), cols]
        weights, grad_prob = pair_weights(query, grad, key, value, diagonal, hd**-0.5)
        inverse = 1.0 / stats[0, place, j : j + 1, :]
        delta = stats[1, place, j : j + 1, :] * inverse
        prob = weights * inverse
        grad_score = (prob * (grad_prob - delta) * hd**-0.5).astype(BF16)
        term_key = dot_nn(grad_score, query)
        term_value = dot_nn(prob.astype(BF16), grad)
        grad_key = term_key if j == 0 else grad_key + term_key
        grad_value = term_value if j == 0 else grad_value + term_value
        dqt[place, j] += dot_tn(key, grad_score)
    return grad_key, grad_value


def second_quadrant(me, hop, low, high, picked, lo, hi):
    wraps = me[0] < hop
    picked[...] = low[...]

    @pl.when(wraps)
    def _():
        picked[...] = high[...]

    return wraps, jnp.where(wraps, 1, 0), pl.multiple_of(jnp.where(wraps, hi, lo), lo_size(picked))


def lo_size(ref):
    return ref.shape[0]


def own_stats_kernel(heads, me, order, q, do, low, high, stats):
    lo, hi = offsets(me, order, low.shape[0])
    stats[...] = jnp.zeros_like(stats)
    add_stats(q, do, stats, heads, low, 1, hi, False)
    add_stats(q, do, stats, heads, high, 1, hi, True)
    add_stats(q, do, stats, heads, low, 0, lo, True)


def hop_stats_kernel(hops, heads, me, order, q, do, lows, highs, before, stats, picked):
    lo, hi = offsets(me, order, picked.shape[0])
    stats[...] = before[...]
    for n, hop in enumerate(hops):
        low, high = lows.at[n], highs.at[n]
        add_stats(q, do, stats, heads, low, 1, hi, False)
        _, place, off = second_quadrant(me, hop, low, high, picked, lo, hi)
        add_stats(q, do, stats, heads, picked, place, off, False)


def hop_terms(me, hop, q, do, stats, dqt, heads, low, high, picked, acc, lo, hi, out_low, out_high):
    hd = picked.shape[1] // 2
    acc[0, :, :hd], acc[0, :, hd:] = add_grads(q, do, stats, dqt, heads, low, 1, hi, False)
    wraps, place, off = second_quadrant(me, hop, low, high, picked, lo, hi)
    acc[1, :, :hd], acc[1, :, hd:] = add_grads(q, do, stats, dqt, heads, picked, place, off, False)

    @pl.when(wraps)
    def _():
        out_low[...] = acc[0].astype(out_low.dtype)
        out_high[...] = acc[1].astype(out_low.dtype)

    @pl.when(jnp.logical_not(wraps))
    def _():
        out_low[...] = (acc[0] + acc[1]).astype(out_low.dtype)
        out_high[...] = jnp.zeros_like(out_high)


def hop_grads_kernel(hops, first, heads, me, order, q, do, stats, lows, highs, *refs):
    refs = list(refs)
    before = None if first else refs.pop(0)
    dqt, out_lows, out_highs, picked, acc = refs
    lo, hi = offsets(me, order, picked.shape[0])
    dqt[...] = jnp.zeros_like(dqt) if first else before[...]
    for n, hop in enumerate(hops):
        hop_terms(
            me, hop, q, do, stats, dqt, heads, lows.at[n], highs.at[n],
            picked, acc, lo, hi, out_lows.at[n], out_highs.at[n],
        )


def last_grads_kernel(
    heads, me, order, q, do, stats, low1, high1, low, high, before,
    dq, own, term_low, term_high, dqt, picked, acc,
):
    half, hd = low.shape[0], low.shape[1] // 2
    lo, hi = offsets(me, order, half)
    dqt[...] = before[...]
    hop_terms(
        me, 1, q, do, stats, dqt, heads, low1, high1, picked, acc, lo, hi, term_low, term_high
    )
    gk, gv = add_grads(q, do, stats, dqt, heads, low, 1, hi, False)
    gk2, gv2 = add_grads(q, do, stats, dqt, heads, low, 0, lo, True)
    own[0, :, :hd] = gk + gk2
    own[0, :, hd:] = gv + gv2
    own[1, :, :hd], own[1, :, hd:] = add_grads(q, do, stats, dqt, heads, high, 1, hi, True)
    for place, off in ((0, lo), (1, hi)):
        for j in range(heads):
            dq[pl.ds(off, half), j * hd : (j + 1) * hd] = dqt[place, j].T.astype(BF16)


def tokens_kernel(nx, nz, at, order, mine, theirs, grads, out):
    half, tokens = mine.shape[1:]
    block = half // nz
    for n, pieces in enumerate((mine, theirs)):
        total = None
        for k in range(nx):
            off = pl.multiple_of(lax.rem(at[0] - k + nx, nx) * tokens, tokens)
            term = dot_nn(pieces[k], grads[pl.ds(off, tokens), :])
            total = term if k == 0 else total + term
        total = total.astype(BF16)
        y = at[1] if n == 0 else 1 - at[1]
        into = pl.ds(pl.multiple_of(y * block, block), block)
        for z in range(nz):
            out[z, into, :] = total[z * block : (z + 1) * block]


def shards(hidden_in, w_qkv, queries, keys, values, d_out, block_order):
    count = lax.axis_size(SEQ)
    nx, ny, nz = (lax.axis_size(axis) for axis in SEQ)
    at_x, at_y = lax.axis_index("x"), lax.axis_index("y_lo")
    core, y_hi = lax.axis_index("core"), lax.axis_index("y_hi")
    index = lax.axis_index(SEQ).astype(jnp.int32)
    me = index.reshape(1)
    rows, width = hidden_in.shape
    half = rows // 2
    hd = keys.shape[1]
    heads = queries.shape[1] // hd
    out_rows = width // count

    piece = jax.ShapeDtypeStruct((half, 2 * hd), BF16)
    stats_shape = jax.ShapeDtypeStruct((2, 2, heads, half), F32)
    partial_q = jax.ShapeDtypeStruct((2, heads, hd, half), F32)
    picked = pltpu.VMEM(piece.shape, BF16)
    acc = pltpu.VMEM((2, half, 2 * hd), F32)

    low, high = call(split_kernel, [piece, piece], (me, block_order, keys, values))
    low1 = shift_seq(low, 1)
    high1 = shift_seq(high, 1, (-3, -2, -1))
    low4 = shift_seq(low, 4)
    high4 = shift_seq(high, 4, (-4, -3, -2, -1))

    base = (me, block_order, queries, d_out)
    stats = call(
        functools.partial(own_stats_kernel, heads), stats_shape, (*base, low, high), cost=2,
    )
    low1, high1, stats = lax.optimization_barrier((low1, high1, stats))
    pair, pair_high = jnp.stack([low, low1]), jnp.stack([high, high1])
    pair, pair_high, hidden_in = lax.optimization_barrier((pair, pair_high, hidden_in))
    low23 = shift_seq(pair, 2)
    high23 = shift_seq(pair_high, 2, (-2, -1, 0))
    hidden_t = lax.optimization_barrier(hidden_in.T)
    low4, high4, hidden_t = lax.optimization_barrier((low4, high4, hidden_t))

    chunks = hidden_t.reshape(nx, ny, nz * out_rows, rows)

    def half_chunk(place, half_place):
        return lax.dynamic_slice(
            chunks, (place % nx, half_place, 0, 0), (1, 1, *chunks.shape[2:])
        ).reshape(chunks.shape[2:])

    arrived = [shift(half_chunk(at_x + k, core), "x", k) for k in range(1, nx)]
    hidden_mine = jnp.stack([half_chunk(at_x, core)] + arrived)

    for hops, lows, highs in (
        ((1,), low1[None], high1[None]), ((4,), low4[None], high4[None]), ((2, 3), low23, high23)
    ):
        stats = call(
            functools.partial(hop_stats_kernel, hops, heads), stats_shape,
            (*base, lows, highs, stats), [picked], cost=1.3 * len(hops),
        )

    two, one = (jax.ShapeDtypeStruct((n, *piece.shape), BF16) for n in (2, 1))
    dqt, out23, out23_high = call(
        functools.partial(hop_grads_kernel, (2, 3), True, heads), [partial_q, two, two],
        (*base, stats, low23, high23), [picked, acc], cost=5,
    )
    back23 = shift_seq(out23, -2)
    back23_high = shift_seq(out23_high, -2, (0, 1, 2))
    dqt, out4, out4_high = call(
        functools.partial(hop_grads_kernel, (4,), False, heads), [partial_q, one, one],
        (*base, stats, low4[None], high4[None], dqt), [picked, acc], cost=3,
    )
    back4 = shift_seq(out4[0], -4)
    back4_high = shift_seq(out4_high[0], -4, (0, 1, 2, 3))
    dqt, hidden_mine = lax.optimization_barrier((dqt, hidden_mine))
    swapped = shift(hidden_mine[1:], "core", 1)
    hidden_theirs = jnp.concatenate([half_chunk(at_x, 1 - core)[None], swapped])
    term = jax.ShapeDtypeStruct(piece.shape, F32)
    grad_q, own, out1, out1_high = call(
        functools.partial(last_grads_kernel, heads),
        [jax.ShapeDtypeStruct(queries.shape, BF16), jax.ShapeDtypeStruct((2, *piece.shape), F32), term, term],
        (*base, stats, low1, high1, low, high, dqt),
        [pltpu.VMEM(partial_q.shape, F32), picked, acc], cost=8,
    )
    out1, hidden_theirs = lax.optimization_barrier((out1, hidden_theirs))
    back1 = shift_seq((out1 + back23[1].astype(F32)).astype(BF16), -1)
    back1_high = shift_seq((out1_high + back23_high[1].astype(F32)).astype(BF16), -1, (-2, -1, 0))
    low_total = own[0] + back23[0].astype(F32) + back1.astype(F32) + back4.astype(F32)
    high_total = (
        own[1] + back23_high[0].astype(F32) + back1_high.astype(F32) + back4_high.astype(F32)
    )
    low_total, high_total = low_total.astype(BF16), high_total.astype(BF16)
    grad_kv = jnp.where(
        low_slot_of(me, block_order) == 0,
        jnp.concatenate([low_total, high_total], axis=0),
        jnp.concatenate([high_total, low_total], axis=0),
    )

    place = jnp.stack([at_x, core]).astype(jnp.int32)

    def x_gathered(matrix):
        whole = jnp.zeros((nx, *matrix.shape), BF16)
        for k in range(nx):
            piece = matrix if k == 0 else shift(matrix, "x", k)
            whole = lax.dynamic_update_index_in_dim(whole, piece, (at_x - k) % nx, 0)
        return whole.reshape(nx * rows, -1)

    def token_sums(matrix, gathered):
        return call(
            functools.partial(tokens_kernel, nx, nz),
            jax.ShapeDtypeStruct((nz, ny * out_rows, matrix.shape[1]), BF16),
            (place, block_order, hidden_mine, hidden_theirs, gathered), cost=2,
        )

    gathered_q = x_gathered(grad_q)
    tokens_q = token_sums(grad_q, gathered_q)
    sums_q = lax.psum_scatter(tokens_q, "z", scatter_dimension=0, tiled=True)

    grads = jnp.concatenate([grad_q, grad_kv], axis=1).reshape(2, 2, rows // 4, -1)
    theirs = lax.dynamic_index_in_dim(grads, 1 - core, 1, keepdims=False).reshape(half, -1)
    mine = lax.dynamic_index_in_dim(grads, core, 1, keepdims=False).reshape(half, -1)
    gathered_kv = x_gathered(lax.optimization_barrier((grad_kv, gathered_q))[0])
    step = width // 2
    kept, sent = [], []
    for start in range(0, width, step):
        weight = w_qkv[start : start + step]
        received = shift(dot_nt(theirs, weight).astype(BF16), "core", 1)
        total = (dot_nt(mine, weight) + received.astype(F32)).reshape(2, rows // 4, step)
        sent.append(lax.dynamic_index_in_dim(total, 1 - y_hi, 0, keepdims=False).astype(BF16))
        kept.append(lax.dynamic_index_in_dim(total, y_hi, 0, keepdims=False))

    tokens_kv = token_sums(grad_kv, gathered_kv)
    tokens_kv, _, sent = lax.optimization_barrier((tokens_kv, tokens_q, sent))
    grad_in = [keep + shift(send, "y_hi", 1).astype(F32) for keep, send in zip(kept, sent)]
    grad_in = jnp.concatenate(grad_in, axis=1).astype(BF16)

    sums_kv = tokens_kv.reshape(nz, ny, out_rows, -1).swapaxes(0, 1)
    sums_kv = lax.all_to_all(
        sums_kv.reshape(count // nx, out_rows, -1), ("y_lo", "z"), 0, 0, tiled=True
    )
    sums_kv, sums_q = lax.optimization_barrier((sums_kv, sums_q))
    sums_kv = jnp.sum(sums_kv.astype(F32), axis=0)
    sums_q = sums_q.reshape(ny, out_rows, -1)
    sums_mine = lax.dynamic_index_in_dim(sums_q, at_y, 0, keepdims=False)
    sums_theirs = lax.dynamic_index_in_dim(sums_q, 1 - at_y, 0, keepdims=False)
    sums_q = sums_mine.astype(F32) + shift(sums_theirs, "y_lo", 1).astype(F32)
    grad_w = jnp.concatenate([sums_q, sums_kv], axis=-1) * float(rows * count) ** (-0.5)
    return grad_in, grad_w.astype(BF16)


def solution(mesh):
    dims = SEQ_DIMS[mesh.shape["seq"]] + (2, 2)
    split = Mesh(np.asarray(mesh.devices).reshape(dims), SEQ + KVH)
    return jax.shard_map(
        shards,
        mesh=split,
        in_specs=(
            P(SEQ, None),
            P(None, KVH),
            P(SEQ, KVH),
            P(SEQ, KVH),
            P(SEQ, KVH),
            P(SEQ, KVH),
            P(),
        ),
        out_specs=(P(SEQ + KVH, None), P(SEQ, KVH)),
        check_vma=False,
    )
```

```python
import functools

import jax
import jax.numpy as jnp
import numpy as np
from jax import lax
from jax.experimental import pallas as pl
from jax.experimental.pallas import tpu as pltpu
from jax.sharding import Mesh
from jax.sharding import PartitionSpec as P

LOG2E = 1.4426950408889634
BF16 = jnp.bfloat16
F32 = jnp.float32
SEQ_DIMS = {64: (4, 2, 8), 16: (2, 2, 4)}
SEQ = ("x", "y_lo", "z")
KVH = ("y_hi", "core")
VMEM_LIMIT = 40 * 1024 * 1024


def shift_seq(value, steps, sources=None):
    count = lax.axis_size(SEQ)
    sources = range(count) if sources is None else [s % count for s in sources]
    return lax.ppermute(value, SEQ, [(s, (s + steps) % count) for s in sources])


def shift(value, axis, steps):
    size = lax.axis_size(axis)
    return lax.ppermute(value, axis, [(s, (s + steps) % size) for s in range(size)])


def dot_nt(a, b):
    return lax.dot_general(a, b, (((1,), (1,)), ((), ())), preferred_element_type=F32)


def dot_nn(a, b):
    return lax.dot_general(a, b, (((1,), (0,)), ((), ())), preferred_element_type=F32)


def dot_tn(a, b):
    return lax.dot_general(a, b, (((0,), (0,)), ((), ())), preferred_element_type=F32)


def low_slot_of(me, order):
    return jnp.where(order[2 * me[0]] == me[0], 0, 1)


def offsets(me, order, half):
    slot = low_slot_of(me, order)
    return pl.multiple_of(slot * half, half), pl.multiple_of((1 - slot) * half, half)


def call(kernel, out_shape, args, scratch=(), cost=1, space=pltpu.VMEM):
    vmem = pl.BlockSpec(memory_space=pltpu.VMEM)
    smem = pl.BlockSpec(memory_space=pltpu.SMEM)
    return pl.pallas_call(
        kernel,
        out_shape=out_shape,
        in_specs=[smem, smem] + [pl.BlockSpec(memory_space=space)] * (len(args) - 2),
        out_specs=jax.tree.map(lambda _: vmem, out_shape),
        scratch_shapes=list(scratch),
        compiler_params=pltpu.CompilerParams(vmem_limit_bytes=VMEM_LIMIT),
        cost_estimate=pl.CostEstimate(flops=0, bytes_accessed=int(cost * 3.5e6), transcendentals=0),
    )(*args)


def split_kernel(me, order, keys, values, low, high, sems):
    half, hd = low.shape[0], keys.shape[1]
    copies = []
    for out, off in zip((low, high), offsets(me, order, half)):
        for n, source in enumerate((keys, values)):
            copies.append(
                pltpu.make_async_copy(
                    source.at[pl.ds(off, half), :],
                    out.at[:, n * hd : (n + 1) * hd],
                    sems.at[len(copies)],
                )
            )
    for copy in copies:
        copy.start()
    for copy in copies:
        copy.wait()


def pair_weights(query, grad, key, value, diagonal, scale):
    weights = jnp.exp2(dot_nt(key, query) * (scale * LOG2E))
    if diagonal:
        rows = lax.broadcasted_iota(jnp.int32, weights.shape, 0)
        cols = lax.broadcasted_iota(jnp.int32, weights.shape, 1)
        weights = jnp.where(rows <= cols, weights, 0.0)
    return weights, dot_nt(value, grad)


def add_stats(q, do, stats, heads, piece, place, off, diagonal):
    half, hd = piece.shape[0], piece.shape[1] // 2
    key, value = piece[:, :hd], piece[:, hd:]
    for j in range(heads):
        cols = slice(j * hd, (j + 1) * hd)
        query, grad = q[pl.ds(off, half), cols], do[pl.ds(off, half), cols]
        weights, grad_prob = pair_weights(query, grad, key, value, diagonal, hd**-0.5)
        stats[0, place, j : j + 1, :] += jnp.sum(weights, axis=0, keepdims=True)
        stats[1, place, j : j + 1, :] += jnp.sum(weights * grad_prob, axis=0, keepdims=True)


def add_grads(q, do, stats, dqt, heads, piece, place, off, diagonal):
    half, hd = piece.shape[0], piece.shape[1] // 2
    key, value = piece[:, :hd], piece[:, hd:]
    grad_key = grad_value = None
    for j in range(heads):
        cols = slice(j * hd, (j + 1) * hd)
        query, grad = q[pl.ds(off, half), cols], do[pl.ds(off, half), cols]
        weights, grad_prob = pair_weights(query, grad, key, value, diagonal, hd**-0.5)
        inverse = 1.0 / stats[0, place, j : j + 1, :]
        delta = stats[1, place, j : j + 1, :] * inverse
        prob = weights * inverse
        grad_score = (prob * (grad_prob - delta) * hd**-0.5).astype(BF16)
        term_key = dot_nn(grad_score, query)
        term_value = dot_nn(prob.astype(BF16), grad)
        grad_key = term_key if j == 0 else grad_key + term_key
        grad_value = term_value if j == 0 else grad_value + term_value
        dqt[place, j] += dot_tn(key, grad_score)
    return grad_key, grad_value


def second_quadrant(me, hop, low, high, picked, lo, hi):
    wraps = me[0] < hop
    picked[...] = low[...]

    @pl.when(wraps)
    def _():
        picked[...] = high[...]

    return wraps, jnp.where(wraps, 1, 0), pl.multiple_of(jnp.where(wraps, hi, lo), lo_size(picked))


def lo_size(ref):
    return ref.shape[0]


def own_stats_kernel(heads, me, order, q, do, low, high, stats):
    lo, hi = offsets(me, order, low.shape[0])
    stats[...] = jnp.zeros_like(stats)
    add_stats(q, do, stats, heads, low, 1, hi, False)
    add_stats(q, do, stats, heads, high, 1, hi, True)
    add_stats(q, do, stats, heads, low, 0, lo, True)


def hop_stats_kernel(hops, heads, me, order, q, do, lows, highs, before, stats, picked):
    lo, hi = offsets(me, order, picked.shape[0])
    stats[...] = before[...]
    for n, hop in enumerate(hops):
        low, high = lows.at[n], highs.at[n]
        add_stats(q, do, stats, heads, low, 1, hi, False)
        _, place, off = second_quadrant(me, hop, low, high, picked, lo, hi)
        add_stats(q, do, stats, heads, picked, place, off, False)


def hop_terms(me, hop, q, do, stats, dqt, heads, low, high, picked, acc, lo, hi, out_low, out_high):
    hd = picked.shape[1] // 2
    acc[0, :, :hd], acc[0, :, hd:] = add_grads(q, do, stats, dqt, heads, low, 1, hi, False)
    wraps, place, off = second_quadrant(me, hop, low, high, picked, lo, hi)
    acc[1, :, :hd], acc[1, :, hd:] = add_grads(q, do, stats, dqt, heads, picked, place, off, False)

    @pl.when(wraps)
    def _():
        out_low[...] = acc[0].astype(out_low.dtype)
        out_high[...] = acc[1].astype(out_low.dtype)

    @pl.when(jnp.logical_not(wraps))
    def _():
        out_low[...] = (acc[0] + acc[1]).astype(out_low.dtype)
        out_high[...] = jnp.zeros_like(out_high)


def hop_grads_kernel(hops, first, heads, me, order, q, do, stats, lows, highs, *refs):
    refs = list(refs)
    before = None if first else refs.pop(0)
    dqt, out_lows, out_highs, picked, acc = refs
    lo, hi = offsets(me, order, picked.shape[0])
    dqt[...] = jnp.zeros_like(dqt) if first else before[...]
    for n, hop in enumerate(hops):
        hop_terms(
            me, hop, q, do, stats, dqt, heads, lows.at[n], highs.at[n],
            picked, acc, lo, hi, out_lows.at[n], out_highs.at[n],
        )


def last_grads_kernel(
    heads, me, order, q, do, stats, low1, high1, low, high, before,
    dq, own, term_low, term_high, dqt, picked, acc,
):
    half, hd = low.shape[0], low.shape[1] // 2
    lo, hi = offsets(me, order, half)
    dqt[...] = before[...]
    hop_terms(
        me, 1, q, do, stats, dqt, heads, low1, high1, picked, acc, lo, hi, term_low, term_high
    )
    gk, gv = add_grads(q, do, stats, dqt, heads, low, 1, hi, False)
    gk2, gv2 = add_grads(q, do, stats, dqt, heads, low, 0, lo, True)
    own[0, :, :hd] = gk + gk2
    own[0, :, hd:] = gv + gv2
    own[1, :, :hd], own[1, :, hd:] = add_grads(q, do, stats, dqt, heads, high, 1, hi, True)
    for place, off in ((0, lo), (1, hi)):
        for j in range(heads):
            dq[pl.ds(off, half), j * hd : (j + 1) * hd] = dqt[place, j].T.astype(BF16)


def tokens_kernel(nx, nz, at, order, *refs):
    own, mine, theirs, grads, out = refs[0], refs[1:nx], refs[nx], refs[nx + 1 : -1], refs[-1]
    block = own.shape[1] // nz
    for n in range(2):
        y = at[0] if n == 0 else 1 - at[0]
        total = dot_nn(own[y], grads[0][...])
        for k in range(1, nx):
            piece = mine[k - 1][...] if n == 0 else theirs[k - 1]
            total = total + dot_nn(piece, grads[k][...])
        total = total.astype(BF16)
        for z in range(nz):
            out[y * nz + z] = total[z * block : (z + 1) * block]


def shards(hidden_in, w_qkv, queries, keys, values, d_out, block_order):
    count = lax.axis_size(SEQ)
    nx, ny, nz = (lax.axis_size(axis) for axis in SEQ)
    at_x, at_y = lax.axis_index("x"), lax.axis_index("y_lo")
    core, y_hi = lax.axis_index("core"), lax.axis_index("y_hi")
    index = lax.axis_index(SEQ).astype(jnp.int32)
    me = index.reshape(1)
    rows, width = hidden_in.shape
    half = rows // 2
    hd = keys.shape[1]
    heads = queries.shape[1] // hd
    out_rows = width // count

    piece = jax.ShapeDtypeStruct((half, 2 * hd), BF16)
    stats_shape = jax.ShapeDtypeStruct((2, 2, heads, half), F32)
    partial_q = jax.ShapeDtypeStruct((2, heads, hd, half), F32)
    picked = pltpu.VMEM(piece.shape, BF16)
    acc = pltpu.VMEM((2, half, 2 * hd), F32)

    low, high = call(
        split_kernel, [piece, piece], (me, block_order, keys, values),
        [pltpu.SemaphoreType.DMA((4,))], space=pl.ANY,
    )
    low1 = shift_seq(low, 1)
    high1 = shift_seq(high, 1, (-3, -2, -1))
    low4 = shift_seq(low, 4)
    high4 = shift_seq(high, 4, (-4, -3, -2, -1))

    base = (me, block_order, queries, d_out)
    stats = call(
        functools.partial(own_stats_kernel, heads), stats_shape, (*base, low, high), cost=0.1
    )
    chunks = lax.optimization_barrier(hidden_in.T).reshape(nx, ny, nz * out_rows, rows)
    leaving = [
        lax.dynamic_slice(
            chunks, ((at_x + k) % nx, core, 0, 0), (1, 1, *chunks.shape[2:])
        ).reshape(chunks.shape[2:])
        for k in range(1, nx)
    ]
    low1, high1, low4, high4, stats, leaving = lax.optimization_barrier(
        (low1, high1, low4, high4, stats, leaving)
    )
    low23 = shift_seq(jnp.stack([low, low1]), 2)
    high23 = shift_seq(jnp.stack([high, high1]), 2, (-2, -1, 0))

    def add_hops(hops, lows, highs, stats):
        return call(
            functools.partial(hop_stats_kernel, hops, heads), stats_shape,
            (*base, lows, highs, stats), [picked], cost=1.3 * len(hops),
        )

    stats = add_hops((1,), low1[None], high1[None], stats)
    stats, leaving = lax.optimization_barrier((stats, leaving))
    hidden1, hidden2, hidden3 = (shift(leaving[k - 1], "x", k) for k in range(1, nx))
    stats = add_hops((4,), low4[None], high4[None], stats)
    stats = add_hops((2, 3), low23, high23, stats)

    two, one = (jax.ShapeDtypeStruct((n, *piece.shape), BF16) for n in (2, 1))
    dqt, out23, out23_high = call(
        functools.partial(hop_grads_kernel, (2, 3), True, heads), [partial_q, two, two],
        (*base, stats, low23, high23), [picked, acc], cost=5,
    )
    back23 = shift_seq(out23, -2)
    back23_high = shift_seq(out23_high, -2, (0, 1, 2))
    dqt, hidden1, hidden3 = lax.optimization_barrier((dqt, hidden1, hidden3))
    dqt, out4, out4_high = call(
        functools.partial(hop_grads_kernel, (4,), False, heads), [partial_q, one, one],
        (*base, stats, low4[None], high4[None], dqt), [picked, acc], cost=3,
    )
    back4 = shift_seq(out4[0], -4)
    back4_high = shift_seq(out4_high[0], -4, (0, 1, 2, 3))
    term = jax.ShapeDtypeStruct(piece.shape, F32)
    grad_q, own, out1, out1_high = call(
        functools.partial(last_grads_kernel, heads),
        [jax.ShapeDtypeStruct(queries.shape, BF16), jax.ShapeDtypeStruct((2, *piece.shape), F32), term, term],
        (*base, stats, low1, high1, low, high, dqt),
        [pltpu.VMEM(partial_q.shape, F32), picked, acc], cost=20,
    )
    grad_q, back23, back23_high, back4, back4_high, hidden2 = lax.optimization_barrier(
        (grad_q, back23, back23_high, back4, back4_high, hidden2)
    )
    back1 = shift_seq((out1 + back23[1].astype(F32)).astype(BF16), -1)
    back1_high = shift_seq((out1_high + back23_high[1].astype(F32)).astype(BF16), -1, (-2, -1, 0))

    def x_gathered(matrix):
        return [matrix] + [shift(matrix, "x", k) for k in range(1, nx)]

    gathered_q = x_gathered(grad_q)
    arrived = jnp.stack([hidden1, hidden2, hidden3])
    arrived, back1, back1_high = lax.optimization_barrier((arrived, back1, back1_high))
    hidden_theirs = shift(arrived, "core", 1)
    hidden_own = lax.dynamic_index_in_dim(chunks, at_x, 0, keepdims=False)

    low_total = own[0] + back23[0].astype(F32) + back1.astype(F32) + back4.astype(F32)
    high_total = (
        own[1] + back23_high[0].astype(F32) + back1_high.astype(F32) + back4_high.astype(F32)
    )
    low_total, high_total = low_total.astype(BF16), high_total.astype(BF16)
    grad_kv = jnp.where(
        low_slot_of(me, block_order) == 0,
        jnp.concatenate([low_total, high_total], axis=0),
        jnp.concatenate([high_total, low_total], axis=0),
    )

    grads = jnp.concatenate([grad_q, grad_kv], axis=1).reshape(2, 2, rows // 4, -1)
    theirs = lax.dynamic_index_in_dim(grads, 1 - core, 1, keepdims=False).reshape(half, -1)
    mine = lax.dynamic_index_in_dim(grads, core, 1, keepdims=False).reshape(half, -1)
    step = width // 2
    kept, sent = [], []
    for start in range(0, width, step):
        weight = w_qkv[start : start + step]
        received = shift(dot_nt(theirs, weight).astype(BF16), "core", 1)
        total = (dot_nt(mine, weight) + received.astype(F32)).reshape(2, rows // 4, step)
        sent.append(lax.dynamic_index_in_dim(total, 1 - y_hi, 0, keepdims=False).astype(BF16))
        kept.append(lax.dynamic_index_in_dim(total, y_hi, 0, keepdims=False))

    def token_sums(gathered):
        return call(
            functools.partial(tokens_kernel, nx, nz),
            jax.ShapeDtypeStruct((ny * nz, out_rows, gathered[0].shape[1]), BF16),
            (
                core.astype(jnp.int32).reshape(1), block_order, hidden_own,
                hidden1, hidden2, hidden3, hidden_theirs, *gathered,
            ),
            cost=2,
        )

    def total_over(pieces):
        return lax.all_to_all(pieces, ("y_lo", "z"), 0, 0, tiled=True)

    grad_kv, gathered_q = lax.optimization_barrier((grad_kv, gathered_q))
    gathered_kv = x_gathered(grad_kv)
    tokens_q, sent = lax.optimization_barrier((token_sums(gathered_q), sent))
    grad_in = [keep + shift(send, "y_hi", 1).astype(F32) for keep, send in zip(kept, sent)]
    grad_in = jnp.concatenate(grad_in, axis=1).astype(BF16)
    sums_q = total_over(tokens_q)
    sums_kv = total_over(token_sums(gathered_kv))
    sums = jnp.concatenate(
        [jnp.sum(part.astype(F32), axis=0) for part in (sums_q, sums_kv)], axis=-1
    )
    return grad_in, (sums * float(rows * count) ** (-0.5)).astype(BF16)


def solution(mesh):
    dims = SEQ_DIMS[mesh.shape["seq"]] + (2, 2)
    split = Mesh(np.asarray(mesh.devices).reshape(dims), SEQ + KVH)
    return jax.shard_map(
        shards,
        mesh=split,
        in_specs=(
            P(SEQ, None),
            P(None, KVH),
            P(SEQ, KVH),
            P(SEQ, KVH),
            P(SEQ, KVH),
            P(SEQ, KVH),
            P(),
        ),
        out_specs=(P(SEQ + KVH, None), P(SEQ, KVH)),
        check_vma=False,
    )
```

```python
import functools

import jax
import jax.numpy as jnp
import numpy as np
from jax import lax
from jax.experimental import pallas as pl
from jax.experimental.pallas import tpu as pltpu
from jax.sharding import Mesh
from jax.sharding import PartitionSpec as P

LOG2E = 1.4426950408889634
BF16 = jnp.bfloat16
F32 = jnp.float32
SEQ_DIMS = {64: (4, 2, 8), 16: (2, 2, 4)}
SEQ = ("x", "y_lo", "z")
KVH = ("y_hi", "core")
VMEM_LIMIT = 40 * 1024 * 1024


def shift_seq(value, steps, sources=None):
    count = lax.axis_size(SEQ)
    sources = range(count) if sources is None else [s % count for s in sources]
    return lax.ppermute(value, SEQ, [(s, (s + steps) % count) for s in sources])


def shift(value, axis, steps):
    size = lax.axis_size(axis)
    return lax.ppermute(value, axis, [(s, (s + steps) % size) for s in range(size)])


def dot_nt(a, b):
    return lax.dot_general(a, b, (((1,), (1,)), ((), ())), preferred_element_type=F32)


def dot_nn(a, b):
    return lax.dot_general(a, b, (((1,), (0,)), ((), ())), preferred_element_type=F32)


def dot_tn(a, b):
    return lax.dot_general(a, b, (((0,), (0,)), ((), ())), preferred_element_type=F32)


def low_slot_of(me, order):
    return jnp.where(order[2 * me[0]] == me[0], 0, 1)


def offsets(me, order, half):
    slot = low_slot_of(me, order)
    return pl.multiple_of(slot * half, half), pl.multiple_of((1 - slot) * half, half)


def call(kernel, out_shape, args, scratch=(), cost=1, space=pltpu.VMEM):
    vmem = pl.BlockSpec(memory_space=pltpu.VMEM)
    smem = pl.BlockSpec(memory_space=pltpu.SMEM)
    return pl.pallas_call(
        kernel,
        out_shape=out_shape,
        in_specs=[smem, smem] + [pl.BlockSpec(memory_space=space)] * (len(args) - 2),
        out_specs=jax.tree.map(lambda _: vmem, out_shape),
        scratch_shapes=list(scratch),
        compiler_params=pltpu.CompilerParams(vmem_limit_bytes=VMEM_LIMIT),
        cost_estimate=pl.CostEstimate(flops=0, bytes_accessed=int(cost * 3.5e6), transcendentals=0),
    )(*args)


def split_kernel(me, order, keys, values, low, high, sems):
    half, hd = low.shape[0], keys.shape[1]
    copies = []
    for out, off in zip((low, high), offsets(me, order, half)):
        for n, source in enumerate((keys, values)):
            copies.append(
                pltpu.make_async_copy(
                    source.at[pl.ds(off, half), :],
                    out.at[:, n * hd : (n + 1) * hd],
                    sems.at[len(copies)],
                )
            )
    for copy in copies:
        copy.start()
    for copy in copies:
        copy.wait()


def pair_weights(query, grad, key, value, diagonal, scale):
    weights = jnp.exp2(dot_nt(key, query) * (scale * LOG2E))
    if diagonal:
        rows = lax.broadcasted_iota(jnp.int32, weights.shape, 0)
        cols = lax.broadcasted_iota(jnp.int32, weights.shape, 1)
        weights = jnp.where(rows <= cols, weights, 0.0)
    return weights, dot_nt(value, grad)


def add_stats(q, do, stats, heads, piece, place, off, diagonal):
    half, hd = piece.shape[0], piece.shape[1] // 2
    key, value = piece[:, :hd], piece[:, hd:]
    for j in range(heads):
        cols = slice(j * hd, (j + 1) * hd)
        query, grad = q[pl.ds(off, half), cols], do[pl.ds(off, half), cols]
        weights, grad_prob = pair_weights(query, grad, key, value, diagonal, hd**-0.5)
        stats[0, place, j : j + 1, :] += jnp.sum(weights, axis=0, keepdims=True)
        stats[1, place, j : j + 1, :] += jnp.sum(weights * grad_prob, axis=0, keepdims=True)


def add_grads(q, do, stats, dqt, heads, piece, place, off, diagonal):
    half, hd = piece.shape[0], piece.shape[1] // 2
    key, value = piece[:, :hd], piece[:, hd:]
    grad_key = grad_value = None
    for j in range(heads):
        cols = slice(j * hd, (j + 1) * hd)
        query, grad = q[pl.ds(off, half), cols], do[pl.ds(off, half), cols]
        weights, grad_prob = pair_weights(query, grad, key, value, diagonal, hd**-0.5)
        inverse = 1.0 / stats[0, place, j : j + 1, :]
        delta = stats[1, place, j : j + 1, :] * inverse
        prob = weights * inverse
        grad_score = (prob * (grad_prob - delta) * hd**-0.5).astype(BF16)
        term_key = dot_nn(grad_score, query)
        term_value = dot_nn(prob.astype(BF16), grad)
        grad_key = term_key if j == 0 else grad_key + term_key
        grad_value = term_value if j == 0 else grad_value + term_value
        dqt[place, j] += dot_tn(key, grad_score)
    return grad_key, grad_value


def second_quadrant(me, hop, low, high, picked, lo, hi):
    wraps = me[0] < hop
    picked[...] = low[...]

    @pl.when(wraps)
    def _():
        picked[...] = high[...]

    return wraps, jnp.where(wraps, 1, 0), pl.multiple_of(jnp.where(wraps, hi, lo), lo_size(picked))


def lo_size(ref):
    return ref.shape[0]


def near_stats_kernel(heads, me, order, q, do, low, high, low1, high1, low4, high4, stats, picked):
    lo, hi = offsets(me, order, low.shape[0])
    stats[...] = jnp.zeros_like(stats)
    add_stats(q, do, stats, heads, low, 1, hi, False)
    add_stats(q, do, stats, heads, high, 1, hi, True)
    add_stats(q, do, stats, heads, low, 0, lo, True)
    hop_stats(me, 1, q, do, stats, heads, low1, high1, picked, lo, hi)
    hop_stats(me, 4, q, do, stats, heads, low4, high4, picked, lo, hi)


def hop_stats(me, hop, q, do, stats, heads, low, high, picked, lo, hi):
    add_stats(q, do, stats, heads, low, 1, hi, False)
    _, place, off = second_quadrant(me, hop, low, high, picked, lo, hi)
    add_stats(q, do, stats, heads, picked, place, off, False)


def hop_terms(me, hop, q, do, stats, dqt, heads, low, high, picked, acc, lo, hi, out_low, out_high):
    hd = picked.shape[1] // 2
    acc[0, :, :hd], acc[0, :, hd:] = add_grads(q, do, stats, dqt, heads, low, 1, hi, False)
    wraps, place, off = second_quadrant(me, hop, low, high, picked, lo, hi)
    acc[1, :, :hd], acc[1, :, hd:] = add_grads(q, do, stats, dqt, heads, picked, place, off, False)

    @pl.when(wraps)
    def _():
        out_low[...] = acc[0].astype(out_low.dtype)
        out_high[...] = acc[1].astype(out_low.dtype)

    @pl.when(jnp.logical_not(wraps))
    def _():
        out_low[...] = (acc[0] + acc[1]).astype(out_low.dtype)
        out_high[...] = jnp.zeros_like(out_high)


def far_grads_kernel(
    heads, me, order, q, do, lows, highs, before, stats, dqt, out_lows, out_highs, picked, acc
):
    lo, hi = offsets(me, order, picked.shape[0])
    stats[...] = before[...]
    for n, hop in enumerate((2, 3)):
        hop_stats(me, hop, q, do, stats, heads, lows.at[n], highs.at[n], picked, lo, hi)
    dqt[...] = jnp.zeros_like(dqt)
    for n, hop in enumerate((2, 3)):
        hop_terms(
            me, hop, q, do, stats, dqt, heads, lows.at[n], highs.at[n],
            picked, acc, lo, hi, out_lows.at[n], out_highs.at[n],
        )


def near_grads_kernel(
    heads, me, order, q, do, stats, low4, high4, low1, high1, low, high, before,
    dq, own, term4_low, term4_high, term1_low, term1_high, dqt, picked, acc,
):
    half, hd = low.shape[0], low.shape[1] // 2
    lo, hi = offsets(me, order, half)
    dqt[...] = before[...]
    for hop, *refs, outs in (
        (4, low4, high4, (term4_low, term4_high)), (1, low1, high1, (term1_low, term1_high))
    ):
        hop_terms(me, hop, q, do, stats, dqt, heads, *refs, picked, acc, lo, hi, *outs)
    gk, gv = add_grads(q, do, stats, dqt, heads, low, 1, hi, False)
    gk2, gv2 = add_grads(q, do, stats, dqt, heads, low, 0, lo, True)
    own[0, :, :hd] = gk + gk2
    own[0, :, hd:] = gv + gv2
    own[1, :, :hd], own[1, :, hd:] = add_grads(q, do, stats, dqt, heads, high, 1, hi, True)
    for place, off in ((0, lo), (1, hi)):
        for j in range(heads):
            dq[pl.ds(off, half), j * hd : (j + 1) * hd] = dqt[place, j].T.astype(BF16)


def tokens_kernel(nx, nz, at, order, *refs):
    own, mine, theirs, grads, out = refs[0], refs[1:nx], refs[nx], refs[nx + 1 : -1], refs[-1]
    block = own.shape[1] // nz
    for n in range(2):
        y = at[0] if n == 0 else 1 - at[0]
        total = dot_nn(own[y], grads[0][...])
        for k in range(1, nx):
            piece = mine[k - 1][...] if n == 0 else theirs[k - 1]
            total = total + dot_nn(piece, grads[k][...])
        total = total.astype(BF16)
        for z in range(nz):
            out[y * nz + z] = total[z * block : (z + 1) * block]


def shards(hidden_in, w_qkv, queries, keys, values, d_out, block_order):
    count = lax.axis_size(SEQ)
    nx, ny, nz = (lax.axis_size(axis) for axis in SEQ)
    at_x, at_y = lax.axis_index("x"), lax.axis_index("y_lo")
    core, y_hi = lax.axis_index("core"), lax.axis_index("y_hi")
    index = lax.axis_index(SEQ).astype(jnp.int32)
    me = index.reshape(1)
    rows, width = hidden_in.shape
    half = rows // 2
    hd = keys.shape[1]
    heads = queries.shape[1] // hd
    out_rows = width // count

    piece = jax.ShapeDtypeStruct((half, 2 * hd), BF16)
    stats_shape = jax.ShapeDtypeStruct((2, 2, heads, half), F32)
    partial_q = jax.ShapeDtypeStruct((2, heads, hd, half), F32)
    picked = pltpu.VMEM(piece.shape, BF16)
    acc = pltpu.VMEM((2, half, 2 * hd), F32)

    low, high = call(
        split_kernel, [piece, piece], (me, block_order, keys, values),
        [pltpu.SemaphoreType.DMA((4,))], space=pltpu.HBM,
    )
    low1 = shift_seq(low, 1)
    high1 = shift_seq(high, 1, (-3, -2, -1))
    low4 = shift_seq(low, 4)
    high4 = shift_seq(high, 4, (-4, -3, -2, -1))

    chunks = lax.optimization_barrier(hidden_in.T).reshape(nx, ny, nz * out_rows, rows)
    low1, high1, chunks = lax.optimization_barrier((low1, high1, chunks))
    low23 = shift_seq(jnp.stack([low, low1]), 2)
    high23 = shift_seq(jnp.stack([high, high1]), 2, (-2, -1, 0))

    base = (me, block_order, queries, d_out)
    stats = call(
        functools.partial(near_stats_kernel, heads), stats_shape,
        (*base, low, high, low1, high1, low4, high4), [picked], cost=5,
    )
    leaving = [
        lax.dynamic_slice(
            chunks, ((at_x + k) % nx, core, 0, 0), (1, 1, *chunks.shape[2:])
        ).reshape(chunks.shape[2:])
        for k in range(1, nx)
    ]
    stats, leaving = lax.optimization_barrier((stats, leaving))
    hidden1, hidden2, hidden3 = (shift(leaving[k - 1], "x", k) for k in range(1, nx))
    two = jax.ShapeDtypeStruct((2, *piece.shape), BF16)
    stats, dqt, out23, out23_high = call(
        functools.partial(far_grads_kernel, heads), [stats_shape, partial_q, two, two],
        (*base, low23, high23, stats), [picked, acc], cost=8,
    )
    back23 = shift_seq(out23, -2)
    back23_high = shift_seq(out23_high, -2, (0, 1, 2))

    dqt, hidden1, hidden3 = lax.optimization_barrier((dqt, hidden1, hidden3))
    term = jax.ShapeDtypeStruct(piece.shape, F32)
    grad_q, own, out4, out4_high, out1, out1_high = call(
        functools.partial(near_grads_kernel, heads),
        [jax.ShapeDtypeStruct(queries.shape, BF16), jax.ShapeDtypeStruct((2, *piece.shape), F32),
         piece, piece, term, term],
        (*base, stats, low4, high4, low1, high1, low, high, dqt),
        [pltpu.VMEM(partial_q.shape, F32), picked, acc], cost=20,
    )
    back4 = shift_seq(out4, -4)
    back4_high = shift_seq(out4_high, -4, (0, 1, 2, 3))
    back1 = shift_seq((out1 + back23[1].astype(F32)).astype(BF16), -1)
    back1_high = shift_seq((out1_high + back23_high[1].astype(F32)).astype(BF16), -1, (-2, -1, 0))

    def x_gathered(matrix):
        return [matrix] + [shift(matrix, "x", k) for k in range(1, nx)]

    grad_q, hidden2 = lax.optimization_barrier((grad_q, hidden2))
    hidden = [hidden1, hidden2, hidden3]
    gathered_q = x_gathered(grad_q)
    arrived, back1, back1_high = lax.optimization_barrier((jnp.stack(hidden), back1, back1_high))
    hidden_theirs = shift(arrived, "core", 1)
    hidden_own = lax.dynamic_index_in_dim(chunks, at_x, 0, keepdims=False)

    low_total = own[0] + back23[0].astype(F32) + back1.astype(F32) + back4.astype(F32)
    high_total = (
        own[1] + back23_high[0].astype(F32) + back1_high.astype(F32) + back4_high.astype(F32)
    )
    low_total, high_total = low_total.astype(BF16), high_total.astype(BF16)
    grad_kv = jnp.where(
        low_slot_of(me, block_order) == 0,
        jnp.concatenate([low_total, high_total], axis=0),
        jnp.concatenate([high_total, low_total], axis=0),
    )

    grads = jnp.concatenate([grad_q, grad_kv], axis=1).reshape(2, 2, rows // 4, -1)
    theirs = lax.dynamic_index_in_dim(grads, 1 - core, 1, keepdims=False).reshape(half, -1)
    mine = lax.dynamic_index_in_dim(grads, core, 1, keepdims=False).reshape(half, -1)
    step = width // 2
    weights = [w_qkv[start : start + step] for start in range(0, width, step)]
    received = [shift(dot_nt(theirs, weight).astype(BF16), "core", 1) for weight in weights]
    totals = lax.optimization_barrier([dot_nt(mine, weight) for weight in weights])
    kept, sent = [], []
    for total, other in zip(totals, received):
        total = (total + other.astype(F32)).reshape(2, rows // 4, step)
        sent.append(lax.dynamic_index_in_dim(total, 1 - y_hi, 0, keepdims=False).astype(BF16))
        kept.append(lax.dynamic_index_in_dim(total, y_hi, 0, keepdims=False))

    def token_sums(gathered):
        return call(
            functools.partial(tokens_kernel, nx, nz),
            jax.ShapeDtypeStruct((ny * nz, out_rows, gathered[0].shape[1]), BF16),
            (
                core.astype(jnp.int32).reshape(1), block_order, hidden_own,
                *hidden, hidden_theirs, *gathered,
            ),
            cost=2,
        )

    def total_over(pieces):
        return lax.all_to_all(pieces, ("y_lo", "z"), 0, 0, tiled=True)

    grad_kv, gathered_q = lax.optimization_barrier((grad_kv, gathered_q))
    gathered_kv = x_gathered(grad_kv)
    tokens_q = token_sums(gathered_q)
    tokens_q, sent = lax.optimization_barrier((tokens_q, sent))
    sums_q = total_over(tokens_q)
    grad_in = [keep + shift(send, "y_hi", 1).astype(F32) for keep, send in zip(kept, sent)]
    grad_in = jnp.concatenate(grad_in, axis=1).astype(BF16)
    gathered_kv, _ = lax.optimization_barrier((gathered_kv, tokens_q))
    sums_kv = total_over(token_sums(gathered_kv))
    sums = jnp.concatenate(
        [jnp.sum(part.astype(F32), axis=0) for part in (sums_q, sums_kv)], axis=-1
    )
    return grad_in, (sums * float(rows * count) ** (-0.5)).astype(BF16)


def solution(mesh):
    dims = SEQ_DIMS[mesh.shape["seq"]] + (2, 2)
    split = Mesh(np.asarray(mesh.devices).reshape(dims), SEQ + KVH)
    return jax.shard_map(
        shards,
        mesh=split,
        in_specs=(
            P(SEQ, None),
            P(None, KVH),
            P(SEQ, KVH),
            P(SEQ, KVH),
            P(SEQ, KVH),
            P(SEQ, KVH),
            P(),
        ),
        out_specs=(P(SEQ + KVH, None), P(SEQ, KVH)),
        check_vma=False,
    )
```

```python
import functools

import jax
import jax.numpy as jnp
import numpy as np
from jax import lax
from jax.experimental import pallas as pl
from jax.experimental.pallas import tpu as pltpu
from jax.sharding import Mesh
from jax.sharding import PartitionSpec as P

LOG2E = 1.4426950408889634
BF16 = jnp.bfloat16
F32 = jnp.float32
SEQ_DIMS = {64: (4, 2, 8), 16: (2, 2, 4)}
SEQ = ("x", "y_lo", "z")
KVH = ("y_hi", "core")
VMEM_LIMIT = 16 * 1024 * 1024


def shift_seq(value, steps, sources=None):
    count = lax.axis_size(SEQ)
    sources = range(count) if sources is None else [s % count for s in sources]
    return lax.ppermute(value, SEQ, [(s, (s + steps) % count) for s in sources])


def shift(value, axis, steps):
    size = lax.axis_size(axis)
    return lax.ppermute(value, axis, [(s, (s + steps) % size) for s in range(size)])


def dot_nt(a, b):
    return lax.dot_general(a, b, (((1,), (1,)), ((), ())), preferred_element_type=F32)


def dot_nn(a, b):
    return lax.dot_general(a, b, (((1,), (0,)), ((), ())), preferred_element_type=F32)


def dot_tn(a, b):
    return lax.dot_general(a, b, (((0,), (0,)), ((), ())), preferred_element_type=F32)


def low_slot_of(me, order):
    return jnp.where(order[2 * me[0]] == me[0], 0, 1)


def offsets(me, order, half):
    slot = low_slot_of(me, order)
    return pl.multiple_of(slot * half, half), pl.multiple_of((1 - slot) * half, half)


def call(kernel, out_shape, args, scratch=(), cost=1, space=pltpu.VMEM):
    vmem = pl.BlockSpec(memory_space=pltpu.VMEM)
    smem = pl.BlockSpec(memory_space=pltpu.SMEM)
    return pl.pallas_call(
        kernel,
        out_shape=out_shape,
        in_specs=[smem, smem] + [pl.BlockSpec(memory_space=space)] * (len(args) - 2),
        out_specs=jax.tree.map(lambda _: vmem, out_shape),
        scratch_shapes=list(scratch),
        compiler_params=pltpu.CompilerParams(vmem_limit_bytes=VMEM_LIMIT),
        cost_estimate=pl.CostEstimate(flops=0, bytes_accessed=int(cost * 3.5e6), transcendentals=0),
    )(*args)


def split_kernel(me, order, keys, values, low, high, sems):
    half, hd = low.shape[0], keys.shape[1]
    copies = []
    for out, off in zip((low, high), offsets(me, order, half)):
        for n, source in enumerate((keys, values)):
            copies.append(
                pltpu.make_async_copy(
                    source.at[pl.ds(off, half), :],
                    out.at[:, n * hd : (n + 1) * hd],
                    sems.at[len(copies)],
                )
            )
    for copy in copies:
        copy.start()
    for copy in copies:
        copy.wait()


def pair_weights(query, grad, key, value, diagonal, scale):
    weights = jnp.exp2(dot_nt(key, query) * (scale * LOG2E))
    if diagonal:
        rows = lax.broadcasted_iota(jnp.int32, weights.shape, 0)
        cols = lax.broadcasted_iota(jnp.int32, weights.shape, 1)
        weights = jnp.where(rows <= cols, weights, 0.0)
    return weights, dot_nt(value, grad)


def add_stats(q, do, stats, heads, piece, place, off, diagonal):
    half, hd = piece.shape[0], piece.shape[1] // 2
    key, value = piece[:, :hd], piece[:, hd:]
    for j in range(heads):
        cols = slice(j * hd, (j + 1) * hd)
        query, grad = q[pl.ds(off, half), cols], do[pl.ds(off, half), cols]
        weights, grad_prob = pair_weights(query, grad, key, value, diagonal, hd**-0.5)
        stats[0, place, j : j + 1, :] += jnp.sum(weights, axis=0, keepdims=True)
        stats[1, place, j : j + 1, :] += jnp.sum(weights * grad_prob, axis=0, keepdims=True)


def add_grads(q, do, stats, dqt, heads, piece, place, off, diagonal):
    half, hd = piece.shape[0], piece.shape[1] // 2
    key, value = piece[:, :hd], piece[:, hd:]
    grad_key = grad_value = None
    for j in range(heads):
        cols = slice(j * hd, (j + 1) * hd)
        query, grad = q[pl.ds(off, half), cols], do[pl.ds(off, half), cols]
        weights, grad_prob = pair_weights(query, grad, key, value, diagonal, hd**-0.5)
        inverse = 1.0 / stats[0, place, j : j + 1, :]
        delta = stats[1, place, j : j + 1, :] * inverse
        prob = weights * inverse
        grad_score = (prob * (grad_prob - delta) * hd**-0.5).astype(BF16)
        term_key = dot_nn(grad_score, query)
        term_value = dot_nn(prob.astype(BF16), grad)
        grad_key = term_key if j == 0 else grad_key + term_key
        grad_value = term_value if j == 0 else grad_value + term_value
        dqt[place, j] += dot_tn(key, grad_score)
    return grad_key, grad_value


def second_quadrant(me, hop, low, high, picked, lo, hi):
    wraps = me[0] < hop
    picked[...] = low[...]

    @pl.when(wraps)
    def _():
        picked[...] = high[...]

    return wraps, jnp.where(wraps, 1, 0), pl.multiple_of(jnp.where(wraps, hi, lo), lo_size(picked))


def lo_size(ref):
    return ref.shape[0]


def near_stats_kernel(heads, me, order, q, do, low, high, low1, high1, low4, high4, stats, picked):
    lo, hi = offsets(me, order, low.shape[0])
    stats[...] = jnp.zeros_like(stats)
    add_stats(q, do, stats, heads, low, 1, hi, False)
    add_stats(q, do, stats, heads, high, 1, hi, True)
    add_stats(q, do, stats, heads, low, 0, lo, True)
    hop_stats(me, 1, q, do, stats, heads, low1, high1, picked, lo, hi)
    hop_stats(me, 4, q, do, stats, heads, low4, high4, picked, lo, hi)


def hop_stats(me, hop, q, do, stats, heads, low, high, picked, lo, hi):
    add_stats(q, do, stats, heads, low, 1, hi, False)
    _, place, off = second_quadrant(me, hop, low, high, picked, lo, hi)
    add_stats(q, do, stats, heads, picked, place, off, False)


def hop_terms(me, hop, q, do, stats, dqt, heads, low, high, picked, acc, lo, hi, out_low, out_high):
    hd = picked.shape[1] // 2
    acc[0, :, :hd], acc[0, :, hd:] = add_grads(q, do, stats, dqt, heads, low, 1, hi, False)
    wraps, place, off = second_quadrant(me, hop, low, high, picked, lo, hi)
    acc[1, :, :hd], acc[1, :, hd:] = add_grads(q, do, stats, dqt, heads, picked, place, off, False)

    @pl.when(wraps)
    def _():
        out_low[...] = acc[0].astype(out_low.dtype)
        out_high[...] = acc[1].astype(out_low.dtype)

    @pl.when(jnp.logical_not(wraps))
    def _():
        out_low[...] = (acc[0] + acc[1]).astype(out_low.dtype)
        out_high[...] = jnp.zeros_like(out_high)


def far_grads_kernel(
    heads, me, order, q, do, lows, highs, before, stats, dqt, out_lows, out_highs, picked, acc
):
    lo, hi = offsets(me, order, picked.shape[0])
    stats[...] = before[...]
    for n, hop in enumerate((2, 3)):
        hop_stats(me, hop, q, do, stats, heads, lows.at[n], highs.at[n], picked, lo, hi)
    dqt[...] = jnp.zeros_like(dqt)
    for n, hop in enumerate((2, 3)):
        hop_terms(
            me, hop, q, do, stats, dqt, heads, lows.at[n], highs.at[n],
            picked, acc, lo, hi, out_lows.at[n], out_highs.at[n],
        )


def near_grads_kernel(
    heads, me, order, q, do, stats, low4, high4, low1, high1, low, high, before,
    dq, own, term4_low, term4_high, term1_low, term1_high, dqt, picked, acc,
):
    half, hd = low.shape[0], low.shape[1] // 2
    lo, hi = offsets(me, order, half)
    dqt[...] = before[...]
    for hop, *refs, outs in (
        (4, low4, high4, (term4_low, term4_high)), (1, low1, high1, (term1_low, term1_high))
    ):
        hop_terms(me, hop, q, do, stats, dqt, heads, *refs, picked, acc, lo, hi, *outs)
    gk, gv = add_grads(q, do, stats, dqt, heads, low, 1, hi, False)
    gk2, gv2 = add_grads(q, do, stats, dqt, heads, low, 0, lo, True)
    own[0, :, :hd] = gk + gk2
    own[0, :, hd:] = gv + gv2
    own[1, :, :hd], own[1, :, hd:] = add_grads(q, do, stats, dqt, heads, high, 1, hi, True)
    for place, off in ((0, lo), (1, hi)):
        for j in range(heads):
            dq[pl.ds(off, half), j * hd : (j + 1) * hd] = dqt[place, j].T.astype(BF16)


def tokens_kernel(nx, nz, at, order, *refs):
    own, mine, theirs, grads, out = refs[0], refs[1:nx], refs[nx], refs[nx + 1 : -1], refs[-1]
    block = own.shape[1] // nz
    for n in range(2):
        y = at[0] if n == 0 else 1 - at[0]
        total = dot_nn(own[y], grads[0][...])
        for k in range(1, nx):
            piece = mine[k - 1][...] if n == 0 else theirs[k - 1]
            total = total + dot_nn(piece, grads[k][...])
        total = total.astype(BF16)
        for z in range(nz):
            out[y * nz + z] = total[z * block : (z + 1) * block]


def shards(hidden_in, w_qkv, queries, keys, values, d_out, block_order):
    count = lax.axis_size(SEQ)
    nx, ny, nz = (lax.axis_size(axis) for axis in SEQ)
    at_x, at_y = lax.axis_index("x"), lax.axis_index("y_lo")
    core, y_hi = lax.axis_index("core"), lax.axis_index("y_hi")
    index = lax.axis_index(SEQ).astype(jnp.int32)
    me = index.reshape(1)
    rows, width = hidden_in.shape
    half = rows // 2
    hd = keys.shape[1]
    heads = queries.shape[1] // hd
    out_rows = width // count

    piece = jax.ShapeDtypeStruct((half, 2 * hd), BF16)
    stats_shape = jax.ShapeDtypeStruct((2, 2, heads, half), F32)
    partial_q = jax.ShapeDtypeStruct((2, heads, hd, half), F32)
    picked = pltpu.VMEM(piece.shape, BF16)
    acc = pltpu.VMEM((2, half, 2 * hd), F32)

    low, high = call(
        split_kernel, [piece, piece], (me, block_order, keys, values),
        [pltpu.SemaphoreType.DMA((4,))], space=pltpu.HBM,
    )
    low1 = shift_seq(low, 1)
    high1 = shift_seq(high, 1, (-3, -2, -1))
    low4 = shift_seq(low, 4)
    high4 = shift_seq(high, 4, (-4, -3, -2, -1))

    hidden_t = lax.optimization_barrier(hidden_in.T)
    low1, high1, low4, high4, hidden_t = lax.optimization_barrier(
        (low1, high1, low4, high4, hidden_t)
    )
    pair, pair_high = jnp.stack([low, low1]), jnp.stack([high, high1])
    low23 = shift_seq(pair, 2)
    high23 = shift_seq(pair_high, 2, (-2, -1, 0))

    base = (me, block_order, queries, d_out)
    stats = call(
        functools.partial(near_stats_kernel, heads), stats_shape,
        (*base, low, high, low1, high1, low4, high4), [picked], cost=5,
    )
    chunks = hidden_t.reshape(nx, ny, nz * out_rows, rows)
    leaving = [
        lax.dynamic_slice(
            chunks, ((at_x + k) % nx, core, 0, 0), (1, 1, *chunks.shape[2:])
        ).reshape(chunks.shape[2:])
        for k in range(1, nx)
    ]
    low23, high23, stats, leaving = lax.optimization_barrier((low23, high23, stats, leaving))
    hidden1, hidden2, hidden3 = (shift(leaving[k - 1], "x", k) for k in range(1, nx))
    two = jax.ShapeDtypeStruct((2, *piece.shape), BF16)
    stats, dqt, out23, out23_high = call(
        functools.partial(far_grads_kernel, heads), [stats_shape, partial_q, two, two],
        (*base, low23, high23, stats), [picked, acc], cost=8,
    )
    back23 = shift_seq(out23, -2)
    back23_high = shift_seq(out23_high, -2, (0, 1, 2))

    dqt, hidden1, hidden3 = lax.optimization_barrier((dqt, hidden1, hidden3))
    term = jax.ShapeDtypeStruct(piece.shape, F32)
    grad_q, own, out4, out4_high, out1, out1_high = call(
        functools.partial(near_grads_kernel, heads),
        [jax.ShapeDtypeStruct(queries.shape, BF16), jax.ShapeDtypeStruct((2, *piece.shape), F32),
         piece, piece, term, term],
        (*base, stats, low4, high4, low1, high1, low, high, dqt),
        [pltpu.VMEM(partial_q.shape, F32), picked, acc], cost=20,
    )
    back4 = shift_seq(out4, -4)
    back4_high = shift_seq(out4_high, -4, (0, 1, 2, 3))
    back1 = shift_seq((out1 + back23[1].astype(F32)).astype(BF16), -1)
    back1_high = shift_seq((out1_high + back23_high[1].astype(F32)).astype(BF16), -1, (-2, -1, 0))

    def x_gathered(matrix):
        return [matrix] + [shift(matrix, "x", k) for k in range(1, nx)]

    grad_q, hidden2 = lax.optimization_barrier((grad_q, hidden2))
    hidden = [hidden1, hidden2, hidden3]
    gathered_q = x_gathered(grad_q)
    arrived, back1, back1_high = lax.optimization_barrier((jnp.stack(hidden), back1, back1_high))
    hidden_theirs = shift(arrived, "core", 1)
    hidden_own = lax.dynamic_index_in_dim(chunks, at_x, 0, keepdims=False)

    low_total = own[0] + back23[0].astype(F32) + back1.astype(F32) + back4.astype(F32)
    high_total = (
        own[1] + back23_high[0].astype(F32) + back1_high.astype(F32) + back4_high.astype(F32)
    )
    low_total, high_total = low_total.astype(BF16), high_total.astype(BF16)
    grad_kv = jnp.where(
        low_slot_of(me, block_order) == 0,
        jnp.concatenate([low_total, high_total], axis=0),
        jnp.concatenate([high_total, low_total], axis=0),
    )

    grad_kv, gathered_q = lax.optimization_barrier((grad_kv, gathered_q))
    gathered_kv = x_gathered(grad_kv)

    grads = jnp.concatenate([grad_q, grad_kv], axis=1).reshape(2, 2, rows // 4, -1)
    theirs = lax.dynamic_index_in_dim(grads, 1 - core, 1, keepdims=False).reshape(half, -1)
    mine = lax.dynamic_index_in_dim(grads, core, 1, keepdims=False).reshape(half, -1)
    step = width // 2
    weights = [w_qkv[start : start + step] for start in range(0, width, step)]
    received = [shift(dot_nt(theirs, weight).astype(BF16), "core", 1) for weight in weights]
    totals = lax.optimization_barrier([dot_nt(mine, weight) for weight in weights])
    kept, sent = [], []
    for total, other in zip(totals, received):
        total = (total + other.astype(F32)).reshape(2, rows // 4, step)
        sent.append(lax.dynamic_index_in_dim(total, 1 - y_hi, 0, keepdims=False).astype(BF16))
        kept.append(lax.dynamic_index_in_dim(total, y_hi, 0, keepdims=False))

    def token_sums(gathered):
        return call(
            functools.partial(tokens_kernel, nx, nz),
            jax.ShapeDtypeStruct((ny * nz, out_rows, gathered[0].shape[1]), BF16),
            (
                core.astype(jnp.int32).reshape(1), block_order, hidden_own,
                *hidden, hidden_theirs, *gathered,
            ),
            cost=2,
        )

    tokens_q = token_sums(gathered_q)
    tokens_q, gathered_kv, sent = lax.optimization_barrier((tokens_q, gathered_kv, sent))
    grad_in = [keep + shift(send, "y_hi", 1).astype(F32) for keep, send in zip(kept, sent)]
    sums = jnp.concatenate([tokens_q, token_sums(gathered_kv)], axis=-1)
    sums = lax.all_to_all(sums, ("y_lo", "z"), 0, 0, tiled=True)
    grad_w = jnp.sum(sums.astype(F32), axis=0) * float(rows * count) ** (-0.5)
    return jnp.concatenate(grad_in, axis=1).astype(BF16), grad_w.astype(BF16)


def solution(mesh):
    dims = SEQ_DIMS[mesh.shape["seq"]] + (2, 2)
    split = Mesh(np.asarray(mesh.devices).reshape(dims), SEQ + KVH)
    return jax.shard_map(
        shards,
        mesh=split,
        in_specs=(
            P(SEQ, None),
            P(None, KVH),
            P(SEQ, KVH),
            P(SEQ, KVH),
            P(SEQ, KVH),
            P(SEQ, KVH),
            P(),
        ),
        out_specs=(P(SEQ + KVH, None), P(SEQ, KVH)),
        check_vma=False,
    )
```

```python
import functools

import jax
import jax.numpy as jnp
import numpy as np
from jax import lax
from jax.experimental import pallas as pl
from jax.experimental.pallas import tpu as pltpu
from jax.sharding import Mesh
from jax.sharding import PartitionSpec as P

LOG2E = 1.4426950408889634
BF16 = jnp.bfloat16
F32 = jnp.float32
SEQ_DIMS = {64: (4, 2, 8), 16: (2, 2, 4)}
SEQ = ("x", "y_lo", "z")
KVH = ("y_hi", "core")
VMEM_LIMIT = 16 * 1024 * 1024


def shift_seq(value, steps, sources=None):
    count = lax.axis_size(SEQ)
    sources = range(count) if sources is None else [s % count for s in sources]
    return lax.ppermute(value, SEQ, [(s, (s + steps) % count) for s in sources])


def shift(value, axis, steps):
    size = lax.axis_size(axis)
    return lax.ppermute(value, axis, [(s, (s + steps) % size) for s in range(size)])


def dot_nt(a, b):
    return lax.dot_general(a, b, (((1,), (1,)), ((), ())), preferred_element_type=F32)


def dot_nn(a, b):
    return lax.dot_general(a, b, (((1,), (0,)), ((), ())), preferred_element_type=F32)


def dot_tn(a, b):
    return lax.dot_general(a, b, (((0,), (0,)), ((), ())), preferred_element_type=F32)


def low_slot_of(me, order):
    return jnp.where(order[2 * me[0]] == me[0], 0, 1)


def offsets(me, order, half):
    slot = low_slot_of(me, order)
    return pl.multiple_of(slot * half, half), pl.multiple_of((1 - slot) * half, half)


def call(kernel, out_shape, args, scratch=(), cost=1, space=pltpu.VMEM):
    vmem = pl.BlockSpec(memory_space=pltpu.VMEM)
    smem = pl.BlockSpec(memory_space=pltpu.SMEM)
    return pl.pallas_call(
        kernel,
        out_shape=out_shape,
        in_specs=[smem, smem] + [pl.BlockSpec(memory_space=space)] * (len(args) - 2),
        out_specs=jax.tree.map(lambda _: vmem, out_shape),
        scratch_shapes=list(scratch),
        compiler_params=pltpu.CompilerParams(vmem_limit_bytes=VMEM_LIMIT),
        cost_estimate=pl.CostEstimate(flops=0, bytes_accessed=int(cost * 3.5e6), transcendentals=0),
    )(*args)


def split_kernel(me, order, keys, values, low, high, sems):
    half, hd = low.shape[0], keys.shape[1]
    copies = []
    for out, off in zip((low, high), offsets(me, order, half)):
        for n, source in enumerate((keys, values)):
            copies.append(
                pltpu.make_async_copy(
                    source.at[pl.ds(off, half), :],
                    out.at[:, n * hd : (n + 1) * hd],
                    sems.at[len(copies)],
                )
            )
    for copy in copies:
        copy.start()
    for copy in copies:
        copy.wait()


def pair_weights(query, grad, key, value, diagonal, scale):
    weights = jnp.exp2(dot_nt(key, query) * (scale * LOG2E))
    if diagonal:
        rows = lax.broadcasted_iota(jnp.int32, weights.shape, 0)
        cols = lax.broadcasted_iota(jnp.int32, weights.shape, 1)
        weights = jnp.where(rows <= cols, weights, 0.0)
    return weights, dot_nt(value, grad)


def add_stats(q, do, stats, heads, piece, place, off, diagonal):
    half, hd = piece.shape[0], piece.shape[1] // 2
    key, value = piece[:, :hd], piece[:, hd:]
    for j in range(heads):
        cols = slice(j * hd, (j + 1) * hd)
        query, grad = q[pl.ds(off, half), cols], do[pl.ds(off, half), cols]
        weights, grad_prob = pair_weights(query, grad, key, value, diagonal, hd**-0.5)
        stats[0, place, j : j + 1, :] += jnp.sum(weights, axis=0, keepdims=True)
        stats[1, place, j : j + 1, :] += jnp.sum(weights * grad_prob, axis=0, keepdims=True)


def add_grads(q, do, stats, dqt, heads, piece, place, off, diagonal):
    half, hd = piece.shape[0], piece.shape[1] // 2
    key, value = piece[:, :hd], piece[:, hd:]
    grad_key = grad_value = None
    for j in range(heads):
        cols = slice(j * hd, (j + 1) * hd)
        query, grad = q[pl.ds(off, half), cols], do[pl.ds(off, half), cols]
        weights, grad_prob = pair_weights(query, grad, key, value, diagonal, hd**-0.5)
        inverse = 1.0 / stats[0, place, j : j + 1, :]
        delta = stats[1, place, j : j + 1, :] * inverse
        prob = weights * inverse
        grad_score = (prob * (grad_prob - delta) * hd**-0.5).astype(BF16)
        term_key = dot_nn(grad_score, query)
        term_value = dot_nn(prob.astype(BF16), grad)
        grad_key = term_key if j == 0 else grad_key + term_key
        grad_value = term_value if j == 0 else grad_value + term_value
        dqt[place, j] += dot_tn(key, grad_score)
    return grad_key, grad_value


def second_quadrant(me, hop, low, high, picked, lo, hi):
    wraps = me[0] < hop
    picked[...] = low[...]

    @pl.when(wraps)
    def _():
        picked[...] = high[...]

    return wraps, jnp.where(wraps, 1, 0), pl.multiple_of(jnp.where(wraps, hi, lo), lo_size(picked))


def lo_size(ref):
    return ref.shape[0]


def near_stats_kernel(heads, me, order, q, do, low, high, low1, high1, low3, high3, stats, picked):
    lo, hi = offsets(me, order, low.shape[0])
    stats[...] = jnp.zeros_like(stats)
    add_stats(q, do, stats, heads, low, 1, hi, False)
    add_stats(q, do, stats, heads, high, 1, hi, True)
    add_stats(q, do, stats, heads, low, 0, lo, True)
    hop_stats(me, 1, q, do, stats, heads, low1, high1, picked, lo, hi)
    hop_stats(me, 3, q, do, stats, heads, low3, high3, picked, lo, hi)


def hop_stats(me, hop, q, do, stats, heads, low, high, picked, lo, hi):
    add_stats(q, do, stats, heads, low, 1, hi, False)
    _, place, off = second_quadrant(me, hop, low, high, picked, lo, hi)
    add_stats(q, do, stats, heads, picked, place, off, False)


def hop_terms(me, hop, q, do, stats, dqt, heads, low, high, picked, acc, lo, hi, out_low, out_high):
    hd = picked.shape[1] // 2
    acc[0, :, :hd], acc[0, :, hd:] = add_grads(q, do, stats, dqt, heads, low, 1, hi, False)
    wraps, place, off = second_quadrant(me, hop, low, high, picked, lo, hi)
    acc[1, :, :hd], acc[1, :, hd:] = add_grads(q, do, stats, dqt, heads, picked, place, off, False)

    @pl.when(wraps)
    def _():
        out_low[...] = acc[0].astype(out_low.dtype)
        out_high[...] = acc[1].astype(out_low.dtype)

    @pl.when(jnp.logical_not(wraps))
    def _():
        out_low[...] = (acc[0] + acc[1]).astype(out_low.dtype)
        out_high[...] = jnp.zeros_like(out_high)


def far_grads_kernel(
    heads, me, order, q, do, lows, highs, before, stats, dqt, out_lows, out_highs, picked, acc
):
    lo, hi = offsets(me, order, picked.shape[0])
    stats[...] = before[...]
    for n, hop in enumerate((2, 4)):
        hop_stats(me, hop, q, do, stats, heads, lows.at[n], highs.at[n], picked, lo, hi)
    dqt[...] = jnp.zeros_like(dqt)
    for n, hop in enumerate((2, 4)):
        hop_terms(
            me, hop, q, do, stats, dqt, heads, lows.at[n], highs.at[n],
            picked, acc, lo, hi, out_lows.at[n], out_highs.at[n],
        )


def near_grads_kernel(
    heads, me, order, q, do, stats, low3, high3, low1, high1, low, high, before,
    dq, own, term3_low, term3_high, term1_low, term1_high, dqt, picked, acc,
):
    half, hd = low.shape[0], low.shape[1] // 2
    lo, hi = offsets(me, order, half)
    dqt[...] = before[...]
    for hop, *refs, outs in (
        (3, low3, high3, (term3_low, term3_high)), (1, low1, high1, (term1_low, term1_high))
    ):
        hop_terms(me, hop, q, do, stats, dqt, heads, *refs, picked, acc, lo, hi, *outs)
    gk, gv = add_grads(q, do, stats, dqt, heads, low, 1, hi, False)
    gk2, gv2 = add_grads(q, do, stats, dqt, heads, low, 0, lo, True)
    own[0, :, :hd] = gk + gk2
    own[0, :, hd:] = gv + gv2
    own[1, :, :hd], own[1, :, hd:] = add_grads(q, do, stats, dqt, heads, high, 1, hi, True)
    for place, off in ((0, lo), (1, hi)):
        for j in range(heads):
            dq[pl.ds(off, half), j * hd : (j + 1) * hd] = dqt[place, j].T.astype(BF16)


def tokens_kernel(nx, nz, at, order, *refs):
    own, mine, theirs, grads, out = refs[0], refs[1:nx], refs[nx], refs[nx + 1 : -1], refs[-1]
    block = own.shape[1] // nz
    for n in range(2):
        y = at[0] if n == 0 else 1 - at[0]
        total = dot_nn(own[y], grads[0][...])
        for k in range(1, nx):
            piece = mine[k - 1][...] if n == 0 else theirs[k - 1]
            total = total + dot_nn(piece, grads[k][...])
        total = total.astype(BF16)
        for z in range(nz):
            out[y * nz + z] = total[z * block : (z + 1) * block]


def shards(hidden_in, w_qkv, queries, keys, values, d_out, block_order):
    count = lax.axis_size(SEQ)
    nx, ny, nz = (lax.axis_size(axis) for axis in SEQ)
    at_x, at_y = lax.axis_index("x"), lax.axis_index("y_lo")
    core, y_hi = lax.axis_index("core"), lax.axis_index("y_hi")
    index = lax.axis_index(SEQ).astype(jnp.int32)
    me = index.reshape(1)
    rows, width = hidden_in.shape
    half = rows // 2
    hd = keys.shape[1]
    heads = queries.shape[1] // hd
    out_rows = width // count

    piece = jax.ShapeDtypeStruct((half, 2 * hd), BF16)
    stats_shape = jax.ShapeDtypeStruct((2, 2, heads, half), F32)
    partial_q = jax.ShapeDtypeStruct((2, heads, hd, half), F32)
    picked = pltpu.VMEM(piece.shape, BF16)
    acc = pltpu.VMEM((2, half, 2 * hd), F32)

    low, high = call(
        split_kernel, [piece, piece], (me, block_order, keys, values),
        [pltpu.SemaphoreType.DMA((4,))], space=pltpu.HBM,
    )
    low1 = shift_seq(low, 1)
    high1 = shift_seq(high, 1, (-2, -1))
    low3 = shift_seq(low, 3)
    high3 = shift_seq(high, 3, (-4, -3, -2, -1))
    low1, high1, low3, high3 = lax.optimization_barrier((low1, high1, low3, high3))
    pair, pair_high = jnp.stack([low1, low3]), jnp.stack([high1, high3])
    pair, pair_high, hidden_in = lax.optimization_barrier((pair, pair_high, hidden_in))
    low24 = shift_seq(pair, 1)
    high24 = shift_seq(pair_high, 1, (-1, 0, 1, 2))

    hidden_t = lax.optimization_barrier(hidden_in.T)
    base = (me, block_order, queries, d_out)
    stats = call(
        functools.partial(near_stats_kernel, heads), stats_shape,
        (*base, low, high, low1, high1, low3, high3), [picked], cost=5,
    )
    chunks = hidden_t.reshape(nx, ny, nz * out_rows, rows)
    to1, to2, to3 = (
        lax.dynamic_slice(
            chunks, ((at_x + k) % nx, core, 0, 0), (1, 1, *chunks.shape[2:])
        ).reshape(chunks.shape[2:])
        for k in range(1, nx)
    )
    split = to2.shape[0] // 2
    leaving = [jnp.concatenate([to1, to2[:split]]), jnp.concatenate([to3, to2[split:]])]
    low24, high24, stats, leaving = lax.optimization_barrier((low24, high24, stats, leaving))
    up, down = shift(leaving[0], "x", 1), shift(leaving[1], "x", -1)
    two = jax.ShapeDtypeStruct((2, *piece.shape), BF16)
    stats, dqt, out24, out24_high = call(
        functools.partial(far_grads_kernel, heads), [stats_shape, partial_q, two, two],
        (*base, low24, high24, stats), [picked, acc], cost=8,
    )
    back24 = shift_seq(out24, -1)
    back24_high = shift_seq(out24_high, -1, (0, 1, 2, 3))
    term = jax.ShapeDtypeStruct(piece.shape, F32)
    grad_q, own, out3, out3_high, out1, out1_high = call(
        functools.partial(near_grads_kernel, heads),
        [jax.ShapeDtypeStruct(queries.shape, BF16), jax.ShapeDtypeStruct((2, *piece.shape), F32),
         term, term, term, term],
        (*base, stats, low3, high3, low1, high1, low, high, dqt),
        [pltpu.VMEM(partial_q.shape, F32), picked, acc], cost=20,
    )
    grad_q, up, down = lax.optimization_barrier((grad_q, up, down))
    back1 = shift_seq((out1 + back24[0].astype(F32)).astype(BF16), -1)
    back3 = shift_seq((out3 + back24[1].astype(F32)).astype(BF16), -3)
    back1_high = shift_seq((out1_high + back24_high[0].astype(F32)).astype(BF16), -1, (0, -1))
    back3_high = shift_seq((out3_high + back24_high[1].astype(F32)).astype(BF16), -3, (-1, 0, 1, 2))

    def x_gathered(matrix):
        behind, ahead = shift(matrix, "x", 1), shift(matrix, "x", -1)
        far = [shift(behind[:half], "x", 1), shift(ahead[half:], "x", -1)]
        return [matrix, behind, jnp.concatenate(far), ahead]

    gathered_q = x_gathered(grad_q)
    passed = (up[2 * split :], down[2 * split :])
    passed, back1, back1_high, back3, back3_high = lax.optimization_barrier(
        (passed, back1, back1_high, back3, back3_high)
    )
    hidden2 = jnp.concatenate([shift(passed[0], "x", 1), shift(passed[1], "x", -1)])
    hidden = [up[: 2 * split], hidden2, down[: 2 * split]]
    hidden_theirs = shift(jnp.stack(hidden), "core", 1)
    hidden_own = lax.dynamic_index_in_dim(chunks, at_x, 0, keepdims=False)

    low_total = own[0] + back1.astype(F32) + back3.astype(F32)
    high_total = own[1] + back1_high.astype(F32) + back3_high.astype(F32)
    low_total, high_total = low_total.astype(BF16), high_total.astype(BF16)
    grad_kv = jnp.where(
        low_slot_of(me, block_order) == 0,
        jnp.concatenate([low_total, high_total], axis=0),
        jnp.concatenate([high_total, low_total], axis=0),
    )

    grad_kv, gathered_q = lax.optimization_barrier((grad_kv, gathered_q))
    gathered_kv = x_gathered(grad_kv)

    grads = jnp.concatenate([grad_q, grad_kv], axis=1).reshape(2, 2, rows // 4, -1)
    theirs = lax.dynamic_index_in_dim(grads, 1 - core, 1, keepdims=False).reshape(half, -1)
    mine = lax.dynamic_index_in_dim(grads, core, 1, keepdims=False).reshape(half, -1)
    step = width // 2
    weights = [w_qkv[start : start + step] for start in range(0, width, step)]
    received = [shift(dot_nt(theirs, weight).astype(BF16), "core", 1) for weight in weights]
    totals = lax.optimization_barrier([dot_nt(mine, weight) for weight in weights])
    kept, sent = [], []
    for total, other in zip(totals, received):
        total = (total + other.astype(F32)).reshape(2, rows // 4, step)
        sent.append(lax.dynamic_index_in_dim(total, 1 - y_hi, 0, keepdims=False).astype(BF16))
        kept.append(lax.dynamic_index_in_dim(total, y_hi, 0, keepdims=False))

    def token_sums(gathered):
        return call(
            functools.partial(tokens_kernel, nx, nz),
            jax.ShapeDtypeStruct((ny * nz, out_rows, gathered[0].shape[1]), BF16),
            (
                core.astype(jnp.int32).reshape(1), block_order, hidden_own,
                *hidden, hidden_theirs, *gathered,
            ),
            cost=2,
        )

    tokens_q = token_sums(gathered_q)
    tokens_q, gathered_kv, sent = lax.optimization_barrier((tokens_q, gathered_kv, sent))
    grad_in = [keep + shift(send, "y_hi", 1).astype(F32) for keep, send in zip(kept, sent)]
    sums = jnp.concatenate([tokens_q, token_sums(gathered_kv)], axis=-1)
    sums, grad_in[0] = lax.optimization_barrier((sums, grad_in[0]))
    sums = lax.all_to_all(sums, ("y_lo", "z"), 0, 0, tiled=True)
    grad_w = jnp.sum(sums.astype(F32), axis=0) * float(rows * count) ** (-0.5)
    return jnp.concatenate(grad_in, axis=1).astype(BF16), grad_w.astype(BF16)


def solution(mesh):
    dims = SEQ_DIMS[mesh.shape["seq"]] + (2, 2)
    split = Mesh(np.asarray(mesh.devices).reshape(dims), SEQ + KVH)
    return jax.shard_map(
        shards,
        mesh=split,
        in_specs=(
            P(SEQ, None),
            P(None, KVH),
            P(SEQ, KVH),
            P(SEQ, KVH),
            P(SEQ, KVH),
            P(SEQ, KVH),
            P(),
        ),
        out_specs=(P(SEQ + KVH, None), P(SEQ, KVH)),
        check_vma=False,
    )
```

```python
import functools

import jax
import jax.numpy as jnp
import numpy as np
from jax import lax
from jax.experimental import pallas as pl
from jax.experimental.pallas import tpu as pltpu
from jax.sharding import Mesh
from jax.sharding import PartitionSpec as P

LOG2E = 1.4426950408889634
BF16 = jnp.bfloat16
F32 = jnp.float32
SEQ_DIMS = {64: (4, 2, 8), 16: (2, 2, 4)}
SEQ = ("x", "y_lo", "z")
KVH = ("y_hi", "core")
VMEM_LIMIT = 10 * 1024 * 1024


def shift_seq(value, steps, sources=None):
    count = lax.axis_size(SEQ)
    sources = range(count) if sources is None else [s % count for s in sources]
    return lax.ppermute(value, SEQ, [(s, (s + steps) % count) for s in sources])


def shift(value, axis, steps):
    size = lax.axis_size(axis)
    return lax.ppermute(value, axis, [(s, (s + steps) % size) for s in range(size)])


def dot_nt(a, b):
    return lax.dot_general(a, b, (((1,), (1,)), ((), ())), preferred_element_type=F32)


def dot_nn(a, b):
    return lax.dot_general(a, b, (((1,), (0,)), ((), ())), preferred_element_type=F32)


def dot_tn(a, b):
    return lax.dot_general(a, b, (((0,), (0,)), ((), ())), preferred_element_type=F32)


def low_slot_of(me, order):
    return jnp.where(order[2 * me[0]] == me[0], 0, 1)


def offsets(me, order, half):
    slot = low_slot_of(me, order)
    return pl.multiple_of(slot * half, half), pl.multiple_of((1 - slot) * half, half)


def call(kernel, out_shape, args, scratch=(), cost=1, space=pltpu.VMEM):
    vmem = pl.BlockSpec(memory_space=pltpu.VMEM)
    smem = pl.BlockSpec(memory_space=pltpu.SMEM)
    return pl.pallas_call(
        kernel,
        out_shape=out_shape,
        in_specs=[smem, smem] + [pl.BlockSpec(memory_space=space)] * (len(args) - 2),
        out_specs=jax.tree.map(lambda _: vmem, out_shape),
        scratch_shapes=list(scratch),
        compiler_params=pltpu.CompilerParams(vmem_limit_bytes=VMEM_LIMIT),
        cost_estimate=pl.CostEstimate(flops=0, bytes_accessed=int(cost * 3.5e6), transcendentals=0),
    )(*args)


def split_kernel(me, order, keys, values, low, high, sems):
    half, hd = low.shape[0], keys.shape[1]
    copies = []
    for out, off in zip((low, high), offsets(me, order, half)):
        for n, source in enumerate((keys, values)):
            copies.append(
                pltpu.make_async_copy(
                    source.at[pl.ds(off, half), :],
                    out.at[:, n * hd : (n + 1) * hd],
                    sems.at[len(copies)],
                )
            )
    for copy in copies:
        copy.start()
    for copy in copies:
        copy.wait()


def pair_weights(query, grad, key, value, diagonal, scale):
    weights = jnp.exp2(dot_nt(key, query) * (scale * LOG2E))
    if diagonal:
        rows = lax.broadcasted_iota(jnp.int32, weights.shape, 0)
        cols = lax.broadcasted_iota(jnp.int32, weights.shape, 1)
        weights = jnp.where(rows <= cols, weights, 0.0)
    return weights, dot_nt(value, grad)


def add_stats(q, do, stats, heads, piece, place, off, diagonal):
    half, hd = piece.shape[0], piece.shape[1] // 2
    key, value = piece[:, :hd], piece[:, hd:]
    for j in range(heads):
        cols = slice(j * hd, (j + 1) * hd)
        query, grad = q[pl.ds(off, half), cols], do[pl.ds(off, half), cols]
        weights, grad_prob = pair_weights(query, grad, key, value, diagonal, hd**-0.5)
        stats[0, place, j : j + 1, :] += jnp.sum(weights, axis=0, keepdims=True)
        stats[1, place, j : j + 1, :] += jnp.sum(weights * grad_prob, axis=0, keepdims=True)


def add_grads(q, do, stats, dqt, heads, piece, place, off, diagonal):
    half, hd = piece.shape[0], piece.shape[1] // 2
    key, value = piece[:, :hd], piece[:, hd:]
    grad_key = grad_value = None
    for j in range(heads):
        cols = slice(j * hd, (j + 1) * hd)
        query, grad = q[pl.ds(off, half), cols], do[pl.ds(off, half), cols]
        weights, grad_prob = pair_weights(query, grad, key, value, diagonal, hd**-0.5)
        inverse = 1.0 / stats[0, place, j : j + 1, :]
        delta = stats[1, place, j : j + 1, :] * inverse
        prob = weights * inverse
        grad_score = (prob * (grad_prob - delta) * hd**-0.5).astype(BF16)
        term_key = dot_nn(grad_score, query)
        term_value = dot_nn(prob.astype(BF16), grad)
        grad_key = term_key if j == 0 else grad_key + term_key
        grad_value = term_value if j == 0 else grad_value + term_value
        dqt[place, j] += dot_tn(key, grad_score)
    return grad_key, grad_value


def second_quadrant(me, hop, low, high, picked, lo, hi):
    wraps = me[0] < hop
    picked[...] = low[...]

    @pl.when(wraps)
    def _():
        picked[...] = high[...]

    return wraps, jnp.where(wraps, 1, 0), pl.multiple_of(jnp.where(wraps, hi, lo), lo_size(picked))


def lo_size(ref):
    return ref.shape[0]


def near_stats_kernel(heads, me, order, q, do, low, high, low1, high1, low3, high3, stats, picked):
    lo, hi = offsets(me, order, low.shape[0])
    stats[...] = jnp.zeros_like(stats)
    add_stats(q, do, stats, heads, low, 1, hi, False)
    add_stats(q, do, stats, heads, high, 1, hi, True)
    add_stats(q, do, stats, heads, low, 0, lo, True)
    hop_stats(me, 1, q, do, stats, heads, low1, high1, picked, lo, hi)
    hop_stats(me, 3, q, do, stats, heads, low3, high3, picked, lo, hi)


def hop_stats(me, hop, q, do, stats, heads, low, high, picked, lo, hi):
    add_stats(q, do, stats, heads, low, 1, hi, False)
    _, place, off = second_quadrant(me, hop, low, high, picked, lo, hi)
    add_stats(q, do, stats, heads, picked, place, off, False)


def hop_terms(me, hop, q, do, stats, dqt, heads, low, high, picked, acc, lo, hi, out_low, out_high):
    hd = picked.shape[1] // 2
    acc[0, :, :hd], acc[0, :, hd:] = add_grads(q, do, stats, dqt, heads, low, 1, hi, False)
    wraps, place, off = second_quadrant(me, hop, low, high, picked, lo, hi)
    acc[1, :, :hd], acc[1, :, hd:] = add_grads(q, do, stats, dqt, heads, picked, place, off, False)

    @pl.when(wraps)
    def _():
        out_low[...] = acc[0].astype(out_low.dtype)
        out_high[...] = acc[1].astype(out_low.dtype)

    @pl.when(jnp.logical_not(wraps))
    def _():
        out_low[...] = (acc[0] + acc[1]).astype(out_low.dtype)
        out_high[...] = jnp.zeros_like(out_high)


def far_grads_kernel(
    heads, me, order, q, do, lows, highs, before, stats, dqt, out_lows, out_highs, picked, acc
):
    lo, hi = offsets(me, order, picked.shape[0])
    stats[...] = before[...]
    for n, hop in enumerate((2, 4)):
        hop_stats(me, hop, q, do, stats, heads, lows.at[n], highs.at[n], picked, lo, hi)
    dqt[...] = jnp.zeros_like(dqt)
    for n, hop in enumerate((2, 4)):
        hop_terms(
            me, hop, q, do, stats, dqt, heads, lows.at[n], highs.at[n],
            picked, acc, lo, hi, out_lows.at[n], out_highs.at[n],
        )


def near_grads_kernel(
    heads, me, order, q, do, stats, low3, high3, low1, high1, low, high, before,
    dq, own, term3_low, term3_high, term1_low, term1_high, dqt, picked, acc,
):
    half, hd = low.shape[0], low.shape[1] // 2
    lo, hi = offsets(me, order, half)
    dqt[...] = before[...]
    for hop, *refs, outs in (
        (3, low3, high3, (term3_low, term3_high)), (1, low1, high1, (term1_low, term1_high))
    ):
        hop_terms(me, hop, q, do, stats, dqt, heads, *refs, picked, acc, lo, hi, *outs)
    gk, gv = add_grads(q, do, stats, dqt, heads, low, 1, hi, False)
    gk2, gv2 = add_grads(q, do, stats, dqt, heads, low, 0, lo, True)
    own[0, :, :hd] = gk + gk2
    own[0, :, hd:] = gv + gv2
    own[1, :, :hd], own[1, :, hd:] = add_grads(q, do, stats, dqt, heads, high, 1, hi, True)
    for place, off in ((0, lo), (1, hi)):
        for j in range(heads):
            dq[pl.ds(off, half), j * hd : (j + 1) * hd] = dqt[place, j].T.astype(BF16)


def tokens_kernel(nz, at, order, own, up, far_up, far_down, down, theirs, *refs):
    grad, behind, grad_far_up, grad_far_down, ahead, out = refs
    rows = own.shape[1]
    block = rows // nz
    grads_far = jnp.concatenate([grad_far_up[...], grad_far_down[...]], axis=0)
    for n in range(2):
        if n == 0:
            y = at[0]
            far = jnp.concatenate([far_up[...], far_down[...]], axis=0)
            pieces = (up[:rows], far, down[:rows])
        else:
            y = 1 - at[0]
            pieces = tuple(theirs[k * rows : (k + 1) * rows] for k in range(3))
        total = dot_nn(own[y], grad[...])
        for piece, grads in zip(pieces, (behind[...], grads_far, ahead[...])):
            total = total + dot_nn(piece, grads)
        total = total.astype(BF16)
        for z in range(nz):
            out[y * nz + z] = total[z * block : (z + 1) * block]


def shards(hidden_in, w_qkv, queries, keys, values, d_out, block_order):
    count = lax.axis_size(SEQ)
    nx, ny, nz = (lax.axis_size(axis) for axis in SEQ)
    at_x, at_y = lax.axis_index("x"), lax.axis_index("y_lo")
    core, y_hi = lax.axis_index("core"), lax.axis_index("y_hi")
    index = lax.axis_index(SEQ).astype(jnp.int32)
    me = index.reshape(1)
    rows, width = hidden_in.shape
    half = rows // 2
    hd = keys.shape[1]
    heads = queries.shape[1] // hd
    out_rows = width // count

    piece = jax.ShapeDtypeStruct((half, 2 * hd), BF16)
    stats_shape = jax.ShapeDtypeStruct((2, 2, heads, half), F32)
    partial_q = jax.ShapeDtypeStruct((2, heads, hd, half), F32)
    picked = pltpu.VMEM(piece.shape, BF16)
    acc = pltpu.VMEM((2, half, 2 * hd), F32)

    low, high = call(
        split_kernel, [piece, piece], (me, block_order, keys, values),
        [pltpu.SemaphoreType.DMA((4,))], space=pltpu.HBM,
    )
    low1 = shift_seq(low, 1)
    high1 = shift_seq(high, 1, (-2, -1))
    low3 = shift_seq(low, 3)
    high3 = shift_seq(high, 3, (-4, -3, -2, -1))

    chunks = hidden_in.T.reshape(nx, ny, nz * out_rows, rows)
    to1, to2, to3 = (
        lax.dynamic_slice(
            chunks, ((at_x + k) % nx, core, 0, 0), (1, 1, *chunks.shape[2:])
        ).reshape(chunks.shape[2:])
        for k in range(1, nx)
    )
    split = to2.shape[0] // 2
    leaving = [jnp.concatenate([to1, to2[:split]]), jnp.concatenate([to3, to2[split:]])]
    hidden_own = lax.dynamic_index_in_dim(chunks, at_x, 0, keepdims=False)
    low1, high1, low3, high3, leaving, hidden_own = lax.optimization_barrier(
        (low1, high1, low3, high3, leaving, hidden_own)
    )
    low24 = shift_seq(jnp.stack([low1, low3]), 1)
    high24 = shift_seq(jnp.stack([high1, high3]), 1, (-1, 0, 1, 2))

    base = (me, block_order, queries, d_out)
    stats = call(
        functools.partial(near_stats_kernel, heads), stats_shape,
        (*base, low, high, low1, high1, low3, high3), [picked], cost=5,
    )
    low24, high24, stats, leaving = lax.optimization_barrier((low24, high24, stats, leaving))
    up, down = shift(leaving[0], "x", 1), shift(leaving[1], "x", -1)
    two = jax.ShapeDtypeStruct((2, *piece.shape), BF16)
    stats, dqt, out24, out24_high = call(
        functools.partial(far_grads_kernel, heads), [stats_shape, partial_q, two, two],
        (*base, low24, high24, stats), [picked, acc], cost=8,
    )
    back24 = shift_seq(out24, -1)
    back24_high = shift_seq(out24_high, -1, (0, 1, 2, 3))
    term = jax.ShapeDtypeStruct(piece.shape, F32)
    grad_q, own, out3, out3_high, out1, out1_high = call(
        functools.partial(near_grads_kernel, heads),
        [jax.ShapeDtypeStruct(queries.shape, BF16), jax.ShapeDtypeStruct((2, *piece.shape), F32),
         term, term, term, term],
        (*base, stats, low3, high3, low1, high1, low, high, dqt),
        [pltpu.VMEM(partial_q.shape, F32), picked, acc], cost=20,
    )
    grad_q, up, down = lax.optimization_barrier((grad_q, up, down))
    back1 = shift_seq((out1 + back24[0].astype(F32)).astype(BF16), -1)
    back3 = shift_seq((out3 + back24[1].astype(F32)).astype(BF16), -3)
    back1_high = shift_seq((out1_high + back24_high[0].astype(F32)).astype(BF16), -1, (0, -1))
    back3_high = shift_seq((out3_high + back24_high[1].astype(F32)).astype(BF16), -3, (-1, 0, 1, 2))

    def neighbours(matrix):
        return matrix, shift(matrix, "x", 1), shift(matrix, "x", -1)

    def x_gathered(matrix, behind, ahead):
        return matrix, behind, shift(behind[:half], "x", 1), shift(ahead[half:], "x", -1), ahead

    gathered_q = neighbours(grad_q)
    passed = (up[2 * split :], down[2 * split :])
    passed, back1, back1_high, back3, back3_high, gathered_q = lax.optimization_barrier(
        (passed, back1, back1_high, back3, back3_high, gathered_q)
    )
    far_up, far_down = shift(passed[0], "x", 1), shift(passed[1], "x", -1)
    hidden_theirs = shift(
        jnp.concatenate([up[: 2 * split], far_up, far_down, down[: 2 * split]]), "core", 1
    )

    def token_sums(gathered):
        return call(
            functools.partial(tokens_kernel, nz),
            jax.ShapeDtypeStruct((ny * nz, out_rows, gathered[0].shape[1]), BF16),
            (
                core.astype(jnp.int32).reshape(1), block_order, hidden_own,
                up, far_up, far_down, down, hidden_theirs, *gathered,
            ),
            cost=2,
        )

    tokens_q = token_sums(x_gathered(*gathered_q))

    low_total = own[0] + back1.astype(F32) + back3.astype(F32)
    high_total = own[1] + back1_high.astype(F32) + back3_high.astype(F32)
    low_total, high_total = low_total.astype(BF16), high_total.astype(BF16)
    grad_kv = jnp.where(
        low_slot_of(me, block_order) == 0,
        jnp.concatenate([low_total, high_total], axis=0),
        jnp.concatenate([high_total, low_total], axis=0),
    )

    grad_kv, tokens_q = lax.optimization_barrier((grad_kv, tokens_q))
    gathered_kv = x_gathered(*neighbours(grad_kv))

    grads = jnp.concatenate([grad_q, grad_kv], axis=1).reshape(2, 2, rows // 4, -1)
    theirs = lax.dynamic_index_in_dim(grads, 1 - core, 1, keepdims=False).reshape(half, -1)
    mine = lax.dynamic_index_in_dim(grads, core, 1, keepdims=False).reshape(half, -1)
    step = width // 2
    weights = [w_qkv[start : start + step] for start in range(0, width, step)]
    received = [shift(dot_nt(theirs, weight).astype(BF16), "core", 1) for weight in weights]
    totals = lax.optimization_barrier([dot_nt(mine, weight) for weight in weights])
    kept, sent = [], []
    for total, other in zip(totals, received):
        total = (total + other.astype(F32)).reshape(2, rows // 4, step)
        sent.append(lax.dynamic_index_in_dim(total, 1 - y_hi, 0, keepdims=False).astype(BF16))
        kept.append(lax.dynamic_index_in_dim(total, y_hi, 0, keepdims=False))

    grad_in = [keep + shift(send, "y_hi", 1).astype(F32) for keep, send in zip(kept, sent)]
    sums_q = lax.all_to_all(tokens_q, ("y_lo", "z"), 0, 0, tiled=True)
    tokens_kv, grad_in[0], sums_q = lax.optimization_barrier(
        (token_sums(gathered_kv), grad_in[0], sums_q)
    )
    sums_kv = lax.all_to_all(tokens_kv, ("y_lo", "z"), 0, 0, tiled=True)
    sums = [jnp.sum(part.astype(F32), axis=0) for part in (sums_q, sums_kv)]
    grad_w = jnp.concatenate(sums, axis=-1) * float(rows * count) ** (-0.5)
    return jnp.concatenate(grad_in, axis=1).astype(BF16), grad_w.astype(BF16)


def solution(mesh):
    dims = SEQ_DIMS[mesh.shape["seq"]] + (2, 2)
    split = Mesh(np.asarray(mesh.devices).reshape(dims), SEQ + KVH)
    return jax.shard_map(
        shards,
        mesh=split,
        in_specs=(
            P(SEQ, None),
            P(None, KVH),
            P(SEQ, KVH),
            P(SEQ, KVH),
            P(SEQ, KVH),
            P(SEQ, KVH),
            P(),
        ),
        out_specs=(P(SEQ + KVH, None), P(SEQ, KVH)),
        check_vma=False,
    )
```

```python
import functools

import jax
import jax.numpy as jnp
import numpy as np
from jax import lax
from jax.experimental import pallas as pl
from jax.experimental.pallas import tpu as pltpu
from jax.sharding import Mesh
from jax.sharding import PartitionSpec as P

LOG2E = 1.4426950408889634
BF16 = jnp.bfloat16
F32 = jnp.float32
SEQ_DIMS = {64: (4, 2, 8), 16: (2, 2, 4)}
SEQ = ("x", "y_lo", "z")
KVH = ("y_hi", "core")
VMEM_LIMIT = 10 * 1024 * 1024


def shift_seq(value, steps, sources=None):
    count = lax.axis_size(SEQ)
    sources = range(count) if sources is None else [s % count for s in sources]
    return lax.ppermute(value, SEQ, [(s, (s + steps) % count) for s in sources])


def shift(value, axis, steps):
    size = lax.axis_size(axis)
    return lax.ppermute(value, axis, [(s, (s + steps) % size) for s in range(size)])


def dot_nt(a, b):
    return lax.dot_general(a, b, (((1,), (1,)), ((), ())), preferred_element_type=F32)


def dot_nn(a, b):
    return lax.dot_general(a, b, (((1,), (0,)), ((), ())), preferred_element_type=F32)


def dot_tn(a, b):
    return lax.dot_general(a, b, (((0,), (0,)), ((), ())), preferred_element_type=F32)


def low_slot_of(me, order):
    return jnp.where(order[2 * me[0]] == me[0], 0, 1)


def offsets(me, order, half):
    slot = low_slot_of(me, order)
    return pl.multiple_of(slot * half, half), pl.multiple_of((1 - slot) * half, half)


def call(kernel, out_shape, args, scratch=(), cost=1, space=pltpu.VMEM):
    vmem = pl.BlockSpec(memory_space=pltpu.VMEM)
    smem = pl.BlockSpec(memory_space=pltpu.SMEM)
    return pl.pallas_call(
        kernel,
        out_shape=out_shape,
        in_specs=[smem, smem] + [pl.BlockSpec(memory_space=space)] * (len(args) - 2),
        out_specs=jax.tree.map(lambda _: vmem, out_shape),
        scratch_shapes=list(scratch),
        compiler_params=pltpu.CompilerParams(vmem_limit_bytes=VMEM_LIMIT),
        cost_estimate=pl.CostEstimate(flops=0, bytes_accessed=int(cost * 3.5e6), transcendentals=0),
    )(*args)


def split_kernel(me, order, keys, values, low, high, sems):
    half, hd = low.shape[0], keys.shape[1]
    copies = []
    for out, off in zip((low, high), offsets(me, order, half)):
        for n, source in enumerate((keys, values)):
            copies.append(
                pltpu.make_async_copy(
                    source.at[pl.ds(off, half), :],
                    out.at[:, n * hd : (n + 1) * hd],
                    sems.at[len(copies)],
                )
            )
    for copy in copies:
        copy.start()
    for copy in copies:
        copy.wait()


def pair_weights(query, grad, key, value, diagonal, scale):
    weights = jnp.exp2(dot_nt(key, query) * (scale * LOG2E))
    if diagonal:
        rows = lax.broadcasted_iota(jnp.int32, weights.shape, 0)
        cols = lax.broadcasted_iota(jnp.int32, weights.shape, 1)
        weights = jnp.where(rows <= cols, weights, 0.0)
    return weights, dot_nt(value, grad)


def add_stats(q, do, stats, heads, piece, place, off, diagonal):
    half, hd = piece.shape[0], piece.shape[1] // 2
    key, value = piece[:, :hd], piece[:, hd:]
    for j in range(heads):
        cols = slice(j * hd, (j + 1) * hd)
        query, grad = q[pl.ds(off, half), cols], do[pl.ds(off, half), cols]
        weights, grad_prob = pair_weights(query, grad, key, value, diagonal, hd**-0.5)
        stats[0, place, j : j + 1, :] += jnp.sum(weights, axis=0, keepdims=True)
        stats[1, place, j : j + 1, :] += jnp.sum(weights * grad_prob, axis=0, keepdims=True)


def add_grads(q, do, stats, dqt, heads, piece, place, off, diagonal):
    half, hd = piece.shape[0], piece.shape[1] // 2
    key, value = piece[:, :hd], piece[:, hd:]
    grad_key = grad_value = None
    for j in range(heads):
        cols = slice(j * hd, (j + 1) * hd)
        query, grad = q[pl.ds(off, half), cols], do[pl.ds(off, half), cols]
        weights, grad_prob = pair_weights(query, grad, key, value, diagonal, hd**-0.5)
        inverse = 1.0 / stats[0, place, j : j + 1, :]
        delta = stats[1, place, j : j + 1, :] * inverse
        prob = weights * inverse
        grad_score = (prob * (grad_prob - delta) * hd**-0.5).astype(BF16)
        term_key = dot_nn(grad_score, query)
        term_value = dot_nn(prob.astype(BF16), grad)
        grad_key = term_key if j == 0 else grad_key + term_key
        grad_value = term_value if j == 0 else grad_value + term_value
        dqt[place, j] += dot_tn(key, grad_score)
    return grad_key, grad_value


def second_quadrant(me, hop, low, high, picked, lo, hi):
    wraps = me[0] < hop
    picked[...] = low[...]

    @pl.when(wraps)
    def _():
        picked[...] = high[...]

    return wraps, jnp.where(wraps, 1, 0), pl.multiple_of(jnp.where(wraps, hi, lo), lo_size(picked))


def lo_size(ref):
    return ref.shape[0]


def near_stats_kernel(heads, me, order, q, do, low, high, low1, high1, low3, high3, stats, picked):
    lo, hi = offsets(me, order, low.shape[0])
    stats[...] = jnp.zeros_like(stats)
    add_stats(q, do, stats, heads, low, 1, hi, False)
    add_stats(q, do, stats, heads, high, 1, hi, True)
    add_stats(q, do, stats, heads, low, 0, lo, True)
    hop_stats(me, 1, q, do, stats, heads, low1, high1, picked, lo, hi)
    hop_stats(me, 3, q, do, stats, heads, low3, high3, picked, lo, hi)


def hop_stats(me, hop, q, do, stats, heads, low, high, picked, lo, hi):
    add_stats(q, do, stats, heads, low, 1, hi, False)
    _, place, off = second_quadrant(me, hop, low, high, picked, lo, hi)
    add_stats(q, do, stats, heads, picked, place, off, False)


def hop_terms(me, hop, q, do, stats, dqt, heads, low, high, picked, acc, lo, hi, out_low, out_high):
    hd = picked.shape[1] // 2
    acc[0, :, :hd], acc[0, :, hd:] = add_grads(q, do, stats, dqt, heads, low, 1, hi, False)
    wraps, place, off = second_quadrant(me, hop, low, high, picked, lo, hi)
    acc[1, :, :hd], acc[1, :, hd:] = add_grads(q, do, stats, dqt, heads, picked, place, off, False)

    @pl.when(wraps)
    def _():
        out_low[...] = acc[0].astype(out_low.dtype)
        out_high[...] = acc[1].astype(out_low.dtype)

    @pl.when(jnp.logical_not(wraps))
    def _():
        out_low[...] = (acc[0] + acc[1]).astype(out_low.dtype)
        out_high[...] = jnp.zeros_like(out_high)


def far_grads_kernel(
    heads, me, order, q, do, lows, highs, before, stats, dqt, out_lows, out_highs, picked, acc
):
    lo, hi = offsets(me, order, picked.shape[0])
    stats[...] = before[...]
    for n, hop in enumerate((2, 4)):
        hop_stats(me, hop, q, do, stats, heads, lows.at[n], highs.at[n], picked, lo, hi)
    dqt[...] = jnp.zeros_like(dqt)
    for n, hop in enumerate((2, 4)):
        hop_terms(
            me, hop, q, do, stats, dqt, heads, lows.at[n], highs.at[n],
            picked, acc, lo, hi, out_lows.at[n], out_highs.at[n],
        )


def near_grads_kernel(
    heads, me, order, q, do, stats, low3, high3, low1, high1, low, high, before,
    dq, own, term3_low, term3_high, term1_low, term1_high, dqt, picked, acc,
):
    half, hd = low.shape[0], low.shape[1] // 2
    lo, hi = offsets(me, order, half)
    dqt[...] = before[...]
    for hop, *refs, outs in (
        (3, low3, high3, (term3_low, term3_high)), (1, low1, high1, (term1_low, term1_high))
    ):
        hop_terms(me, hop, q, do, stats, dqt, heads, *refs, picked, acc, lo, hi, *outs)
    gk, gv = add_grads(q, do, stats, dqt, heads, low, 1, hi, False)
    gk2, gv2 = add_grads(q, do, stats, dqt, heads, low, 0, lo, True)
    own[0, :, :hd] = gk + gk2
    own[0, :, hd:] = gv + gv2
    own[1, :, :hd], own[1, :, hd:] = add_grads(q, do, stats, dqt, heads, high, 1, hi, True)
    for place, off in ((0, lo), (1, hi)):
        for j in range(heads):
            dq[pl.ds(off, half), j * hd : (j + 1) * hd] = dqt[place, j].T.astype(BF16)


def tokens_kernel(nz, at, order, own, up, far_up, far_down, down, theirs, *refs):
    grad, behind, grad_far_up, grad_far_down, ahead, out = refs
    rows = own.shape[1]
    block = rows // nz
    grads_far = jnp.concatenate([grad_far_up[...], grad_far_down[...]], axis=0)
    for n in range(2):
        if n == 0:
            y = at[0]
            far = jnp.concatenate([far_up[...], far_down[...]], axis=0)
            pieces = (up[:rows], far, down[:rows])
        else:
            y = 1 - at[0]
            pieces = tuple(theirs[k * rows : (k + 1) * rows] for k in range(3))
        total = dot_nn(own[y], grad[...])
        for piece, grads in zip(pieces, (behind[...], grads_far, ahead[...])):
            total = total + dot_nn(piece, grads)
        total = total.astype(BF16)
        for z in range(nz):
            out[y * nz + z] = total[z * block : (z + 1) * block]


def shards(hidden_in, w_qkv, queries, keys, values, d_out, block_order):
    count = lax.axis_size(SEQ)
    nx, ny, nz = (lax.axis_size(axis) for axis in SEQ)
    at_x, at_y = lax.axis_index("x"), lax.axis_index("y_lo")
    core, y_hi = lax.axis_index("core"), lax.axis_index("y_hi")
    index = lax.axis_index(SEQ).astype(jnp.int32)
    me = index.reshape(1)
    rows, width = hidden_in.shape
    half = rows // 2
    hd = keys.shape[1]
    heads = queries.shape[1] // hd
    out_rows = width // count

    piece = jax.ShapeDtypeStruct((half, 2 * hd), BF16)
    stats_shape = jax.ShapeDtypeStruct((2, 2, heads, half), F32)
    partial_q = jax.ShapeDtypeStruct((2, heads, hd, half), F32)
    picked = pltpu.VMEM(piece.shape, BF16)
    acc = pltpu.VMEM((2, half, 2 * hd), F32)

    low, high = call(
        split_kernel, [piece, piece], (me, block_order, keys, values),
        [pltpu.SemaphoreType.DMA((4,))], space=pltpu.HBM,
    )
    low1 = shift_seq(low, 1)
    high1 = shift_seq(high, 1, (-2, -1))
    low3 = shift_seq(low, 3)
    high3 = shift_seq(high, 3, (-4, -3, -2, -1))

    chunks = hidden_in.T.reshape(nx, ny, nz * out_rows, rows)
    to1, to2, to3 = (
        lax.dynamic_slice(
            chunks, ((at_x + k) % nx, core, 0, 0), (1, 1, *chunks.shape[2:])
        ).reshape(chunks.shape[2:])
        for k in range(1, nx)
    )
    split = to2.shape[0] // 2
    leaving = [jnp.concatenate([to1, to2[:split]]), jnp.concatenate([to3, to2[split:]])]
    hidden_own = lax.dynamic_index_in_dim(chunks, at_x, 0, keepdims=False)
    low1, high1, low3, high3, leaving, hidden_own = lax.optimization_barrier(
        (low1, high1, low3, high3, leaving, hidden_own)
    )
    low24 = shift_seq(jnp.stack([low1, low3]), 1)
    high24 = shift_seq(jnp.stack([high1, high3]), 1, (-1, 0, 1, 2))

    base = (me, block_order, queries, d_out)
    stats = call(
        functools.partial(near_stats_kernel, heads), stats_shape,
        (*base, low, high, low1, high1, low3, high3), [picked], cost=5,
    )
    low24, high24, stats, leaving = lax.optimization_barrier((low24, high24, stats, leaving))
    up, down = shift(leaving[0], "x", 1), shift(leaving[1], "x", -1)
    two = jax.ShapeDtypeStruct((2, *piece.shape), BF16)
    stats, dqt, out24, out24_high = call(
        functools.partial(far_grads_kernel, heads), [stats_shape, partial_q, two, two],
        (*base, low24, high24, stats), [picked, acc], cost=8,
    )
    back24 = shift_seq(out24, -1)
    back24_high = shift_seq(out24_high, -1, (0, 1, 2, 3))
    term = jax.ShapeDtypeStruct(piece.shape, F32)
    grad_q, own, out3, out3_high, out1, out1_high = call(
        functools.partial(near_grads_kernel, heads),
        [jax.ShapeDtypeStruct(queries.shape, BF16), jax.ShapeDtypeStruct((2, *piece.shape), F32),
         term, term, term, term],
        (*base, stats, low3, high3, low1, high1, low, high, dqt),
        [pltpu.VMEM(partial_q.shape, F32), picked, acc], cost=20,
    )
    grad_q, up, down, back24, back24_high = lax.optimization_barrier(
        (grad_q, up, down, back24, back24_high)
    )
    back1 = shift_seq((out1 + back24[0].astype(F32)).astype(BF16), -1)
    back3 = shift_seq((out3 + back24[1].astype(F32)).astype(BF16), -3)
    back1_high = shift_seq((out1_high + back24_high[0].astype(F32)).astype(BF16), -1, (0, -1))
    back3_high = shift_seq((out3_high + back24_high[1].astype(F32)).astype(BF16), -3, (-1, 0, 1, 2))

    def neighbours(matrix):
        return matrix, shift(matrix, "x", 1), shift(matrix, "x", -1)

    def x_gathered(matrix, behind, ahead):
        return matrix, behind, shift(behind[:half], "x", 1), shift(ahead[half:], "x", -1), ahead

    def pinned(value, *others):
        return lax.optimization_barrier((value, others))[0]

    near_q = neighbours(grad_q)
    gathered_q = x_gathered(*pinned(near_q, back1, back3))
    passed = (up[2 * split :], down[2 * split :])
    passed = pinned(passed, gathered_q, back1, back1_high, back3, back3_high)
    far_up, far_down = shift(passed[0], "x", 1), shift(passed[1], "x", -1)
    hidden_theirs = shift(
        jnp.concatenate([up[: 2 * split], far_up, far_down, down[: 2 * split]]), "core", 1
    )

    def token_sums(gathered):
        return call(
            functools.partial(tokens_kernel, nz),
            jax.ShapeDtypeStruct((ny * nz, out_rows, gathered[0].shape[1]), BF16),
            (
                core.astype(jnp.int32).reshape(1), block_order, hidden_own,
                up, far_up, far_down, down, hidden_theirs, *gathered,
            ),
            cost=2,
        )

    tokens_q = token_sums(gathered_q)

    low_total = own[0] + back1.astype(F32) + back3.astype(F32)
    high_total = own[1] + back1_high.astype(F32) + back3_high.astype(F32)
    low_total, high_total = low_total.astype(BF16), high_total.astype(BF16)
    grad_kv = jnp.where(
        low_slot_of(me, block_order) == 0,
        jnp.concatenate([low_total, high_total], axis=0),
        jnp.concatenate([high_total, low_total], axis=0),
    )

    near_kv = neighbours(pinned(grad_kv, gathered_q))
    gathered_kv = x_gathered(*near_kv)
    grad_kv = pinned(grad_kv, near_kv, tokens_q)

    grads = jnp.concatenate([grad_q, grad_kv], axis=1).reshape(2, 2, rows // 4, -1)
    theirs = lax.dynamic_index_in_dim(grads, 1 - core, 1, keepdims=False).reshape(half, -1)
    mine = lax.dynamic_index_in_dim(grads, core, 1, keepdims=False).reshape(half, -1)
    first = width // 4
    weights = [w_qkv[:first], w_qkv[first:]]
    received = [shift(dot_nt(theirs, weight).astype(BF16), "core", 1) for weight in weights]
    totals = lax.optimization_barrier([dot_nt(mine, weight) for weight in weights])
    kept, sent = [], []
    for total, other in zip(totals, received):
        total = (total + other.astype(F32)).reshape(2, rows // 4, -1)
        sent.append(lax.dynamic_index_in_dim(total, 1 - y_hi, 0, keepdims=False).astype(BF16))
        kept.append(lax.dynamic_index_in_dim(total, y_hi, 0, keepdims=False))

    grad_in = [keep + shift(send, "y_hi", 1).astype(F32) for keep, send in zip(kept, sent)]
    sums_q = lax.all_to_all(tokens_q, ("y_lo", "z"), 0, 0, tiled=True)
    tokens_kv, grad_in[0], sums_q = lax.optimization_barrier(
        (token_sums(gathered_kv), grad_in[0], sums_q)
    )
    sums_kv = lax.all_to_all(tokens_kv, ("y_lo", "z"), 0, 0, tiled=True)
    sums = [jnp.sum(part.astype(F32), axis=0) for part in (sums_q, sums_kv)]
    grad_w = jnp.concatenate(sums, axis=-1) * float(rows * count) ** (-0.5)
    return jnp.concatenate(grad_in, axis=1).astype(BF16), grad_w.astype(BF16)


def solution(mesh):
    dims = SEQ_DIMS[mesh.shape["seq"]] + (2, 2)
    split = Mesh(np.asarray(mesh.devices).reshape(dims), SEQ + KVH)
    return jax.shard_map(
        shards,
        mesh=split,
        in_specs=(
            P(SEQ, None),
            P(None, KVH),
            P(SEQ, KVH),
            P(SEQ, KVH),
            P(SEQ, KVH),
            P(SEQ, KVH),
            P(),
        ),
        out_specs=(P(SEQ + KVH, None), P(SEQ, KVH)),
        check_vma=False,
    )
```

```python
import functools

import jax
import jax.numpy as jnp
import numpy as np
from jax import lax
from jax.experimental import pallas as pl
from jax.experimental.pallas import tpu as pltpu
from jax.sharding import Mesh
from jax.sharding import PartitionSpec as P

LOG2E = 1.4426950408889634
BF16 = jnp.bfloat16
F32 = jnp.float32
SEQ_DIMS = {64: (4, 2, 8), 16: (2, 2, 4)}
SEQ = ("x", "y_lo", "z")
KVH = ("y_hi", "core")
VMEM_LIMIT = 10 * 1024 * 1024


def shift_seq(value, steps, sources=None):
    count = lax.axis_size(SEQ)
    sources = range(count) if sources is None else [s % count for s in sources]
    return lax.ppermute(value, SEQ, [(s, (s + steps) % count) for s in sources])


def shift(value, axis, steps):
    size = lax.axis_size(axis)
    return lax.ppermute(value, axis, [(s, (s + steps) % size) for s in range(size)])


def dot_nt(a, b):
    return lax.dot_general(a, b, (((1,), (1,)), ((), ())), preferred_element_type=F32)


def dot_nn(a, b):
    return lax.dot_general(a, b, (((1,), (0,)), ((), ())), preferred_element_type=F32)


def dot_tn(a, b):
    return lax.dot_general(a, b, (((0,), (0,)), ((), ())), preferred_element_type=F32)


def low_slot_of(me, order):
    return jnp.where(order[2 * me[0]] == me[0], 0, 1)


def offsets(me, order, half):
    slot = low_slot_of(me, order)
    return pl.multiple_of(slot * half, half), pl.multiple_of((1 - slot) * half, half)


def call(kernel, out_shape, args, scratch=(), cost=1, space=pltpu.VMEM):
    vmem = pl.BlockSpec(memory_space=pltpu.VMEM)
    smem = pl.BlockSpec(memory_space=pltpu.SMEM)
    return pl.pallas_call(
        kernel,
        out_shape=out_shape,
        in_specs=[smem, smem] + [pl.BlockSpec(memory_space=space)] * (len(args) - 2),
        out_specs=jax.tree.map(lambda _: vmem, out_shape),
        scratch_shapes=list(scratch),
        compiler_params=pltpu.CompilerParams(vmem_limit_bytes=VMEM_LIMIT),
        cost_estimate=pl.CostEstimate(flops=0, bytes_accessed=int(cost * 3.5e6), transcendentals=0),
    )(*args)


def split_kernel(me, order, keys, values, low, high, sems):
    half, hd = low.shape[0], keys.shape[1]
    copies = []
    for out, off in zip((low, high), offsets(me, order, half)):
        for n, source in enumerate((keys, values)):
            copies.append(
                pltpu.make_async_copy(
                    source.at[pl.ds(off, half), :],
                    out.at[:, n * hd : (n + 1) * hd],
                    sems.at[len(copies)],
                )
            )
    for copy in copies:
        copy.start()
    for copy in copies:
        copy.wait()


def pair_weights(query, grad, key, value, diagonal, scale):
    weights = jnp.exp2(dot_nt(key, query) * (scale * LOG2E))
    if diagonal:
        rows = lax.broadcasted_iota(jnp.int32, weights.shape, 0)
        cols = lax.broadcasted_iota(jnp.int32, weights.shape, 1)
        weights = jnp.where(rows <= cols, weights, 0.0)
    return weights, dot_nt(value, grad)


def add_stats(q, do, stats, heads, piece, place, off, diagonal):
    half, hd = piece.shape[0], piece.shape[1] // 2
    key, value = piece[:, :hd], piece[:, hd:]
    for j in range(heads):
        cols = slice(j * hd, (j + 1) * hd)
        query, grad = q[pl.ds(off, half), cols], do[pl.ds(off, half), cols]
        weights, grad_prob = pair_weights(query, grad, key, value, diagonal, hd**-0.5)
        stats[0, place, j : j + 1, :] += jnp.sum(weights, axis=0, keepdims=True)
        stats[1, place, j : j + 1, :] += jnp.sum(weights * grad_prob, axis=0, keepdims=True)


def add_grads(q, do, stats, dqt, heads, piece, place, off, diagonal):
    half, hd = piece.shape[0], piece.shape[1] // 2
    key, value = piece[:, :hd], piece[:, hd:]
    grad_key = grad_value = None
    for j in range(heads):
        cols = slice(j * hd, (j + 1) * hd)
        query, grad = q[pl.ds(off, half), cols], do[pl.ds(off, half), cols]
        weights, grad_prob = pair_weights(query, grad, key, value, diagonal, hd**-0.5)
        inverse = 1.0 / stats[0, place, j : j + 1, :]
        delta = stats[1, place, j : j + 1, :] * inverse
        prob = weights * inverse
        grad_score = (prob * (grad_prob - delta) * hd**-0.5).astype(BF16)
        term_key = dot_nn(grad_score, query)
        term_value = dot_nn(prob.astype(BF16), grad)
        grad_key = term_key if j == 0 else grad_key + term_key
        grad_value = term_value if j == 0 else grad_value + term_value
        dqt[place, j] += dot_tn(key, grad_score)
    return grad_key, grad_value


def second_quadrant(me, hop, low, high, picked, lo, hi):
    wraps = me[0] < hop
    picked[...] = low[...]

    @pl.when(wraps)
    def _():
        picked[...] = high[...]

    return wraps, jnp.where(wraps, 1, 0), pl.multiple_of(jnp.where(wraps, hi, lo), lo_size(picked))


def lo_size(ref):
    return ref.shape[0]


def near_stats_kernel(heads, me, order, q, do, low, high, low1, high1, low3, high3, stats, picked):
    lo, hi = offsets(me, order, low.shape[0])
    stats[...] = jnp.zeros_like(stats)
    add_stats(q, do, stats, heads, low, 1, hi, False)
    add_stats(q, do, stats, heads, high, 1, hi, True)
    add_stats(q, do, stats, heads, low, 0, lo, True)
    hop_stats(me, 1, q, do, stats, heads, low1, high1, picked, lo, hi)
    hop_stats(me, 3, q, do, stats, heads, low3, high3, picked, lo, hi)


def hop_stats(me, hop, q, do, stats, heads, low, high, picked, lo, hi):
    add_stats(q, do, stats, heads, low, 1, hi, False)
    _, place, off = second_quadrant(me, hop, low, high, picked, lo, hi)
    add_stats(q, do, stats, heads, picked, place, off, False)


def hop_terms(me, hop, q, do, stats, dqt, heads, low, high, picked, acc, lo, hi, out_low, out_high):
    hd = picked.shape[1] // 2
    acc[0, :, :hd], acc[0, :, hd:] = add_grads(q, do, stats, dqt, heads, low, 1, hi, False)
    wraps, place, off = second_quadrant(me, hop, low, high, picked, lo, hi)
    acc[1, :, :hd], acc[1, :, hd:] = add_grads(q, do, stats, dqt, heads, picked, place, off, False)

    @pl.when(wraps)
    def _():
        out_low[...] = acc[0].astype(out_low.dtype)
        out_high[...] = acc[1].astype(out_low.dtype)

    @pl.when(jnp.logical_not(wraps))
    def _():
        out_low[...] = (acc[0] + acc[1]).astype(out_low.dtype)
        out_high[...] = jnp.zeros_like(out_high)


def far_grads_kernel(
    heads, me, order, q, do, lows, highs, before, stats, dqt, out_lows, out_highs, picked, acc
):
    lo, hi = offsets(me, order, picked.shape[0])
    stats[...] = before[...]
    for n, hop in enumerate((2, 4)):
        hop_stats(me, hop, q, do, stats, heads, lows.at[n], highs.at[n], picked, lo, hi)
    dqt[...] = jnp.zeros_like(dqt)
    for n, hop in enumerate((2, 4)):
        hop_terms(
            me, hop, q, do, stats, dqt, heads, lows.at[n], highs.at[n],
            picked, acc, lo, hi, out_lows.at[n], out_highs.at[n],
        )


def near_grads_kernel(
    heads, me, order, q, do, stats, low3, high3, low1, high1, low, high, before,
    dq, own, term3_low, term3_high, term1_low, term1_high, dqt, picked, acc,
):
    half, hd = low.shape[0], low.shape[1] // 2
    lo, hi = offsets(me, order, half)
    dqt[...] = before[...]
    for hop, *refs, outs in (
        (3, low3, high3, (term3_low, term3_high)), (1, low1, high1, (term1_low, term1_high))
    ):
        hop_terms(me, hop, q, do, stats, dqt, heads, *refs, picked, acc, lo, hi, *outs)
    gk, gv = add_grads(q, do, stats, dqt, heads, low, 1, hi, False)
    gk2, gv2 = add_grads(q, do, stats, dqt, heads, low, 0, lo, True)
    own[0, :, :hd] = gk + gk2
    own[0, :, hd:] = gv + gv2
    own[1, :, :hd], own[1, :, hd:] = add_grads(q, do, stats, dqt, heads, high, 1, hi, True)
    for place, off in ((0, lo), (1, hi)):
        for j in range(heads):
            dq[pl.ds(off, half), j * hd : (j + 1) * hd] = dqt[place, j].T.astype(BF16)


def tokens_kernel(nz, at, order, own, up, far_up, far_down, down, theirs, *refs):
    grad, behind, grad_far_up, grad_far_down, ahead, out = refs
    rows = own.shape[1]
    block = rows // nz
    grads_far = jnp.concatenate([grad_far_up[...], grad_far_down[...]], axis=0)
    for n in range(2):
        if n == 0:
            y = at[0]
            far = jnp.concatenate([far_up[...], far_down[...]], axis=0)
            pieces = (up[:rows], far, down[:rows])
        else:
            y = 1 - at[0]
            pieces = tuple(theirs[k * rows : (k + 1) * rows] for k in range(3))
        total = dot_nn(own[y], grad[...])
        for piece, grads in zip(pieces, (behind[...], grads_far, ahead[...])):
            total = total + dot_nn(piece, grads)
        total = total.astype(BF16)
        for z in range(nz):
            out[y * nz + z] = total[z * block : (z + 1) * block]


def shards(hidden_in, w_qkv, queries, keys, values, d_out, block_order):
    count = lax.axis_size(SEQ)
    nx, ny, nz = (lax.axis_size(axis) for axis in SEQ)
    at_x, at_y = lax.axis_index("x"), lax.axis_index("y_lo")
    core, y_hi = lax.axis_index("core"), lax.axis_index("y_hi")
    index = lax.axis_index(SEQ).astype(jnp.int32)
    me = index.reshape(1)
    rows, width = hidden_in.shape
    half = rows // 2
    hd = keys.shape[1]
    heads = queries.shape[1] // hd
    out_rows = width // count

    piece = jax.ShapeDtypeStruct((half, 2 * hd), BF16)
    stats_shape = jax.ShapeDtypeStruct((2, 2, heads, half), F32)
    partial_q = jax.ShapeDtypeStruct((2, heads, hd, half), F32)
    picked = pltpu.VMEM(piece.shape, BF16)
    acc = pltpu.VMEM((2, half, 2 * hd), F32)

    low, high = call(
        split_kernel, [piece, piece], (me, block_order, keys, values),
        [pltpu.SemaphoreType.DMA((4,))], space=pltpu.HBM,
    )
    low1 = shift_seq(low, 1)
    high1 = shift_seq(high, 1, (-2, -1))
    low3 = shift_seq(low, 3)
    high3 = shift_seq(high, 3, (-4, -3, -2, -1))

    chunks = hidden_in.T.reshape(nx, ny, nz * out_rows, rows)
    to1, to2, to3 = (
        lax.dynamic_slice(
            chunks, ((at_x + k) % nx, core, 0, 0), (1, 1, *chunks.shape[2:])
        ).reshape(chunks.shape[2:])
        for k in range(1, nx)
    )
    split = to2.shape[0] // 2
    leaving = [jnp.concatenate([to1, to2[:split]]), jnp.concatenate([to3, to2[split:]])]
    hidden_own = lax.dynamic_index_in_dim(chunks, at_x, 0, keepdims=False)
    low1, high1, low3, high3, leaving, hidden_own = lax.optimization_barrier(
        (low1, high1, low3, high3, leaving, hidden_own)
    )
    low24 = shift_seq(jnp.stack([low1, low3]), 1)
    high24 = shift_seq(jnp.stack([high1, high3]), 1, (-1, 0, 1, 2))

    base = (me, block_order, queries, d_out)
    stats = call(
        functools.partial(near_stats_kernel, heads), stats_shape,
        (*base, low, high, low1, high1, low3, high3), [picked], cost=5,
    )
    low24, high24, stats, leaving = lax.optimization_barrier((low24, high24, stats, leaving))
    up, down = shift(leaving[0], "x", 1), shift(leaving[1], "x", -1)
    two = jax.ShapeDtypeStruct((2, *piece.shape), BF16)
    stats, dqt, out24, out24_high = call(
        functools.partial(far_grads_kernel, heads), [stats_shape, partial_q, two, two],
        (*base, low24, high24, stats), [picked, acc], cost=8,
    )
    back24 = shift_seq(out24, -1)
    back24_high = shift_seq(out24_high, -1, (0, 1, 2, 3))
    term = jax.ShapeDtypeStruct(piece.shape, F32)
    grad_q, own, out3, out3_high, out1, out1_high = call(
        functools.partial(near_grads_kernel, heads),
        [jax.ShapeDtypeStruct(queries.shape, BF16), jax.ShapeDtypeStruct((2, *piece.shape), F32),
         term, term, term, term],
        (*base, stats, low3, high3, low1, high1, low, high, dqt),
        [pltpu.VMEM(partial_q.shape, F32), picked, acc], cost=20,
    )
    grad_q, up, down = lax.optimization_barrier((grad_q, up, down))
    back1 = shift_seq((out1 + back24[0].astype(F32)).astype(BF16), -1)
    back3 = shift_seq((out3 + back24[1].astype(F32)).astype(BF16), -3)
    back1_high = shift_seq((out1_high + back24_high[0].astype(F32)).astype(BF16), -1, (0, -1))
    back3_high = shift_seq((out3_high + back24_high[1].astype(F32)).astype(BF16), -3, (-1, 0, 1, 2))

    def neighbours(matrix):
        return matrix, shift(matrix, "x", 1), shift(matrix, "x", -1)

    def x_gathered(matrix, behind, ahead):
        return matrix, behind, shift(behind[:half], "x", 1), shift(ahead[half:], "x", -1), ahead

    gathered_q = neighbours(grad_q)
    passed = (up[2 * split :], down[2 * split :])
    passed, back1, back1_high, back3, back3_high, gathered_q = lax.optimization_barrier(
        (passed, back1, back1_high, back3, back3_high, gathered_q)
    )
    far_up, far_down = shift(passed[0], "x", 1), shift(passed[1], "x", -1)
    gathered_q = x_gathered(*gathered_q)
    swapping = jnp.concatenate([up[: 2 * split], far_up, far_down, down[: 2 * split]])
    hidden_theirs = shift(lax.optimization_barrier((swapping, gathered_q))[0], "core", 1)

    def token_sums(gathered):
        return call(
            functools.partial(tokens_kernel, nz),
            jax.ShapeDtypeStruct((ny * nz, out_rows, gathered[0].shape[1]), BF16),
            (
                core.astype(jnp.int32).reshape(1), block_order, hidden_own,
                up, far_up, far_down, down, hidden_theirs, *gathered,
            ),
            cost=2,
        )


    low_total = own[0] + back1.astype(F32) + back3.astype(F32)
    high_total = own[1] + back1_high.astype(F32) + back3_high.astype(F32)
    low_total, high_total = low_total.astype(BF16), high_total.astype(BF16)
    grad_kv = jnp.where(
        low_slot_of(me, block_order) == 0,
        jnp.concatenate([low_total, high_total], axis=0),
        jnp.concatenate([high_total, low_total], axis=0),
    )

    def rows_of(owner, part):
        whole = jnp.concatenate([grad_q, part], axis=1).reshape(2, 2, rows // 4, -1)
        return lax.dynamic_index_in_dim(whole, owner, 1, keepdims=False).reshape(half, -1)

    step = width // 2
    weights = [w_qkv[start : start + step] for start in range(0, width, step)]
    theirs = rows_of(1 - core, grad_kv)
    for_core = [dot_nt(theirs, weight).astype(BF16) for weight in weights]
    gathered_q, for_core = lax.optimization_barrier((gathered_q, for_core))
    tokens_q = token_sums(gathered_q)
    received = [shift(product, "core", 1) for product in for_core]
    late_kv, tokens_q = lax.optimization_barrier((grad_kv, tokens_q))
    gathered_kv = x_gathered(*neighbours(late_kv))
    mine = rows_of(core, late_kv)
    totals = lax.optimization_barrier([dot_nt(mine, weight) for weight in weights])
    kept, sent = [], []
    for total, other in zip(totals, received):
        total = (total + other.astype(F32)).reshape(2, rows // 4, step)
        sent.append(lax.dynamic_index_in_dim(total, 1 - y_hi, 0, keepdims=False).astype(BF16))
        kept.append(lax.dynamic_index_in_dim(total, y_hi, 0, keepdims=False))

    grad_in = [keep + shift(send, "y_hi", 1).astype(F32) for keep, send in zip(kept, sent)]
    sums_q = lax.all_to_all(tokens_q, ("y_lo", "z"), 0, 0, tiled=True)
    tokens_kv, grad_in[0], sums_q = lax.optimization_barrier(
        (token_sums(gathered_kv), grad_in[0], sums_q)
    )
    sums_kv = lax.all_to_all(tokens_kv, ("y_lo", "z"), 0, 0, tiled=True)
    sums = [jnp.sum(part.astype(F32), axis=0) for part in (sums_q, sums_kv)]
    grad_w = jnp.concatenate(sums, axis=-1) * float(rows * count) ** (-0.5)
    return jnp.concatenate(grad_in, axis=1).astype(BF16), grad_w.astype(BF16)


def solution(mesh):
    dims = SEQ_DIMS[mesh.shape["seq"]] + (2, 2)
    split = Mesh(np.asarray(mesh.devices).reshape(dims), SEQ + KVH)
    return jax.shard_map(
        shards,
        mesh=split,
        in_specs=(
            P(SEQ, None),
            P(None, KVH),
            P(SEQ, KVH),
            P(SEQ, KVH),
            P(SEQ, KVH),
            P(SEQ, KVH),
            P(),
        ),
        out_specs=(P(SEQ + KVH, None), P(SEQ, KVH)),
        check_vma=False,
    )
```

```python
import functools

import jax
import jax.numpy as jnp
import numpy as np
from jax import lax
from jax.experimental import pallas as pl
from jax.experimental.pallas import tpu as pltpu
from jax.sharding import Mesh
from jax.sharding import PartitionSpec as P

LOG2E = 1.4426950408889634
BF16 = jnp.bfloat16
F32 = jnp.float32
SEQ_DIMS = {64: (4, 2, 8), 16: (2, 2, 4)}
SEQ = ("x", "y_lo", "z")
KVH = ("y_hi", "core")
VMEM_LIMIT = 10 * 1024 * 1024


def shift_seq(value, steps, sources=None):
    count = lax.axis_size(SEQ)
    sources = range(count) if sources is None else [s % count for s in sources]
    return lax.ppermute(value, SEQ, [(s, (s + steps) % count) for s in sources])


def shift(value, axis, steps):
    size = lax.axis_size(axis)
    return lax.ppermute(value, axis, [(s, (s + steps) % size) for s in range(size)])


def dot_nt(a, b):
    return lax.dot_general(a, b, (((1,), (1,)), ((), ())), preferred_element_type=F32)


def dot_nn(a, b):
    return lax.dot_general(a, b, (((1,), (0,)), ((), ())), preferred_element_type=F32)


def dot_tn(a, b):
    return lax.dot_general(a, b, (((0,), (0,)), ((), ())), preferred_element_type=F32)


def low_slot_of(me, order):
    return jnp.where(order[2 * me[0]] == me[0], 0, 1)


def offsets(me, order, half):
    slot = low_slot_of(me, order)
    return pl.multiple_of(slot * half, half), pl.multiple_of((1 - slot) * half, half)


def call(kernel, out_shape, args, scratch=(), cost=1, space=pltpu.VMEM):
    vmem = pl.BlockSpec(memory_space=pltpu.VMEM)
    smem = pl.BlockSpec(memory_space=pltpu.SMEM)
    return pl.pallas_call(
        kernel,
        out_shape=out_shape,
        in_specs=[smem, smem] + [pl.BlockSpec(memory_space=space)] * (len(args) - 2),
        out_specs=jax.tree.map(lambda _: vmem, out_shape),
        scratch_shapes=list(scratch),
        compiler_params=pltpu.CompilerParams(vmem_limit_bytes=VMEM_LIMIT),
        cost_estimate=pl.CostEstimate(flops=0, bytes_accessed=int(cost * 3.5e6), transcendentals=0),
    )(*args)


def split_kernel(me, order, keys, values, low, high, sems):
    half, hd = low.shape[0], keys.shape[1]
    copies = []
    for out, off in zip((low, high), offsets(me, order, half)):
        for n, source in enumerate((keys, values)):
            copies.append(
                pltpu.make_async_copy(
                    source.at[pl.ds(off, half), :],
                    out.at[:, n * hd : (n + 1) * hd],
                    sems.at[len(copies)],
                )
            )
    for copy in copies:
        copy.start()
    for copy in copies:
        copy.wait()


def pair_weights(query, grad, key, value, diagonal, scale):
    weights = jnp.exp2(dot_nt(key, query) * (scale * LOG2E))
    if diagonal:
        rows = lax.broadcasted_iota(jnp.int32, weights.shape, 0)
        cols = lax.broadcasted_iota(jnp.int32, weights.shape, 1)
        weights = jnp.where(rows <= cols, weights, 0.0)
    return weights, dot_nt(value, grad)


def add_stats(q, do, stats, heads, piece, place, off, diagonal):
    half, hd = piece.shape[0], piece.shape[1] // 2
    key, value = piece[:, :hd], piece[:, hd:]
    for j in range(heads):
        cols = slice(j * hd, (j + 1) * hd)
        query, grad = q[pl.ds(off, half), cols], do[pl.ds(off, half), cols]
        weights, grad_prob = pair_weights(query, grad, key, value, diagonal, hd**-0.5)
        stats[0, place, j : j + 1, :] += jnp.sum(weights, axis=0, keepdims=True)
        stats[1, place, j : j + 1, :] += jnp.sum(weights * grad_prob, axis=0, keepdims=True)


def add_grads(q, do, stats, dqt, heads, piece, place, off, diagonal):
    half, hd = piece.shape[0], piece.shape[1] // 2
    key, value = piece[:, :hd], piece[:, hd:]
    grad_key = grad_value = None
    for j in range(heads):
        cols = slice(j * hd, (j + 1) * hd)
        query, grad = q[pl.ds(off, half), cols], do[pl.ds(off, half), cols]
        weights, grad_prob = pair_weights(query, grad, key, value, diagonal, hd**-0.5)
        inverse = 1.0 / stats[0, place, j : j + 1, :]
        delta = stats[1, place, j : j + 1, :] * inverse
        prob = weights * inverse
        grad_score = (prob * (grad_prob - delta) * hd**-0.5).astype(BF16)
        term_key = dot_nn(grad_score, query)
        term_value = dot_nn(prob.astype(BF16), grad)
        grad_key = term_key if j == 0 else grad_key + term_key
        grad_value = term_value if j == 0 else grad_value + term_value
        dqt[place, j] += dot_tn(key, grad_score)
    return grad_key, grad_value


def second_quadrant(me, hop, low, high, picked, lo, hi):
    wraps = me[0] < hop
    picked[...] = low[...]

    @pl.when(wraps)
    def _():
        picked[...] = high[...]

    return wraps, jnp.where(wraps, 1, 0), pl.multiple_of(jnp.where(wraps, hi, lo), lo_size(picked))


def lo_size(ref):
    return ref.shape[0]


def near_stats_kernel(heads, me, order, q, do, low, high, low1, high1, low3, high3, stats, picked):
    lo, hi = offsets(me, order, low.shape[0])
    stats[...] = jnp.zeros_like(stats)
    add_stats(q, do, stats, heads, low, 1, hi, False)
    add_stats(q, do, stats, heads, high, 1, hi, True)
    add_stats(q, do, stats, heads, low, 0, lo, True)
    hop_stats(me, 1, q, do, stats, heads, low1, high1, picked, lo, hi)
    hop_stats(me, 3, q, do, stats, heads, low3, high3, picked, lo, hi)


def hop_stats(me, hop, q, do, stats, heads, low, high, picked, lo, hi):
    add_stats(q, do, stats, heads, low, 1, hi, False)
    _, place, off = second_quadrant(me, hop, low, high, picked, lo, hi)
    add_stats(q, do, stats, heads, picked, place, off, False)


def hop_terms(me, hop, q, do, stats, dqt, heads, low, high, picked, acc, lo, hi, out_low, out_high):
    hd = picked.shape[1] // 2
    acc[0, :, :hd], acc[0, :, hd:] = add_grads(q, do, stats, dqt, heads, low, 1, hi, False)
    wraps, place, off = second_quadrant(me, hop, low, high, picked, lo, hi)
    acc[1, :, :hd], acc[1, :, hd:] = add_grads(q, do, stats, dqt, heads, picked, place, off, False)

    @pl.when(wraps)
    def _():
        out_low[...] = acc[0].astype(out_low.dtype)
        out_high[...] = acc[1].astype(out_low.dtype)

    @pl.when(jnp.logical_not(wraps))
    def _():
        out_low[...] = (acc[0] + acc[1]).astype(out_low.dtype)
        out_high[...] = jnp.zeros_like(out_high)


def far_grads_kernel(
    heads, me, order, q, do, lows, highs, before, stats, dqt, out_lows, out_highs, picked, acc
):
    lo, hi = offsets(me, order, picked.shape[0])
    stats[...] = before[...]
    for n, hop in enumerate((2, 4)):
        hop_stats(me, hop, q, do, stats, heads, lows.at[n], highs.at[n], picked, lo, hi)
    dqt[...] = jnp.zeros_like(dqt)
    for n, hop in enumerate((2, 4)):
        hop_terms(
            me, hop, q, do, stats, dqt, heads, lows.at[n], highs.at[n],
            picked, acc, lo, hi, out_lows.at[n], out_highs.at[n],
        )


def near_grads_kernel(
    heads, me, order, q, do, stats, low3, high3, low1, high1, low, high, before,
    dq, own, term3_low, term3_high, term1_low, term1_high, dqt, picked, acc,
):
    half, hd = low.shape[0], low.shape[1] // 2
    lo, hi = offsets(me, order, half)
    dqt[...] = before[...]
    for hop, *refs, outs in (
        (3, low3, high3, (term3_low, term3_high)), (1, low1, high1, (term1_low, term1_high))
    ):
        hop_terms(me, hop, q, do, stats, dqt, heads, *refs, picked, acc, lo, hi, *outs)
    gk, gv = add_grads(q, do, stats, dqt, heads, low, 1, hi, False)
    gk2, gv2 = add_grads(q, do, stats, dqt, heads, low, 0, lo, True)
    own[0, :, :hd] = gk + gk2
    own[0, :, hd:] = gv + gv2
    own[1, :, :hd], own[1, :, hd:] = add_grads(q, do, stats, dqt, heads, high, 1, hi, True)
    for place, off in ((0, lo), (1, hi)):
        for j in range(heads):
            dq[pl.ds(off, half), j * hd : (j + 1) * hd] = dqt[place, j].T.astype(BF16)


def tokens_kernel(nz, at, order, own, up, far_up, far_down, down, theirs, *refs):
    grad, behind, grad_far_up, grad_far_down, ahead, out = refs
    rows = own.shape[1]
    block = rows // nz
    grads_far = jnp.concatenate([grad_far_up[...], grad_far_down[...]], axis=0)
    for n in range(2):
        if n == 0:
            y = at[0]
            far = jnp.concatenate([far_up[...], far_down[...]], axis=0)
            pieces = (up[:rows], far, down[:rows])
        else:
            y = 1 - at[0]
            pieces = tuple(theirs[k * rows : (k + 1) * rows] for k in range(3))
        total = dot_nn(own[y], grad[...])
        for piece, grads in zip(pieces, (behind[...], grads_far, ahead[...])):
            total = total + dot_nn(piece, grads)
        total = total.astype(BF16)
        for z in range(nz):
            out[y * nz + z] = total[z * block : (z + 1) * block]


def shards(hidden_in, w_qkv, queries, keys, values, d_out, block_order):
    count = lax.axis_size(SEQ)
    nx, ny, nz = (lax.axis_size(axis) for axis in SEQ)
    at_x, at_y = lax.axis_index("x"), lax.axis_index("y_lo")
    core, y_hi = lax.axis_index("core"), lax.axis_index("y_hi")
    index = lax.axis_index(SEQ).astype(jnp.int32)
    me = index.reshape(1)
    rows, width = hidden_in.shape
    half = rows // 2
    hd = keys.shape[1]
    heads = queries.shape[1] // hd
    out_rows = width // count

    piece = jax.ShapeDtypeStruct((half, 2 * hd), BF16)
    stats_shape = jax.ShapeDtypeStruct((2, 2, heads, half), F32)
    partial_q = jax.ShapeDtypeStruct((2, heads, hd, half), F32)
    picked = pltpu.VMEM(piece.shape, BF16)
    acc = pltpu.VMEM((2, half, 2 * hd), F32)

    low, high = call(
        split_kernel, [piece, piece], (me, block_order, keys, values),
        [pltpu.SemaphoreType.DMA((4,))], space=pltpu.HBM,
    )
    low1 = shift_seq(low, 1)
    high1 = shift_seq(high, 1, (-2, -1))
    low3 = shift_seq(low, 3)
    high3 = shift_seq(high, 3, (-4, -3, -2, -1))

    chunks = hidden_in.T.reshape(nx, ny, nz * out_rows, rows)
    to1, to2, to3 = (
        lax.dynamic_slice(
            chunks, ((at_x + k) % nx, core, 0, 0), (1, 1, *chunks.shape[2:])
        ).reshape(chunks.shape[2:])
        for k in range(1, nx)
    )
    split = to2.shape[0] // 2
    leaving = [jnp.concatenate([to1, to2[:split]]), jnp.concatenate([to3, to2[split:]])]
    hidden_own = lax.dynamic_index_in_dim(chunks, at_x, 0, keepdims=False)
    low1, high1, low3, high3, leaving, hidden_own = lax.optimization_barrier(
        (low1, high1, low3, high3, leaving, hidden_own)
    )
    low24 = shift_seq(jnp.stack([low1, low3]), 1)
    high24 = shift_seq(jnp.stack([high1, high3]), 1, (-1, 0, 1, 2))

    base = (me, block_order, queries, d_out)
    stats = call(
        functools.partial(near_stats_kernel, heads), stats_shape,
        (*base, low, high, low1, high1, low3, high3), [picked], cost=5,
    )
    low24, high24, stats, leaving = lax.optimization_barrier((low24, high24, stats, leaving))
    up, down = shift(leaving[0], "x", 1), shift(leaving[1], "x", -1)
    two = jax.ShapeDtypeStruct((2, *piece.shape), BF16)
    stats, dqt, out24, out24_high = call(
        functools.partial(far_grads_kernel, heads), [stats_shape, partial_q, two, two],
        (*base, low24, high24, stats), [picked, acc], cost=8,
    )
    back24 = shift_seq(out24, -1)
    back24_high = shift_seq(out24_high, -1, (0, 1, 2, 3))
    term = jax.ShapeDtypeStruct(piece.shape, F32)
    grad_q, own, out3, out3_high, out1, out1_high = call(
        functools.partial(near_grads_kernel, heads),
        [jax.ShapeDtypeStruct(queries.shape, BF16), jax.ShapeDtypeStruct((2, *piece.shape), F32),
         term, term, term, term],
        (*base, stats, low3, high3, low1, high1, low, high, dqt),
        [pltpu.VMEM(partial_q.shape, F32), picked, acc], cost=20,
    )
    grad_q, up, down = lax.optimization_barrier((grad_q, up, down))
    back1 = shift_seq((out1 + back24[0].astype(F32)).astype(BF16), -1)
    back3 = shift_seq((out3 + back24[1].astype(F32)).astype(BF16), -3)
    back1_high = shift_seq((out1_high + back24_high[0].astype(F32)).astype(BF16), -1, (0, -1))
    back3_high = shift_seq((out3_high + back24_high[1].astype(F32)).astype(BF16), -3, (-1, 0, 1, 2))

    def neighbours(matrix):
        return matrix, shift(matrix, "x", 1), shift(matrix, "x", -1)

    def x_gathered(matrix, behind, ahead):
        return matrix, behind, shift(behind[:half], "x", 1), shift(ahead[half:], "x", -1), ahead

    gathered_q = neighbours(grad_q)
    passed = (up[2 * split :], down[2 * split :])
    passed, back1, back1_high, back3, back3_high, gathered_q = lax.optimization_barrier(
        (passed, back1, back1_high, back3, back3_high, gathered_q)
    )
    far_up, far_down = shift(passed[0], "x", 1), shift(passed[1], "x", -1)
    gathered_q = x_gathered(*gathered_q)
    swapping = jnp.concatenate([up[: 2 * split], far_up, far_down, down[: 2 * split]])
    hidden_theirs = shift(lax.optimization_barrier((swapping, gathered_q))[0], "core", 1)

    def token_sums(gathered):
        return call(
            functools.partial(tokens_kernel, nz),
            jax.ShapeDtypeStruct((ny * nz, out_rows, gathered[0].shape[1]), BF16),
            (
                core.astype(jnp.int32).reshape(1), block_order, hidden_own,
                up, far_up, far_down, down, hidden_theirs, *gathered,
            ),
            cost=2,
        )

    tokens_q = token_sums(gathered_q)

    low_total = own[0] + back1.astype(F32) + back3.astype(F32)
    high_total = own[1] + back1_high.astype(F32) + back3_high.astype(F32)
    low_total, high_total = low_total.astype(BF16), high_total.astype(BF16)
    grad_kv = jnp.where(
        low_slot_of(me, block_order) == 0,
        jnp.concatenate([low_total, high_total], axis=0),
        jnp.concatenate([high_total, low_total], axis=0),
    )

    grad_kv, tokens_q = lax.optimization_barrier((grad_kv, tokens_q))
    gathered_kv = x_gathered(*neighbours(grad_kv))

    grads = jnp.concatenate([grad_q, grad_kv], axis=1).reshape(2, 2, rows // 4, -1)
    theirs = lax.dynamic_index_in_dim(grads, 1 - core, 1, keepdims=False).reshape(half, -1)
    mine = lax.dynamic_index_in_dim(grads, core, 1, keepdims=False).reshape(half, -1)
    step = width // 2
    weights = [w_qkv[start : start + step] for start in range(0, width, step)]
    received = [shift(dot_nt(theirs, weight).astype(BF16), "core", 1) for weight in weights]
    totals = lax.optimization_barrier([dot_nt(mine, weight) for weight in weights])
    kept, sent = [], []
    for total, other in zip(totals, received):
        total = (total + other.astype(F32)).reshape(2, rows // 4, step)
        sent.append(lax.dynamic_index_in_dim(total, 1 - y_hi, 0, keepdims=False).astype(BF16))
        kept.append(lax.dynamic_index_in_dim(total, y_hi, 0, keepdims=False))

    grad_in = [keep + shift(send, "y_hi", 1).astype(F32) for keep, send in zip(kept, sent)]
    sums_q = lax.all_to_all(tokens_q, ("y_lo", "z"), 0, 0, tiled=True)
    tokens_kv, grad_in[0], sums_q = lax.optimization_barrier(
        (token_sums(gathered_kv), grad_in[0], sums_q)
    )
    sums_kv = lax.all_to_all(tokens_kv, ("y_lo", "z"), 0, 0, tiled=True)
    sums = [jnp.sum(part.astype(F32), axis=0) for part in (sums_q, sums_kv)]
    grad_w = jnp.concatenate(sums, axis=-1) * float(rows * count) ** (-0.5)
    return jnp.concatenate(grad_in, axis=1).astype(BF16), grad_w.astype(BF16)


def solution(mesh):
    dims = SEQ_DIMS[mesh.shape["seq"]] + (2, 2)
    split = Mesh(np.asarray(mesh.devices).reshape(dims), SEQ + KVH)
    return jax.shard_map(
        shards,
        mesh=split,
        in_specs=(
            P(SEQ, None),
            P(None, KVH),
            P(SEQ, KVH),
            P(SEQ, KVH),
            P(SEQ, KVH),
            P(SEQ, KVH),
            P(),
        ),
        out_specs=(P(SEQ + KVH, None), P(SEQ, KVH)),
        check_vma=False,
    )
```

```python
import functools

import jax
import jax.numpy as jnp
import numpy as np
from jax import lax
from jax.experimental import pallas as pl
from jax.experimental.pallas import tpu as pltpu
from jax.sharding import Mesh
from jax.sharding import PartitionSpec as P

LOG2E = 1.4426950408889634
BF16 = jnp.bfloat16
F32 = jnp.float32
SEQ_DIMS = {64: (4, 2, 8), 16: (2, 2, 4)}
SEQ = ("x", "y_lo", "z")
KVH = ("y_hi", "core")
VMEM_LIMIT = 10 * 1024 * 1024


def shift_seq(value, steps, sources=None):
    count = lax.axis_size(SEQ)
    sources = range(count) if sources is None else [s % count for s in sources]
    return lax.ppermute(value, SEQ, [(s, (s + steps) % count) for s in sources])


def shift(value, axis, steps):
    size = lax.axis_size(axis)
    return lax.ppermute(value, axis, [(s, (s + steps) % size) for s in range(size)])


def dot_nt(a, b):
    return lax.dot_general(a, b, (((1,), (1,)), ((), ())), preferred_element_type=F32)


def dot_nn(a, b):
    return lax.dot_general(a, b, (((1,), (0,)), ((), ())), preferred_element_type=F32)


def dot_tn(a, b):
    return lax.dot_general(a, b, (((0,), (0,)), ((), ())), preferred_element_type=F32)


def low_slot_of(me, order):
    return jnp.where(order[2 * me[0]] == me[0], 0, 1)


def offsets(me, order, half):
    slot = low_slot_of(me, order)
    return pl.multiple_of(slot * half, half), pl.multiple_of((1 - slot) * half, half)


def call(kernel, out_shape, args, scratch=(), cost=1, space=pltpu.VMEM):
    vmem = pl.BlockSpec(memory_space=pltpu.VMEM)
    smem = pl.BlockSpec(memory_space=pltpu.SMEM)
    return pl.pallas_call(
        kernel,
        out_shape=out_shape,
        in_specs=[smem, smem] + [pl.BlockSpec(memory_space=space)] * (len(args) - 2),
        out_specs=jax.tree.map(lambda _: vmem, out_shape),
        scratch_shapes=list(scratch),
        compiler_params=pltpu.CompilerParams(vmem_limit_bytes=VMEM_LIMIT),
        cost_estimate=pl.CostEstimate(flops=0, bytes_accessed=int(cost * 3.5e6), transcendentals=0),
    )(*args)


def split_kernel(me, order, keys, values, low, high, sems):
    half, hd = low.shape[0], keys.shape[1]
    copies = []
    for out, off in zip((low, high), offsets(me, order, half)):
        for n, source in enumerate((keys, values)):
            copies.append(
                pltpu.make_async_copy(
                    source.at[pl.ds(off, half), :],
                    out.at[:, n * hd : (n + 1) * hd],
                    sems.at[len(copies)],
                )
            )
    for copy in copies:
        copy.start()
    for copy in copies:
        copy.wait()


def pair_weights(query, grad, key, value, diagonal, scale):
    weights = jnp.exp2(dot_nt(key, query) * (scale * LOG2E))
    if diagonal:
        rows = lax.broadcasted_iota(jnp.int32, weights.shape, 0)
        cols = lax.broadcasted_iota(jnp.int32, weights.shape, 1)
        weights = jnp.where(rows <= cols, weights, 0.0)
    return weights, dot_nt(value, grad)


def add_stats(q, do, stats, heads, piece, place, off, diagonal):
    half, hd = piece.shape[0], piece.shape[1] // 2
    key, value = piece[:, :hd], piece[:, hd:]
    for j in range(heads):
        cols = slice(j * hd, (j + 1) * hd)
        query, grad = q[pl.ds(off, half), cols], do[pl.ds(off, half), cols]
        weights, grad_prob = pair_weights(query, grad, key, value, diagonal, hd**-0.5)
        stats[0, place, j : j + 1, :] += jnp.sum(weights, axis=0, keepdims=True)
        stats[1, place, j : j + 1, :] += jnp.sum(weights * grad_prob, axis=0, keepdims=True)


def add_grads(q, do, stats, dqt, heads, piece, place, off, diagonal):
    half, hd = piece.shape[0], piece.shape[1] // 2
    key, value = piece[:, :hd], piece[:, hd:]
    grad_key = grad_value = None
    for j in range(heads):
        cols = slice(j * hd, (j + 1) * hd)
        query, grad = q[pl.ds(off, half), cols], do[pl.ds(off, half), cols]
        weights, grad_prob = pair_weights(query, grad, key, value, diagonal, hd**-0.5)
        inverse = 1.0 / stats[0, place, j : j + 1, :]
        delta = stats[1, place, j : j + 1, :] * inverse
        prob = weights * inverse
        grad_score = (prob * (grad_prob - delta) * hd**-0.5).astype(BF16)
        term_key = dot_nn(grad_score, query)
        term_value = dot_nn(prob.astype(BF16), grad)
        grad_key = term_key if j == 0 else grad_key + term_key
        grad_value = term_value if j == 0 else grad_value + term_value
        dqt[place, j] += dot_tn(key, grad_score)
    return grad_key, grad_value


def second_quadrant(me, hop, low, high, picked, lo, hi):
    wraps = me[0] < hop
    picked[...] = low[...]

    @pl.when(wraps)
    def _():
        picked[...] = high[...]

    return wraps, jnp.where(wraps, 1, 0), pl.multiple_of(jnp.where(wraps, hi, lo), lo_size(picked))


def lo_size(ref):
    return ref.shape[0]


def near_stats_kernel(heads, me, order, q, do, low, high, low1, high1, low3, high3, stats, picked):
    lo, hi = offsets(me, order, low.shape[0])
    stats[...] = jnp.zeros_like(stats)
    add_stats(q, do, stats, heads, low, 1, hi, False)
    add_stats(q, do, stats, heads, high, 1, hi, True)
    add_stats(q, do, stats, heads, low, 0, lo, True)
    hop_stats(me, 1, q, do, stats, heads, low1, high1, picked, lo, hi)
    hop_stats(me, 3, q, do, stats, heads, low3, high3, picked, lo, hi)


def hop_stats(me, hop, q, do, stats, heads, low, high, picked, lo, hi):
    add_stats(q, do, stats, heads, low, 1, hi, False)
    _, place, off = second_quadrant(me, hop, low, high, picked, lo, hi)
    add_stats(q, do, stats, heads, picked, place, off, False)


def hop_terms(me, hop, q, do, stats, dqt, heads, low, high, picked, acc, lo, hi, out_low, out_high):
    hd = picked.shape[1] // 2
    acc[0, :, :hd], acc[0, :, hd:] = add_grads(q, do, stats, dqt, heads, low, 1, hi, False)
    wraps, place, off = second_quadrant(me, hop, low, high, picked, lo, hi)
    acc[1, :, :hd], acc[1, :, hd:] = add_grads(q, do, stats, dqt, heads, picked, place, off, False)

    @pl.when(wraps)
    def _():
        out_low[...] = acc[0].astype(out_low.dtype)
        out_high[...] = acc[1].astype(out_low.dtype)

    @pl.when(jnp.logical_not(wraps))
    def _():
        out_low[...] = (acc[0] + acc[1]).astype(out_low.dtype)
        out_high[...] = jnp.zeros_like(out_high)


def far_grads_kernel(
    heads, me, order, q, do, lows, highs, before, stats, dqt, out_lows, out_highs, picked, acc
):
    lo, hi = offsets(me, order, picked.shape[0])
    stats[...] = before[...]
    for n, hop in enumerate((2, 4)):
        hop_stats(me, hop, q, do, stats, heads, lows.at[n], highs.at[n], picked, lo, hi)
    dqt[...] = jnp.zeros_like(dqt)
    for n, hop in enumerate((2, 4)):
        hop_terms(
            me, hop, q, do, stats, dqt, heads, lows.at[n], highs.at[n],
            picked, acc, lo, hi, out_lows.at[n], out_highs.at[n],
        )


def near_grads_kernel(
    heads, me, order, q, do, stats, low3, high3, low1, high1, low, high, before,
    dq, own, term3_low, term3_high, term1_low, term1_high, dqt, picked, acc,
):
    half, hd = low.shape[0], low.shape[1] // 2
    lo, hi = offsets(me, order, half)
    dqt[...] = before[...]
    for hop, *refs, outs in (
        (3, low3, high3, (term3_low, term3_high)), (1, low1, high1, (term1_low, term1_high))
    ):
        hop_terms(me, hop, q, do, stats, dqt, heads, *refs, picked, acc, lo, hi, *outs)
    gk, gv = add_grads(q, do, stats, dqt, heads, low, 1, hi, False)
    gk2, gv2 = add_grads(q, do, stats, dqt, heads, low, 0, lo, True)
    own[0, :, :hd] = gk + gk2
    own[0, :, hd:] = gv + gv2
    own[1, :, :hd], own[1, :, hd:] = add_grads(q, do, stats, dqt, heads, high, 1, hi, True)
    for place, off in ((0, lo), (1, hi)):
        for j in range(heads):
            dq[pl.ds(off, half), j * hd : (j + 1) * hd] = dqt[place, j].T.astype(BF16)


def tokens_kernel(nz, at, order, own, up, far_up, far_down, down, theirs, *refs):
    grad, behind, *grads_far, ahead, out = refs
    rows = own.shape[1]
    block = rows // nz
    grads_far = jnp.concatenate([part[...] for part in grads_far], axis=0)
    for n in range(2):
        if n == 0:
            y = at[0]
            far = jnp.concatenate([far_up[...], far_down[...]], axis=0)
            pieces = (up[:rows], far, down[:rows])
        else:
            y = 1 - at[0]
            pieces = tuple(theirs[k * rows : (k + 1) * rows] for k in range(3))
        total = dot_nn(own[y], grad[...])
        for piece, grads in zip(pieces, (behind[...], grads_far, ahead[...])):
            total = total + dot_nn(piece, grads)
        total = total.astype(BF16)
        for z in range(nz):
            out[y * nz + z] = total[z * block : (z + 1) * block]


def shards(hidden_in, w_qkv, queries, keys, values, d_out, block_order):
    count = lax.axis_size(SEQ)
    nx, ny, nz = (lax.axis_size(axis) for axis in SEQ)
    at_x, at_y = lax.axis_index("x"), lax.axis_index("y_lo")
    core, y_hi = lax.axis_index("core"), lax.axis_index("y_hi")
    index = lax.axis_index(SEQ).astype(jnp.int32)
    me = index.reshape(1)
    rows, width = hidden_in.shape
    half = rows // 2
    hd = keys.shape[1]
    heads = queries.shape[1] // hd
    out_rows = width // count

    piece = jax.ShapeDtypeStruct((half, 2 * hd), BF16)
    stats_shape = jax.ShapeDtypeStruct((2, 2, heads, half), F32)
    partial_q = jax.ShapeDtypeStruct((2, heads, hd, half), F32)
    picked = pltpu.VMEM(piece.shape, BF16)
    acc = pltpu.VMEM((2, half, 2 * hd), F32)

    low, high = call(
        split_kernel, [piece, piece], (me, block_order, keys, values),
        [pltpu.SemaphoreType.DMA((4,))], space=pltpu.HBM,
    )
    low1 = shift_seq(low, 1)
    high1 = shift_seq(high, 1, (-2, -1))
    low3 = shift_seq(low, 3)
    high3 = shift_seq(high, 3, (-4, -3, -2, -1))

    chunks = hidden_in.T.reshape(nx, ny, nz * out_rows, rows)
    to1, to2, to3 = (
        lax.dynamic_slice(
            chunks, ((at_x + k) % nx, core, 0, 0), (1, 1, *chunks.shape[2:])
        ).reshape(chunks.shape[2:])
        for k in range(1, nx)
    )
    split = to2.shape[0] // 2
    leaving = [jnp.concatenate([to1, to2[:split]]), jnp.concatenate([to3, to2[split:]])]
    hidden_own = lax.dynamic_index_in_dim(chunks, at_x, 0, keepdims=False)
    low1, high1, low3, high3, leaving, hidden_own = lax.optimization_barrier(
        (low1, high1, low3, high3, leaving, hidden_own)
    )
    low24 = shift_seq(jnp.stack([low1, low3]), 1)
    high24 = shift_seq(jnp.stack([high1, high3]), 1, (-1, 0, 1, 2))

    base = (me, block_order, queries, d_out)
    stats = call(
        functools.partial(near_stats_kernel, heads), stats_shape,
        (*base, low, high, low1, high1, low3, high3), [picked], cost=5,
    )
    low24, high24, stats, leaving = lax.optimization_barrier((low24, high24, stats, leaving))
    up, down = shift(leaving[0], "x", 1), shift(leaving[1], "x", -1)
    two = jax.ShapeDtypeStruct((2, *piece.shape), BF16)
    stats, dqt, out24, out24_high = call(
        functools.partial(far_grads_kernel, heads), [stats_shape, partial_q, two, two],
        (*base, low24, high24, stats), [picked, acc], cost=8,
    )
    back24 = shift_seq(out24, -1)
    back24_high = shift_seq(out24_high, -1, (0, 1, 2, 3))
    term = jax.ShapeDtypeStruct(piece.shape, F32)
    grad_q, own, out3, out3_high, out1, out1_high = call(
        functools.partial(near_grads_kernel, heads),
        [jax.ShapeDtypeStruct(queries.shape, BF16), jax.ShapeDtypeStruct((2, *piece.shape), F32),
         term, term, term, term],
        (*base, stats, low3, high3, low1, high1, low, high, dqt),
        [pltpu.VMEM(partial_q.shape, F32), picked, acc], cost=20,
    )
    grad_q, up, down = lax.optimization_barrier((grad_q, up, down))
    back1 = shift_seq((out1 + back24[0].astype(F32)).astype(BF16), -1)
    back3 = shift_seq((out3 + back24[1].astype(F32)).astype(BF16), -3)
    back1_high = shift_seq((out1_high + back24_high[0].astype(F32)).astype(BF16), -1, (0, -1))
    back3_high = shift_seq((out3_high + back24_high[1].astype(F32)).astype(BF16), -3, (-1, 0, 1, 2))

    def neighbours(matrix):
        return matrix, shift(matrix, "x", 1), shift(matrix, "x", -1)

    def x_gathered(matrix, behind, ahead):
        return matrix, behind, shift(behind[:half], "x", 1), shift(ahead[half:], "x", -1), ahead

    gathered_q = neighbours(grad_q)
    passed = (up[2 * split :], down[2 * split :])
    passed, back1, back1_high, back3, back3_high, gathered_q = lax.optimization_barrier(
        (passed, back1, back1_high, back3, back3_high, gathered_q)
    )
    far_up, far_down = shift(passed[0], "x", 1), shift(passed[1], "x", -1)
    gathered_q = x_gathered(*gathered_q)
    swapping = jnp.concatenate([up[: 2 * split], far_up, far_down, down[: 2 * split]])
    hidden_theirs = shift(lax.optimization_barrier((swapping, gathered_q))[0], "core", 1)

    def token_sums(gathered):
        return call(
            functools.partial(tokens_kernel, nz),
            jax.ShapeDtypeStruct((ny * nz, out_rows, gathered[0].shape[1]), BF16),
            (
                core.astype(jnp.int32).reshape(1), block_order, hidden_own,
                up, far_up, far_down, down, hidden_theirs, *gathered,
            ),
            cost=2,
        )

    tokens_q = token_sums(gathered_q)

    low_total = own[0] + back1.astype(F32) + back3.astype(F32)
    high_total = own[1] + back1_high.astype(F32) + back3_high.astype(F32)
    low_total, high_total = low_total.astype(BF16), high_total.astype(BF16)
    grad_kv = jnp.where(
        low_slot_of(me, block_order) == 0,
        jnp.concatenate([low_total, high_total], axis=0),
        jnp.concatenate([high_total, low_total], axis=0),
    )

    grad_kv, tokens_q = lax.optimization_barrier((grad_kv, tokens_q))
    near_kv = neighbours(grad_kv)
    gathered_kv = (*near_kv[:2], shift(near_kv[1], "x", 1), near_kv[2])

    grads = jnp.concatenate([grad_q, grad_kv], axis=1).reshape(2, 2, rows // 4, -1)
    theirs = lax.dynamic_index_in_dim(grads, 1 - core, 1, keepdims=False).reshape(half, -1)
    mine = lax.dynamic_index_in_dim(grads, core, 1, keepdims=False).reshape(half, -1)
    step = width // 2
    weights = [w_qkv[start : start + step] for start in range(0, width, step)]
    received = [shift(dot_nt(theirs, weight).astype(BF16), "core", 1) for weight in weights]
    totals = lax.optimization_barrier([dot_nt(mine, weight) for weight in weights])
    kept, sent = [], []
    for total, other in zip(totals, received):
        total = (total + other.astype(F32)).reshape(2, rows // 4, step)
        sent.append(lax.dynamic_index_in_dim(total, 1 - y_hi, 0, keepdims=False).astype(BF16))
        kept.append(lax.dynamic_index_in_dim(total, y_hi, 0, keepdims=False))

    grad_in = [keep + shift(send, "y_hi", 1).astype(F32) for keep, send in zip(kept, sent)]
    sums_q = lax.all_to_all(tokens_q, ("y_lo", "z"), 0, 0, tiled=True)
    tokens_kv, grad_in[0], sums_q = lax.optimization_barrier(
        (token_sums(gathered_kv), grad_in[0], sums_q)
    )
    sums_kv = lax.all_to_all(tokens_kv, ("y_lo", "z"), 0, 0, tiled=True)
    sums = [jnp.sum(part.astype(F32), axis=0) for part in (sums_q, sums_kv)]
    grad_w = jnp.concatenate(sums, axis=-1) * float(rows * count) ** (-0.5)
    return jnp.concatenate(grad_in, axis=1).astype(BF16), grad_w.astype(BF16)


def solution(mesh):
    dims = SEQ_DIMS[mesh.shape["seq"]] + (2, 2)
    split = Mesh(np.asarray(mesh.devices).reshape(dims), SEQ + KVH)
    return jax.shard_map(
        shards,
        mesh=split,
        in_specs=(
            P(SEQ, None),
            P(None, KVH),
            P(SEQ, KVH),
            P(SEQ, KVH),
            P(SEQ, KVH),
            P(SEQ, KVH),
            P(),
        ),
        out_specs=(P(SEQ + KVH, None), P(SEQ, KVH)),
        check_vma=False,
    )
```

```python
import functools

import jax
import jax.numpy as jnp
import numpy as np
from jax import lax
from jax.experimental import pallas as pl
from jax.experimental.pallas import tpu as pltpu
from jax.sharding import Mesh
from jax.sharding import PartitionSpec as P

LOG2E = 1.4426950408889634
BF16 = jnp.bfloat16
F32 = jnp.float32
SEQ_DIMS = {64: (4, 2, 8), 16: (2, 2, 4)}
SEQ = ("x", "y_lo", "z")
KVH = ("y_hi", "core")
VMEM_LIMIT = 10 * 1024 * 1024


def shift_seq(value, steps, sources=None):
    count = lax.axis_size(SEQ)
    sources = range(count) if sources is None else [s % count for s in sources]
    return lax.ppermute(value, SEQ, [(s, (s + steps) % count) for s in sources])


def shift(value, axis, steps):
    size = lax.axis_size(axis)
    return lax.ppermute(value, axis, [(s, (s + steps) % size) for s in range(size)])


def dot_nt(a, b):
    return lax.dot_general(a, b, (((1,), (1,)), ((), ())), preferred_element_type=F32)


def dot_nn(a, b):
    return lax.dot_general(a, b, (((1,), (0,)), ((), ())), preferred_element_type=F32)


def dot_tn(a, b):
    return lax.dot_general(a, b, (((0,), (0,)), ((), ())), preferred_element_type=F32)


def low_slot_of(me, order):
    return jnp.where(order[2 * me[0]] == me[0], 0, 1)


def offsets(me, order, half):
    slot = low_slot_of(me, order)
    return pl.multiple_of(slot * half, half), pl.multiple_of((1 - slot) * half, half)


def call(kernel, out_shape, args, scratch=(), cost=1, space=pltpu.VMEM):
    vmem = pl.BlockSpec(memory_space=pltpu.VMEM)
    smem = pl.BlockSpec(memory_space=pltpu.SMEM)
    return pl.pallas_call(
        kernel,
        out_shape=out_shape,
        in_specs=[smem, smem] + [pl.BlockSpec(memory_space=space)] * (len(args) - 2),
        out_specs=jax.tree.map(lambda _: vmem, out_shape),
        scratch_shapes=list(scratch),
        compiler_params=pltpu.CompilerParams(vmem_limit_bytes=VMEM_LIMIT),
        cost_estimate=pl.CostEstimate(flops=0, bytes_accessed=int(cost * 3.5e6), transcendentals=0),
    )(*args)


def split_kernel(me, order, keys, values, low, high, sems):
    half, hd = low.shape[0], keys.shape[1]
    copies = []
    for out, off in zip((low, high), offsets(me, order, half)):
        for n, source in enumerate((keys, values)):
            copies.append(
                pltpu.make_async_copy(
                    source.at[pl.ds(off, half), :],
                    out.at[:, n * hd : (n + 1) * hd],
                    sems.at[len(copies)],
                )
            )
    for copy in copies:
        copy.start()
    for copy in copies:
        copy.wait()


def pair_weights(query, grad, key, value, diagonal, scale):
    weights = jnp.exp2(dot_nt(key, query) * (scale * LOG2E))
    if diagonal:
        rows = lax.broadcasted_iota(jnp.int32, weights.shape, 0)
        cols = lax.broadcasted_iota(jnp.int32, weights.shape, 1)
        weights = jnp.where(rows <= cols, weights, 0.0)
    return weights, dot_nt(value, grad)


def add_stats(q, do, stats, heads, piece, place, off, diagonal):
    half, hd = piece.shape[0], piece.shape[1] // 2
    key, value = piece[:, :hd], piece[:, hd:]
    for j in range(heads):
        cols = slice(j * hd, (j + 1) * hd)
        query, grad = q[pl.ds(off, half), cols], do[pl.ds(off, half), cols]
        weights, grad_prob = pair_weights(query, grad, key, value, diagonal, hd**-0.5)
        stats[0, place, j : j + 1, :] += jnp.sum(weights, axis=0, keepdims=True)
        stats[1, place, j : j + 1, :] += jnp.sum(weights * grad_prob, axis=0, keepdims=True)


def add_grads(q, do, stats, dqt, heads, piece, place, off, diagonal):
    half, hd = piece.shape[0], piece.shape[1] // 2
    key, value = piece[:, :hd], piece[:, hd:]
    grad_key = grad_value = None
    for j in range(heads):
        cols = slice(j * hd, (j + 1) * hd)
        query, grad = q[pl.ds(off, half), cols], do[pl.ds(off, half), cols]
        weights, grad_prob = pair_weights(query, grad, key, value, diagonal, hd**-0.5)
        inverse = 1.0 / stats[0, place, j : j + 1, :]
        delta = stats[1, place, j : j + 1, :] * inverse
        prob = weights * inverse
        grad_score = (prob * (grad_prob - delta) * hd**-0.5).astype(BF16)
        term_key = dot_nn(grad_score, query)
        term_value = dot_nn(prob.astype(BF16), grad)
        grad_key = term_key if j == 0 else grad_key + term_key
        grad_value = term_value if j == 0 else grad_value + term_value
        dqt[place, j] += dot_tn(key, grad_score)
    return grad_key, grad_value


def second_quadrant(me, hop, low, high, picked, lo, hi):
    wraps = me[0] < hop
    picked[...] = low[...]

    @pl.when(wraps)
    def _():
        picked[...] = high[...]

    return wraps, jnp.where(wraps, 1, 0), pl.multiple_of(jnp.where(wraps, hi, lo), lo_size(picked))


def lo_size(ref):
    return ref.shape[0]


def near_stats_kernel(heads, me, order, q, do, low, high, low1, high1, low3, high3, stats, picked):
    lo, hi = offsets(me, order, low.shape[0])
    stats[...] = jnp.zeros_like(stats)
    add_stats(q, do, stats, heads, low, 1, hi, False)
    add_stats(q, do, stats, heads, high, 1, hi, True)
    add_stats(q, do, stats, heads, low, 0, lo, True)
    hop_stats(me, 1, q, do, stats, heads, low1, high1, picked, lo, hi)
    hop_stats(me, 3, q, do, stats, heads, low3, high3, picked, lo, hi)


def hop_stats(me, hop, q, do, stats, heads, low, high, picked, lo, hi):
    add_stats(q, do, stats, heads, low, 1, hi, False)
    _, place, off = second_quadrant(me, hop, low, high, picked, lo, hi)
    add_stats(q, do, stats, heads, picked, place, off, False)


def hop_terms(me, hop, q, do, stats, dqt, heads, low, high, picked, acc, lo, hi, out_low, out_high):
    hd = picked.shape[1] // 2
    acc[0, :, :hd], acc[0, :, hd:] = add_grads(q, do, stats, dqt, heads, low, 1, hi, False)
    wraps, place, off = second_quadrant(me, hop, low, high, picked, lo, hi)
    acc[1, :, :hd], acc[1, :, hd:] = add_grads(q, do, stats, dqt, heads, picked, place, off, False)

    @pl.when(wraps)
    def _():
        out_low[...] = acc[0].astype(out_low.dtype)
        out_high[...] = acc[1].astype(out_low.dtype)

    @pl.when(jnp.logical_not(wraps))
    def _():
        out_low[...] = (acc[0] + acc[1]).astype(out_low.dtype)
        out_high[...] = jnp.zeros_like(out_high)


def far_grads_kernel(
    heads, me, order, q, do, lows, highs, before, stats, dqt, out_lows, out_highs, picked, acc
):
    lo, hi = offsets(me, order, picked.shape[0])
    stats[...] = before[...]
    for n, hop in enumerate((2, 4)):
        hop_stats(me, hop, q, do, stats, heads, lows.at[n], highs.at[n], picked, lo, hi)
    dqt[...] = jnp.zeros_like(dqt)
    for n, hop in enumerate((2, 4)):
        hop_terms(
            me, hop, q, do, stats, dqt, heads, lows.at[n], highs.at[n],
            picked, acc, lo, hi, out_lows.at[n], out_highs.at[n],
        )


def near_grads_kernel(
    heads, me, order, q, do, stats, low3, high3, low1, high1, low, high, before,
    dq, own, term3_low, term3_high, term1_low, term1_high, dqt, picked, acc,
):
    half, hd = low.shape[0], low.shape[1] // 2
    lo, hi = offsets(me, order, half)
    dqt[...] = before[...]
    for hop, *refs, outs in (
        (3, low3, high3, (term3_low, term3_high)), (1, low1, high1, (term1_low, term1_high))
    ):
        hop_terms(me, hop, q, do, stats, dqt, heads, *refs, picked, acc, lo, hi, *outs)
    gk, gv = add_grads(q, do, stats, dqt, heads, low, 1, hi, False)
    gk2, gv2 = add_grads(q, do, stats, dqt, heads, low, 0, lo, True)
    own[0, :, :hd] = gk + gk2
    own[0, :, hd:] = gv + gv2
    own[1, :, :hd], own[1, :, hd:] = add_grads(q, do, stats, dqt, heads, high, 1, hi, True)
    for place, off in ((0, lo), (1, hi)):
        for j in range(heads):
            dq[pl.ds(off, half), j * hd : (j + 1) * hd] = dqt[place, j].T.astype(BF16)


def tokens_kernel(nz, at, order, own, up, far_up, far_down, down, theirs, *refs):
    grad, behind, *grads_far, ahead, out = refs
    rows = own.shape[1]
    block = rows // nz
    grads_far = jnp.concatenate([part[...] for part in grads_far], axis=0)
    for n in range(2):
        if n == 0:
            y = at[0]
            far = jnp.concatenate([far_up[...], far_down[...]], axis=0)
            pieces = (up[:rows], far, down[:rows])
        else:
            y = 1 - at[0]
            pieces = tuple(theirs[k * rows : (k + 1) * rows] for k in range(3))
        total = dot_nn(own[y], grad[...])
        for piece, grads in zip(pieces, (behind[...], grads_far, ahead[...])):
            total = total + dot_nn(piece, grads)
        total = total.astype(BF16)
        for z in range(nz):
            out[y * nz + z] = total[z * block : (z + 1) * block]


def shards(hidden_in, w_qkv, queries, keys, values, d_out, block_order):
    count = lax.axis_size(SEQ)
    nx, ny, nz = (lax.axis_size(axis) for axis in SEQ)
    at_x, at_y = lax.axis_index("x"), lax.axis_index("y_lo")
    core, y_hi = lax.axis_index("core"), lax.axis_index("y_hi")
    index = lax.axis_index(SEQ).astype(jnp.int32)
    me = index.reshape(1)
    rows, width = hidden_in.shape
    half = rows // 2
    hd = keys.shape[1]
    heads = queries.shape[1] // hd
    out_rows = width // count

    piece = jax.ShapeDtypeStruct((half, 2 * hd), BF16)
    stats_shape = jax.ShapeDtypeStruct((2, 2, heads, half), F32)
    partial_q = jax.ShapeDtypeStruct((2, heads, hd, half), F32)
    picked = pltpu.VMEM(piece.shape, BF16)
    acc = pltpu.VMEM((2, half, 2 * hd), F32)

    low, high = call(
        split_kernel, [piece, piece], (me, block_order, keys, values),
        [pltpu.SemaphoreType.DMA((4,))], space=pltpu.HBM,
    )
    low1 = shift_seq(low, 1)
    high1 = shift_seq(high, 1, (-2, -1))
    low3 = shift_seq(low, 3)
    high3 = shift_seq(high, 3, (-4, -3, -2, -1))

    chunks = hidden_in.T.reshape(nx, ny, nz * out_rows, rows)
    to1, to2, to3 = (
        lax.dynamic_slice(
            chunks, ((at_x + k) % nx, core, 0, 0), (1, 1, *chunks.shape[2:])
        ).reshape(chunks.shape[2:])
        for k in range(1, nx)
    )
    split = to2.shape[0] // 2
    leaving = [jnp.concatenate([to1, to2[:split]]), jnp.concatenate([to3, to2[split:]])]
    hidden_own = lax.dynamic_index_in_dim(chunks, at_x, 0, keepdims=False)
    low1, high1, low3, high3, leaving, hidden_own = lax.optimization_barrier(
        (low1, high1, low3, high3, leaving, hidden_own)
    )
    low24 = shift_seq(jnp.stack([low1, low3]), 1)
    high24 = shift_seq(jnp.stack([high1, high3]), 1, (-1, 0, 1, 2))

    base = (me, block_order, queries, d_out)
    stats = call(
        functools.partial(near_stats_kernel, heads), stats_shape,
        (*base, low, high, low1, high1, low3, high3), [picked], cost=5,
    )
    low24, high24, stats, leaving = lax.optimization_barrier((low24, high24, stats, leaving))
    up, down = shift(leaving[0], "x", 1), shift(leaving[1], "x", -1)
    two = jax.ShapeDtypeStruct((2, *piece.shape), BF16)
    stats, dqt, out24, out24_high = call(
        functools.partial(far_grads_kernel, heads), [stats_shape, partial_q, two, two],
        (*base, low24, high24, stats), [picked, acc], cost=8,
    )
    back24 = shift_seq(out24, -1)
    back24_high = shift_seq(out24_high, -1, (0, 1, 2, 3))
    term = jax.ShapeDtypeStruct(piece.shape, F32)
    grad_q, own, out3, out3_high, out1, out1_high = call(
        functools.partial(near_grads_kernel, heads),
        [jax.ShapeDtypeStruct(queries.shape, BF16), jax.ShapeDtypeStruct((2, *piece.shape), F32),
         term, term, term, term],
        (*base, stats, low3, high3, low1, high1, low, high, dqt),
        [pltpu.VMEM(partial_q.shape, F32), picked, acc], cost=20,
    )
    grad_q, up, down = lax.optimization_barrier((grad_q, up, down))
    back1 = shift_seq((out1 + back24[0].astype(F32)).astype(BF16), -1)
    back3 = shift_seq((out3 + back24[1].astype(F32)).astype(BF16), -3)
    back1_high = shift_seq((out1_high + back24_high[0].astype(F32)).astype(BF16), -1, (0, -1))
    back3_high = shift_seq((out3_high + back24_high[1].astype(F32)).astype(BF16), -3, (-1, 0, 1, 2))

    def neighbours(matrix):
        return matrix, shift(matrix, "x", 1), shift(matrix, "x", -1)

    def x_gathered(matrix, behind, ahead):
        return matrix, behind, shift(behind[:half], "x", 1), shift(ahead[half:], "x", -1), ahead

    gathered_q = neighbours(grad_q)
    passed = (up[2 * split :], down[2 * split :])
    passed, back1, back1_high, back3, back3_high, gathered_q = lax.optimization_barrier(
        (passed, back1, back1_high, back3, back3_high, gathered_q)
    )
    far_up, far_down = shift(passed[0], "x", 1), shift(passed[1], "x", -1)
    gathered_q = x_gathered(*gathered_q)
    swapping = jnp.concatenate([up[: 2 * split], far_up, far_down, down[: 2 * split]])
    hidden_theirs = shift(lax.optimization_barrier((swapping, gathered_q))[0], "core", 1)

    def token_sums(gathered):
        return call(
            functools.partial(tokens_kernel, nz),
            jax.ShapeDtypeStruct((ny * nz, out_rows, gathered[0].shape[1]), BF16),
            (
                core.astype(jnp.int32).reshape(1), block_order, hidden_own,
                up, far_up, far_down, down, hidden_theirs, *gathered,
            ),
            cost=2,
        )

    tokens_q = token_sums(gathered_q)

    low_total = own[0] + back1.astype(F32) + back3.astype(F32)
    high_total = own[1] + back1_high.astype(F32) + back3_high.astype(F32)
    low_total, high_total = low_total.astype(BF16), high_total.astype(BF16)
    grad_kv = jnp.where(
        low_slot_of(me, block_order) == 0,
        jnp.concatenate([low_total, high_total], axis=0),
        jnp.concatenate([high_total, low_total], axis=0),
    )

    grad_kv, tokens_q = lax.optimization_barrier((grad_kv, tokens_q))
    near_kv = neighbours(grad_kv)
    gathered_kv = (*near_kv[:2], shift(near_kv[1], "x", 1), near_kv[2])

    grads = jnp.concatenate([grad_q, grad_kv], axis=1).reshape(2, 2, rows // 4, -1)
    theirs = lax.dynamic_index_in_dim(grads, 1 - core, 1, keepdims=False).reshape(half, -1)
    mine = lax.dynamic_index_in_dim(grads, core, 1, keepdims=False).reshape(half, -1)
    step = width // 2
    weights = [w_qkv[start : start + step] for start in range(0, width, step)]
    received = [shift(dot_nt(theirs, weight).astype(BF16), "core", 1) for weight in weights]
    totals = lax.optimization_barrier([dot_nt(mine, weight) for weight in weights])
    kept, sent = [], []
    for total, other in zip(totals, received):
        total = (total + other.astype(F32)).reshape(2, rows // 4, step)
        sent.append(lax.dynamic_index_in_dim(total, 1 - y_hi, 0, keepdims=False).astype(BF16))
        kept.append(lax.dynamic_index_in_dim(total, y_hi, 0, keepdims=False))

    grad_in = [keep + shift(send, "y_hi", 1).astype(F32) for keep, send in zip(kept, sent)]
    sums_q = lax.all_to_all(tokens_q, ("y_lo", "z"), 0, 0, tiled=True)
    tokens_kv, sums_q, _ = lax.optimization_barrier((token_sums(gathered_kv), sums_q, sent))
    sums_kv = lax.all_to_all(tokens_kv, ("y_lo", "z"), 0, 0, tiled=True)
    sums = [jnp.sum(part.astype(F32), axis=0) for part in (sums_q, sums_kv)]
    grad_w = jnp.concatenate(sums, axis=-1) * float(rows * count) ** (-0.5)
    return jnp.concatenate(grad_in, axis=1).astype(BF16), grad_w.astype(BF16)


def solution(mesh):
    dims = SEQ_DIMS[mesh.shape["seq"]] + (2, 2)
    split = Mesh(np.asarray(mesh.devices).reshape(dims), SEQ + KVH)
    return jax.shard_map(
        shards,
        mesh=split,
        in_specs=(
            P(SEQ, None),
            P(None, KVH),
            P(SEQ, KVH),
            P(SEQ, KVH),
            P(SEQ, KVH),
            P(SEQ, KVH),
            P(),
        ),
        out_specs=(P(SEQ + KVH, None), P(SEQ, KVH)),
        check_vma=False,
    )
```
